32 devices in a mesh: cuts: 8 (over z, core), rank: 4 (over y, x).
Axes of the slice: x: 2, y: 2, z: 4, core: 2. Of those that a mesh axis runs over, the one named last changes fastest.
Arguments:
- core_one: float32 [512, 320, 512], P('rank', 'cuts'), may hold values from -6 to 6
- core_two: float32 [512, 320, 512], P('rank', 'cuts'), may hold values from -0.25 to 0.25
- right_sketch: float32 [512, 128], replicated, may hold values from -0.25 to 0.25
- sketch_core: float32 [128, 320, 128], P(None, 'cuts'), may hold values from -0.03125 to 0.03125
Outputs:
- left_core: float32 [512, 320, 128], P('rank', 'cuts')
- middle_core: float32 [128, 320, 128], P('rank', 'cuts')
- carry: float32 [128, 512], replicated
The draws below stay inside these ranges and needn't reach their ends.
All inputs are finite; a program needn't handle non-finite values.
Results may differ from the reference program's by a relative error of at most 0.00015.
Values sent between devices are 32-bit elements; how exact they have to be, the bound alone decides.
No kernel may reach another device: no remote copies, remote signals or barrier semaphores. Data moves between devices by JAX's collectives and lax.ppermute only.
A program may use at most 128 MiB of HBM per device.

```python
import jax
import jax.numpy as jnp
from jax import lax

R = 512
NM = 320
L = 128


def shard_levels(own_key, extent, pieces, low, top_value):
    level, own = 1.0, jax.random.fold_in(own_key, 6)
    for position, shards_of in pieces:
        draws = jnp.exp(jax.random.uniform(jax.random.fold_in(own, position), (shards_of,), jnp.float32, low / len(pieces), top_value / len(pieces)))
        level = level * jnp.repeat(draws, extent[position] // shards_of).reshape([-1 if axis == position else 1 for axis in range(len(extent))])
    return level


def normal_values(key, extent, width, reach, pieces=(), held_as=jnp.bfloat16):
    result = width * jax.random.normal(key, extent, jnp.float32)
    if pieces:
        result = result * shard_levels(key, extent, pieces, -0.22, 0.18)
    return jnp.clip(result, -reach, reach).astype(held_as)


def setup_inputs(seed: int = 0) -> dict:
    arg_keys = jax.random.split(jax.random.key(seed), 5)
    return {
        "core_one": normal_values(arg_keys[0], (R, NM, R), 1.0, 6.0, ((0, 4), (1, 8)), jnp.float32),
        "core_two": normal_values(arg_keys[1], (R, NM, R), R ** -0.5, 0.25, ((0, 4), (1, 8)), jnp.float32),
        "right_sketch": normal_values(arg_keys[2], (R, L), R ** -0.5, 0.25, (), jnp.float32),
        "sketch_core": normal_values(arg_keys[3], (L, NM, L), (NM * L) ** -0.5, 0.03125, ((1, 8),), jnp.float32),
    }


def orthonormalize(rows, unfolded):
    highest = lax.Precision.HIGHEST
    gram = jnp.dot(rows.T.astype(jnp.float32), rows.astype(jnp.float32), precision=highest, preferred_element_type=jnp.float32)
    factor = jnp.linalg.cholesky(gram)
    ortho = lax.linalg.triangular_solve(factor, rows, left_side=False, lower=True, transpose_a=True)
    carried = jnp.dot(ortho.T.astype(jnp.float32), unfolded.astype(jnp.float32), precision=highest, preferred_element_type=jnp.float32)
    return (ortho, carried)

def reference(core_one, core_two, right_sketch, sketch_core):
    highest = lax.Precision.HIGHEST
    sketched = jnp.einsum('anj,jc->anc', core_two, right_sketch, precision=highest)
    bridge = jnp.einsum('anc,bnc->ab', sketched, sketch_core, precision=highest)
    flat_one = core_one.reshape(R * NM, R)
    first_rows = jnp.dot(flat_one.astype(jnp.float32), bridge.astype(jnp.float32), precision=highest, preferred_element_type=jnp.float32)
    first_q, first_carry = orthonormalize(first_rows, flat_one)
    projected = jnp.einsum('ba,ank->bnk', first_carry, core_two, precision=highest)
    flat_two = projected.reshape(L * NM, R)
    second_rows = jnp.dot(flat_two.astype(jnp.float32), right_sketch.astype(jnp.float32), precision=highest, preferred_element_type=jnp.float32)
    second_q, carry = orthonormalize(second_rows, flat_two)
    left_core = (jnp.sqrt(jnp.float32(R * NM)) * first_q).reshape(R, NM, L)
    middle_core = (jnp.sqrt(jnp.float32(L * NM)) * second_q).reshape(L, NM, L)
    return (left_core, middle_core, carry)
```

```python
import jax
import jax.numpy as jnp
from jax import lax
from jax.sharding import PartitionSpec as P

HIGHEST = lax.Precision.HIGHEST
HIGH = lax.Precision.HIGH


def axis_bits(axis):
    return [(axis, bit) for bit in range((lax.axis_size(axis) - 1).bit_length())]


def swap(value, step):
    axis, bit = step
    pairs = [(i, i ^ (1 << bit)) for i in range(lax.axis_size(axis))]
    return lax.ppermute(value, axis, pairs)


def side(step):
    axis, bit = step
    return lax.rem(lax.div(lax.axis_index(axis), 1 << bit), 2)


def halve(value, step):
    half = value.shape[0] // 2
    own = side(step)
    keep = lax.dynamic_slice_in_dim(value, own * half, half, 0)
    give = lax.dynamic_slice_in_dim(value, (1 - own) * half, half, 0)
    return keep + swap(give, step)


def double(value, step):
    other = swap(value, step)
    own = side(step) == 0
    return jnp.concatenate([jnp.where(own, value, other), jnp.where(own, other, value)], axis=0)


def scatter_sum(value, steps):
    for step in steps:
        value = halve(value, step)
    return value


def gather(value, steps):
    for step in reversed(steps):
        value = double(value, step)
    return value


def total(value, steps):
    for step in steps:
        value = value + swap(value, step)
    return value


def invert_factor(gram):
    factor = jnp.linalg.cholesky(gram)
    unit = jnp.eye(gram.shape[0], dtype=jnp.float32)
    return lax.linalg.triangular_solve(factor, unit, left_side=True, lower=True)


def dot(a, b, contract, precision=HIGHEST):
    return lax.dot_general(
        a, b, (contract, ((), ())), precision=precision, preferred_element_type=jnp.float32
    )


def on_device(core_one, core_two, right_sketch, sketch_core):
    local_rows, slices, width = core_one.shape
    sketch_width = right_sketch.shape[1]
    ranks, cuts = lax.axis_size("rank"), lax.axis_size("cuts")
    rank = lax.axis_index("rank")
    band = sketch_width // ranks
    cut_steps, rank_steps = axis_bits("cuts"), axis_bits("rank")
    steps = cut_steps[:1] + rank_steps + cut_steps[1:]
    share = -(-slices // ranks)

    sketched = jnp.einsum("anj,jc->nac", core_two, right_sketch, precision=HIGH)
    part = jnp.einsum("nac,bnc->ab", sketched, sketch_core, precision=HIGH)
    bridge = gather(total(part, cut_steps), rank_steps[::-1])

    padded = jnp.pad(sketched, ((0, share * ranks - slices), (0, 0), (0, 0)))
    blocks = []
    for offset in range(ranks):
        block = lax.dynamic_slice_in_dim(padded, (rank ^ offset) * share, share, 0)
        if offset:
            block = lax.ppermute(block, "rank", [(i, i ^ offset) for i in range(ranks)])
        blocks.append(block)

    flat_one = core_one.reshape(local_rows * slices, width)
    square = dot(flat_one, flat_one, ((0,), (0,)), HIGH)
    own_square = scatter_sum(square, steps)
    raw = gather(dot(own_square, bridge, ((1,), (0,))), steps)
    gram = dot(bridge, raw, ((0,), (0,)))

    loose = 0.0
    for offset in range(ranks):
        rows = lax.dynamic_slice_in_dim(raw, (rank ^ offset) * local_rows, local_rows, 0)
        loose = loose + jnp.einsum("ab,nac->nbc", rows, blocks[offset], precision=HIGH)
    first = share // 2
    pieces = []
    for piece, order in ((loose[:first], rank_steps), (loose[first:], rank_steps[::-1])):
        if piece.shape[0]:
            count = piece.shape[0]
            piece = piece[None]
            for step in order:
                piece = double(piece, step)
            if order is not rank_steps:
                bits = len(rank_steps)
                piece = piece.reshape((2,) * bits + piece.shape[1:])
                piece = piece.transpose(tuple(range(bits))[::-1] + tuple(range(bits, bits + 3)))
                piece = piece.reshape((ranks, count) + piece.shape[bits + 1:])
            pieces.append(piece)
    everyone = jnp.concatenate(pieces, axis=1)
    everyone = everyone.reshape((ranks * share,) + everyone.shape[2:])[:slices]

    inverse = invert_factor(gram)
    tight = jnp.einsum("bd,ndc->nbc", inverse, loose, precision=HIGH)
    flat_tight = tight.reshape(share * sketch_width, sketch_width)
    second_gram = total(dot(flat_tight, flat_tight, ((0,), (0,))), steps)
    second_inverse = invert_factor(second_gram)

    scale = jnp.sqrt(jnp.float32(local_rows * ranks * slices * cuts))
    solve = scale * dot(bridge, inverse, ((1,), (1,)))
    left_core = dot(flat_one, solve, ((1,), (0,)), HIGH).reshape(local_rows, slices, sketch_width)

    own_raw = lax.dynamic_slice_in_dim(raw, rank * local_rows, local_rows, 0)
    weight = dot(dot(own_raw, inverse, ((1,), (1,))), inverse, ((1,), (0,)))
    spread = jnp.einsum("ab,nbc->anc", weight, everyone, precision=HIGH)
    flat_two = core_two.reshape(local_rows * slices, width)
    flat_spread = spread.reshape(local_rows * slices, sketch_width)
    second_raw = gather(scatter_sum(dot(flat_two, flat_spread, ((0,), (0,)), HIGH), steps), steps)
    carry = dot(second_inverse, second_raw, ((1,), (1,)))

    own_inverse = lax.dynamic_slice_in_dim(inverse, rank * band, band, 0)
    scale = jnp.sqrt(jnp.float32(sketch_width * slices * cuts))
    rows = jnp.einsum("bd,ndc->bnc", own_inverse, everyone, precision=HIGH)
    middle_core = scale * jnp.einsum("bnc,dc->bnd", rows, second_inverse, precision=HIGH)
    return (left_core, middle_core, carry)


def solution(mesh):
    placed = (P("rank", "cuts", None), P("rank", "cuts", None), P(), P(None, "cuts", None))
    return jax.shard_map(
        on_device,
        mesh=mesh,
        in_specs=placed,
        out_specs=(P("rank", "cuts", None), P("rank", "cuts", None), P()),
        check_vma=False,
    )
```

```python
import jax
import jax.numpy as jnp
from jax import lax
from jax.sharding import PartitionSpec as P

HIGHEST = lax.Precision.HIGHEST
HIGH = lax.Precision.HIGH


def axis_bits(axis):
    return [(axis, bit) for bit in range((lax.axis_size(axis) - 1).bit_length())]


def swap(value, step):
    axis, bit = step
    pairs = [(i, i ^ (1 << bit)) for i in range(lax.axis_size(axis))]
    return lax.ppermute(value, axis, pairs)


def side(step):
    axis, bit = step
    return lax.rem(lax.div(lax.axis_index(axis), 1 << bit), 2)


def halve(value, step):
    half = value.shape[0] // 2
    own = side(step)
    keep = lax.dynamic_slice_in_dim(value, own * half, half, 0)
    give = lax.dynamic_slice_in_dim(value, (1 - own) * half, half, 0)
    return keep + swap(give, step)


def double(value, step):
    other = swap(value, step)
    own = side(step) == 0
    return jnp.concatenate([jnp.where(own, value, other), jnp.where(own, other, value)], axis=0)


def scatter_sum(value, steps):
    for step in steps:
        value = halve(value, step)
    return value


def gather(value, steps):
    for step in reversed(steps):
        value = double(value, step)
    return value


def total(value, steps):
    for step in steps:
        value = value + swap(value, step)
    return value


def exchange(value, axes):
    return lax.all_to_all(value, axes, 0, 0, tiled=True)


def split_sum(value, axes):
    parts = lax.axis_size(axes)
    blocks = value.reshape((parts, value.shape[0] // parts) + value.shape[1:])
    return jnp.sum(exchange(blocks, axes), axis=0)


def gather_all(value, axes):
    parts = lax.axis_size(axes)
    return exchange(jnp.broadcast_to(value[None], (parts,) + value.shape), axes)


def invert_factor(gram):
    factor = jnp.linalg.cholesky(gram)
    unit = jnp.eye(gram.shape[0], dtype=jnp.float32)
    return lax.linalg.triangular_solve(factor, unit, left_side=True, lower=True)


def dot(a, b, contract, precision=HIGHEST):
    return lax.dot_general(
        a, b, (contract, ((), ())), precision=precision, preferred_element_type=jnp.float32
    )


def on_device(core_one, core_two, right_sketch, sketch_core):
    local_rows, slices, width = core_one.shape
    sketch_width = right_sketch.shape[1]
    ranks, cuts = lax.axis_size("rank"), lax.axis_size("cuts")
    rank = lax.axis_index("rank")
    band = sketch_width // ranks
    cut_steps, rank_steps = axis_bits("cuts"), axis_bits("rank")
    steps = cut_steps[:1] + rank_steps + cut_steps[1:]
    both = ("cuts", "rank")
    share = -(-slices // ranks)

    sketched = jnp.einsum("anj,jc->nac", core_two, right_sketch, precision=HIGH)
    part = jnp.einsum("nac,bnc->ab", sketched, sketch_core, precision=HIGH)
    bridge = gather_all(split_sum(part, "cuts"), both)
    bridge = bridge.reshape(cuts, ranks, -1, sketch_width).swapaxes(0, 1).reshape(width, sketch_width)

    padded = jnp.pad(sketched, ((0, share * ranks - slices), (0, 0), (0, 0)))
    blocks = []
    for offset in range(ranks):
        block = lax.dynamic_slice_in_dim(padded, (rank ^ offset) * share, share, 0)
        if offset:
            block = lax.ppermute(block, "rank", [(i, i ^ offset) for i in range(ranks)])
        blocks.append(block)

    flat_one = core_one.reshape(local_rows * slices, width)
    square = dot(flat_one, flat_one, ((0,), (0,)), HIGH)
    square = square.reshape(cuts // 2, 2, ranks, -1, width)
    square = square.transpose(1, 2, 0, 3, 4).reshape(2 * ranks, cuts // 2, -1, width)
    square = scatter_sum(square, cut_steps[:1] + rank_steps[::-1])[0]
    groups = [list(range(core, cuts, 2)) for core in range(2)]
    own_square = jnp.sum(lax.all_to_all(square, "cuts", 0, 0, axis_index_groups=groups, tiled=True), axis=0)
    raw_rows = dot(own_square, bridge, ((1,), (0,)))
    raw = gather_all(raw_rows, both).reshape(width, sketch_width)
    gram = dot(bridge, raw, ((0,), (0,)))

    loose = 0.0
    for offset in range(ranks):
        rows = lax.dynamic_slice_in_dim(raw, (rank ^ offset) * local_rows, local_rows, 0)
        loose = loose + jnp.einsum("ab,nac->nbc", rows, blocks[offset], precision=HIGH)
    first = share // 2
    pieces = []
    for piece, order in ((loose[:first], rank_steps), (loose[first:], rank_steps[::-1])):
        if piece.shape[0]:
            count = piece.shape[0]
            piece = piece[None]
            for step in order:
                piece = double(piece, step)
            if order is not rank_steps:
                bits = len(rank_steps)
                piece = piece.reshape((2,) * bits + piece.shape[1:])
                piece = piece.transpose(tuple(range(bits))[::-1] + tuple(range(bits, bits + 3)))
                piece = piece.reshape((ranks, count) + piece.shape[bits + 1:])
            pieces.append(piece)
    everyone = jnp.concatenate(pieces, axis=1)
    everyone = everyone.reshape((ranks * share,) + everyone.shape[2:])[:slices]

    inverse = invert_factor(gram)
    tight = jnp.einsum("bd,ndc->nbc", inverse, loose, precision=HIGH)
    flat_tight = tight.reshape(share * sketch_width, sketch_width)
    second_gram = total(dot(flat_tight, flat_tight, ((0,), (0,))), steps)
    second_inverse = invert_factor(second_gram)

    scale = jnp.sqrt(jnp.float32(local_rows * ranks * slices * cuts))
    solve = scale * dot(bridge, inverse, ((1,), (1,)))
    left_core = dot(flat_one, solve, ((1,), (0,)), HIGH).reshape(local_rows, slices, sketch_width)

    own_raw = lax.dynamic_slice_in_dim(raw, rank * local_rows, local_rows, 0)
    weight = dot(dot(own_raw, inverse, ((1,), (1,))), inverse, ((1,), (0,)))
    spread = jnp.einsum("ab,nbc->anc", weight, everyone, precision=HIGH)
    flat_two = core_two.reshape(local_rows * slices, width)
    flat_spread = spread.reshape(local_rows * slices, sketch_width)
    second_raw = split_sum(dot(flat_two, flat_spread, ((0,), (0,)), HIGH), both)
    second_raw = gather_all(second_raw, both).reshape(width, sketch_width)
    carry = dot(second_inverse, second_raw, ((1,), (1,)))

    own_inverse = lax.dynamic_slice_in_dim(inverse, rank * band, band, 0)
    scale = jnp.sqrt(jnp.float32(sketch_width * slices * cuts))
    rows = jnp.einsum("bd,ndc->bnc", own_inverse, everyone, precision=HIGH)
    middle_core = scale * jnp.einsum("bnc,dc->bnd", rows, second_inverse, precision=HIGH)
    return (left_core, middle_core, carry)


def solution(mesh):
    placed = (P("rank", "cuts", None), P("rank", "cuts", None), P(), P(None, "cuts", None))
    return jax.shard_map(
        on_device,
        mesh=mesh,
        in_specs=placed,
        out_specs=(P("rank", "cuts", None), P("rank", "cuts", None), P()),
        check_vma=False,
    )
```

```python
import jax
import jax.numpy as jnp
from jax import lax
from jax.experimental import pallas as pl
from jax.experimental.pallas import tpu as pltpu
from jax.sharding import PartitionSpec as P

HIGHEST = lax.Precision.HIGHEST
NT = (((1,), (1,)), ((), ()))
NN = (((1,), (0,)), ((), ()))
TN = (((0,), (0,)), ((), ()))
VMEM_LIMIT = 56 * 1024 * 1024
BLOCK = 8


def call(kernel, flops, size, **more):
    return pl.pallas_call(
        kernel,
        compiler_params=pltpu.CompilerParams(vmem_limit_bytes=VMEM_LIMIT),
        cost_estimate=pl.CostEstimate(flops=flops, bytes_accessed=size, transcendentals=0),
        **more,
    )


def shape(*extent):
    return jax.ShapeDtypeStruct(extent, jnp.float32)


def split(value):
    high = value.astype(jnp.bfloat16)
    return high, (value - high.astype(jnp.float32)).astype(jnp.bfloat16)


def mxu(a, b, form):
    return lax.dot_general(a, b, form, preferred_element_type=jnp.float32)


def both_parts(value, axis):
    return jnp.concatenate(split(value), axis=axis)


def fold(value, axis):
    half = value.shape[axis] // 2
    return lax.slice_in_dim(value, 0, half, axis=axis) + lax.slice_in_dim(value, half, 2 * half, axis=axis)


def rows_of(ref):
    return ref.reshape(ref.shape[0] * ref.shape[1], ref.shape[2])


def sketch_kernel(core_ref, right_ref, left_ref, sketched_ref, part_ref, rows_ref):
    local_rows, block, _ = core_ref.shape
    columns = right_ref.shape[1]
    right = both_parts(right_ref[...], 1)
    high, low = split(rows_of(core_ref)[...])
    rows_ref[...] = fold(mxu(high, right, NN) + mxu(low, right, NN), 1)
    left_rows = rows_of(left_ref)

    @pl.when(pl.program_id(0) == 0)
    def _():
        part_ref[...] = jnp.zeros_like(part_ref)

    total = jnp.zeros(part_ref.shape, jnp.float32)
    for pair in range(0, block, 2):
        sides, lefts = [], []
        for n in (pair, pair + 1):
            rows = rows_ref[pl.ds(n, local_rows, stride=block), :]
            sketched_ref[n] = rows
            sides.append(rows)
            lefts.append(left_rows[pl.ds(n, columns, stride=block), :])
        high, low = split(jnp.concatenate(sides, axis=1))
        left = both_parts(jnp.concatenate(lefts, axis=1), 0)
        total = total + fold(mxu(high, left, NT) + mxu(low, left, NT), 1)
    part_ref[...] += total


def sketch(core_two, right_sketch, sketch_core):
    local_rows, slices, width = core_two.shape
    columns = right_sketch.shape[1]
    return call(
        sketch_kernel,
        2 * core_two.size * columns * 4,
        4 * (core_two.size + 2 * sketch_core.size),
        grid=(slices // BLOCK,),
        in_specs=[
            pl.BlockSpec((local_rows, BLOCK, width), lambda i: (0, i, 0)),
            pl.BlockSpec((width, columns), lambda i: (0, 0)),
            pl.BlockSpec((columns, BLOCK, columns), lambda i: (0, i, 0)),
        ],
        out_specs=[
            pl.BlockSpec((BLOCK, local_rows, columns), lambda i: (i, 0, 0)),
            pl.BlockSpec((local_rows, columns), lambda i: (0, 0)),
        ],
        out_shape=[shape(slices, local_rows, columns), shape(local_rows, columns)],
        scratch_shapes=[pltpu.VMEM((local_rows * BLOCK, columns), jnp.float32)],
    )(core_two, right_sketch, sketch_core)


def square_kernel(core_ref, square_ref, same_ref, cross_ref):
    step = pl.program_id(0)
    high, low = split(core_ref[...])

    @pl.when(step == 0)
    def _():
        same_ref[...] = jnp.zeros_like(same_ref)
        cross_ref[...] = jnp.zeros_like(cross_ref)

    same_ref[...] += mxu(high, high, TN)
    cross_ref[...] += mxu(high, low, TN)

    @pl.when(step == pl.num_programs(0) - 1)
    def _():
        cross = cross_ref[...]
        square_ref[...] = same_ref[...] + cross + cross.T


def square_of(flat_one):
    rows, width = flat_one.shape
    block = rows // 10
    return call(
        square_kernel,
        4 * rows * width * width,
        4 * flat_one.size,
        grid=(10,),
        in_specs=[pl.BlockSpec((block, width), lambda i: (i, 0))],
        out_specs=pl.BlockSpec((width, width), lambda i: (0, 0)),
        out_shape=shape(width, width),
        scratch_shapes=[pltpu.VMEM((width, width), jnp.float32)] * 2,
    )(flat_one)


def loose_kernel(raw_ref, *refs):
    block_refs, out_ref = refs[:-1], refs[-1]
    count, local_rows, columns = block_refs[0].shape
    raw = both_parts(raw_ref[...], 1)
    for n in range(count):
        high, low = split(jnp.concatenate([ref[n] for ref in block_refs], axis=0))
        out_ref[n] = fold(mxu(raw, high, TN) + mxu(raw, low, TN), 0)


def loosen(raw, blocks):
    count, local_rows, columns = blocks[0].shape
    return call(
        loose_kernel,
        8 * raw.size * count * columns,
        4 * raw.size + 4 * len(blocks) * blocks[0].size,
        out_shape=shape(count, raw.shape[1], columns),
    )(raw, *blocks)


def carry_kernel(everyone_ref, weight_ref, core_ref, raw_ref, middle_ref, rows_ref, sum_ref):
    step = pl.program_id(0)
    block, columns, _ = everyone_ref.shape
    local_rows = core_ref.shape[0]
    band = middle_ref.shape[0]
    weight_high, weight_low = split(weight_ref[...])
    everyone = jnp.concatenate([everyone_ref[n] for n in range(block)], axis=1)
    high, low = split(everyone)
    spread = mxu(weight_high, high, NN) + mxu(weight_high, low, NN) + mxu(weight_low, high, NN)
    middle_rows = rows_of(middle_ref)
    for n in range(block):
        piece = lax.slice_in_dim(spread, n * columns, (n + 1) * columns, axis=1)
        rows_ref[pl.ds(n, local_rows, stride=block), :] = piece[:local_rows]
        middle_rows[pl.ds(n, band, stride=block), :] = piece[local_rows:]
    rows = both_parts(rows_ref[...], 1)
    high, low = split(rows_of(core_ref)[...])

    @pl.when(step == 0)
    def _():
        sum_ref[...] = jnp.zeros_like(sum_ref)

    total = fold(mxu(rows, high, TN) + mxu(rows, low, TN), 0)
    sum_ref[...] += total

    @pl.when(step == pl.num_programs(0) - 1)
    def _():
        raw_ref[...] = sum_ref[...].T


def carry_rows(everyone, weight, core_two, band):
    local_rows, slices, width = core_two.shape
    columns = everyone.shape[2]
    return call(
        carry_kernel,
        2 * core_two.size * columns * 4,
        4 * core_two.size + 4 * everyone.size,
        grid=(slices // BLOCK,),
        in_specs=[
            pl.BlockSpec((BLOCK, columns, columns), lambda i: (i, 0, 0)),
            pl.BlockSpec((local_rows + band, columns), lambda i: (0, 0)),
            pl.BlockSpec((local_rows, BLOCK, width), lambda i: (0, i, 0)),
        ],
        out_specs=[
            pl.BlockSpec((width, columns), lambda i: (0, 0)),
            pl.BlockSpec((band, BLOCK, columns), lambda i: (0, i, 0)),
        ],
        out_shape=[shape(width, columns), shape(band, slices, columns)],
        scratch_shapes=[
            pltpu.VMEM((local_rows * BLOCK, columns), jnp.float32),
            pltpu.VMEM((columns, width), jnp.float32),
        ],
    )(everyone, weight, core_two)


def apply_kernel(rows_ref, weight_ref, out_ref):
    weight = both_parts(weight_ref[...], 1)
    high, low = split(rows_ref[...])
    out_ref[...] = fold(mxu(high, weight, NN) + mxu(low, weight, NN), 1)


def apply_to(rows, weight, steps):
    count, width = rows.shape
    columns = weight.shape[1]
    return call(
        apply_kernel,
        8 * rows.size * columns,
        4 * (rows.size + count * columns),
        grid=(steps,),
        in_specs=[
            pl.BlockSpec((count // steps, width), lambda i: (i, 0)),
            pl.BlockSpec((width, columns), lambda i: (0, 0)),
        ],
        out_specs=pl.BlockSpec((count // steps, columns), lambda i: (i, 0)),
        out_shape=shape(count, columns),
    )(rows, weight)


def axis_bits(axis):
    return [(axis, bit) for bit in range((lax.axis_size(axis) - 1).bit_length())]


def swap(value, step):
    axis, bit = step
    pairs = [(i, i ^ (1 << bit)) for i in range(lax.axis_size(axis))]
    return lax.ppermute(value, axis, pairs)


def side(step):
    axis, bit = step
    return lax.rem(lax.div(lax.axis_index(axis), 1 << bit), 2)


def halve(value, step):
    half = value.shape[0] // 2
    own = side(step)
    keep = lax.dynamic_slice_in_dim(value, own * half, half, 0)
    give = lax.dynamic_slice_in_dim(value, (1 - own) * half, half, 0)
    return keep + swap(give, step)


def double(value, step):
    other = swap(value, step)
    own = side(step) == 0
    return jnp.concatenate([jnp.where(own, value, other), jnp.where(own, other, value)], axis=0)


def scatter_sum(value, steps):
    for step in steps:
        value = halve(value, step)
    return value


def gather(value, steps):
    for step in reversed(steps):
        value = double(value, step)
    return value


def total(value, steps):
    for step in steps:
        value = value + swap(value, step)
    return value


def exchange(value, axes):
    return lax.all_to_all(value, axes, 0, 0, tiled=True)


def split_sum(value, axes):
    parts = lax.axis_size(axes)
    blocks = value.reshape((parts, value.shape[0] // parts) + value.shape[1:])
    return jnp.sum(exchange(blocks, axes), axis=0)


def gather_all(value, axes):
    parts = lax.axis_size(axes)
    return exchange(jnp.broadcast_to(value[None], (parts,) + value.shape), axes)


def invert_factor(gram):
    factor = jnp.linalg.cholesky(gram)
    unit = jnp.eye(gram.shape[0], dtype=jnp.float32)
    return lax.linalg.triangular_solve(factor, unit, left_side=True, lower=True)


def dot(a, b, contract, precision=HIGHEST):
    return lax.dot_general(
        a, b, (contract, ((), ())), precision=precision, preferred_element_type=jnp.float32
    )


def on_device(core_one, core_two, right_sketch, sketch_core):
    local_rows, slices, width = core_one.shape
    sketch_width = right_sketch.shape[1]
    ranks, cuts = lax.axis_size("rank"), lax.axis_size("cuts")
    rank = lax.axis_index("rank")
    band = sketch_width // ranks
    cut_steps, rank_steps = axis_bits("cuts"), axis_bits("rank")
    steps = cut_steps[:1] + rank_steps + cut_steps[1:]
    both = ("cuts", "rank")
    share = -(-slices // ranks)

    filler = ((0, 0), (0, -slices % BLOCK), (0, 0))
    core_two, sketch_core = jnp.pad(core_two, filler), jnp.pad(sketch_core, filler)
    sketched, part = sketch(core_two, right_sketch, sketch_core)
    sketched = sketched[:slices]
    bridge = gather_all(split_sum(part, "cuts"), both)
    bridge = bridge.reshape(cuts, ranks, -1, sketch_width).swapaxes(0, 1).reshape(width, sketch_width)

    padded = jnp.pad(sketched, ((0, share * ranks - slices), (0, 0), (0, 0)))
    blocks = []
    for offset in range(ranks):
        block = lax.dynamic_slice_in_dim(padded, (rank ^ offset) * share, share, 0)
        if offset:
            block = lax.ppermute(block, "rank", [(i, i ^ offset) for i in range(ranks)])
        blocks.append(block)

    flat_one = core_one.reshape(local_rows * slices, width)
    square = square_of(flat_one)
    square = square.reshape(cuts // 2, 2, ranks, -1, width)
    square = square.transpose(1, 2, 0, 3, 4).reshape(2 * ranks, cuts // 2, -1, width)
    square = scatter_sum(square, cut_steps[:1] + rank_steps[::-1])[0]
    groups = [list(range(core, cuts, 2)) for core in range(2)]
    own_square = jnp.sum(lax.all_to_all(square, "cuts", 0, 0, axis_index_groups=groups, tiled=True), axis=0)
    raw_rows = dot(own_square, bridge, ((1,), (0,)))
    raw = gather_all(raw_rows, both).reshape(width, sketch_width)
    gram = dot(bridge, raw, ((0,), (0,)))

    order = [lax.dynamic_slice_in_dim(raw, (rank ^ i) * local_rows, local_rows, 0) for i in range(ranks)]
    loose = loosen(jnp.concatenate(order, axis=0), blocks)
    first = share // 2
    pieces = []
    for piece, order in ((loose[:first], rank_steps), (loose[first:], rank_steps[::-1])):
        if piece.shape[0]:
            count = piece.shape[0]
            piece = piece[None]
            for step in order:
                piece = double(piece, step)
            if order is not rank_steps:
                bits = len(rank_steps)
                piece = piece.reshape((2,) * bits + piece.shape[1:])
                piece = piece.transpose(tuple(range(bits))[::-1] + tuple(range(bits, bits + 3)))
                piece = piece.reshape((ranks, count) + piece.shape[bits + 1:])
            pieces.append(piece)
    everyone = jnp.concatenate(pieces, axis=1)
    everyone = everyone.reshape((ranks * share,) + everyone.shape[2:])[:slices]

    inverse = invert_factor(gram)
    tight = jnp.einsum("bd,ndc->nbc", inverse, loose, precision=HIGHEST)
    flat_tight = tight.reshape(share * sketch_width, sketch_width)
    second_gram = total(dot(flat_tight, flat_tight, ((0,), (0,))), steps)
    second_inverse = invert_factor(second_gram)

    scale = jnp.sqrt(jnp.float32(local_rows * ranks * slices * cuts))
    solve = scale * dot(bridge, inverse, ((1,), (1,)))
    left_core = apply_to(flat_one, solve, 5).reshape(local_rows, slices, sketch_width)

    own_raw = lax.dynamic_slice_in_dim(raw, rank * local_rows, local_rows, 0)
    weight = dot(dot(own_raw, inverse, ((1,), (1,))), inverse, ((1,), (0,)))
    own_inverse = lax.dynamic_slice_in_dim(inverse, rank * band, band, 0)
    weight = jnp.concatenate([weight, own_inverse], axis=0)
    everyone = jnp.pad(everyone, ((0, -slices % BLOCK), (0, 0), (0, 0)))
    second_raw, rows = carry_rows(everyone, weight, core_two, band)
    second_raw = split_sum(second_raw, both)
    second_raw = gather_all(second_raw, both).reshape(width, sketch_width)
    carry = dot(second_inverse, second_raw, ((1,), (1,)))

    scale = jnp.sqrt(jnp.float32(sketch_width * slices * cuts))
    rows = rows[:, :slices].reshape(band * slices, sketch_width)
    middle_core = scale * dot(rows, second_inverse, ((1,), (1,)))
    middle_core = middle_core.reshape(band, slices, sketch_width)
    return (left_core, middle_core, carry)


def solution(mesh):
    placed = (P("rank", "cuts", None), P("rank", "cuts", None), P(), P(None, "cuts", None))
    return jax.shard_map(
        on_device,
        mesh=mesh,
        in_specs=placed,
        out_specs=(P("rank", "cuts", None), P("rank", "cuts", None), P()),
        check_vma=False,
    )
```

```python
import jax
import jax.numpy as jnp
from jax import lax
from jax.experimental import pallas as pl
from jax.experimental.pallas import tpu as pltpu
from jax.sharding import PartitionSpec as P

HIGHEST = lax.Precision.HIGHEST
NT = (((1,), (1,)), ((), ()))
NN = (((1,), (0,)), ((), ()))
TN = (((0,), (0,)), ((), ()))
VMEM_LIMIT = 56 * 1024 * 1024
BLOCK = 8


def call(kernel, flops, size, **more):
    return pl.pallas_call(
        kernel,
        compiler_params=pltpu.CompilerParams(vmem_limit_bytes=VMEM_LIMIT),
        cost_estimate=pl.CostEstimate(flops=flops, bytes_accessed=size, transcendentals=0),
        **more,
    )


def shape(*extent):
    return jax.ShapeDtypeStruct(extent, jnp.float32)


def split(value):
    high = value.astype(jnp.bfloat16)
    return high, (value - high.astype(jnp.float32)).astype(jnp.bfloat16)


def mxu(a, b, form):
    return lax.dot_general(a, b, form, preferred_element_type=jnp.float32)


def both_parts(value, axis):
    return jnp.concatenate(split(value), axis=axis)


def fold(value, axis):
    half = value.shape[axis] // 2
    return lax.slice_in_dim(value, 0, half, axis=axis) + lax.slice_in_dim(value, half, 2 * half, axis=axis)


def rows_of(ref):
    return ref.reshape(ref.shape[0] * ref.shape[1], ref.shape[2])


def sketch_kernel(core_ref, right_ref, left_ref, sketched_ref, part_ref, rows_ref):
    local_rows, block, _ = core_ref.shape
    columns = right_ref.shape[1]
    right = both_parts(right_ref[...], 1)
    high, low = split(rows_of(core_ref)[...])
    rows_ref[...] = fold(mxu(high, right, NN) + mxu(low, right, NN), 1)
    left_rows = rows_of(left_ref)

    @pl.when(pl.program_id(0) == 0)
    def _():
        part_ref[...] = jnp.zeros_like(part_ref)

    total = jnp.zeros(part_ref.shape, jnp.float32)
    for pair in range(0, block, 2):
        sides, lefts = [], []
        for n in (pair, pair + 1):
            rows = rows_ref[pl.ds(n, local_rows, stride=block), :]
            sketched_ref[n] = rows
            sides.append(rows)
            lefts.append(left_rows[pl.ds(n, columns, stride=block), :])
        high, low = split(jnp.concatenate(sides, axis=1))
        left = both_parts(jnp.concatenate(lefts, axis=1), 0)
        total = total + fold(mxu(high, left, NT) + mxu(low, left, NT), 1)
    part_ref[...] += total


def sketch(core_two, right_sketch, sketch_core):
    local_rows, slices, width = core_two.shape
    columns = right_sketch.shape[1]
    return call(
        sketch_kernel,
        2 * core_two.size * columns * 4,
        4 * (core_two.size + 2 * sketch_core.size),
        grid=(slices // BLOCK,),
        in_specs=[
            pl.BlockSpec((local_rows, BLOCK, width), lambda i: (0, i, 0)),
            pl.BlockSpec((width, columns), lambda i: (0, 0)),
            pl.BlockSpec((columns, BLOCK, columns), lambda i: (0, i, 0)),
        ],
        out_specs=[
            pl.BlockSpec((BLOCK, local_rows, columns), lambda i: (i, 0, 0)),
            pl.BlockSpec((local_rows, columns), lambda i: (0, 0)),
        ],
        out_shape=[shape(slices, local_rows, columns), shape(local_rows, columns)],
        scratch_shapes=[pltpu.VMEM((local_rows * BLOCK, columns), jnp.float32)],
    )(core_two, right_sketch, sketch_core)


def square_kernel(core_ref, square_ref, same_ref, cross_ref):
    step = pl.program_id(0)
    high, low = split(core_ref[...])

    @pl.when(step == 0)
    def _():
        same_ref[...] = jnp.zeros_like(same_ref)
        cross_ref[...] = jnp.zeros_like(cross_ref)

    same_ref[...] += mxu(high, high, TN)
    cross_ref[...] += mxu(high, low, TN)

    @pl.when(step == pl.num_programs(0) - 1)
    def _():
        cross = cross_ref[...]
        square_ref[...] = same_ref[...] + cross + cross.T


def square_of(flat_one):
    rows, width = flat_one.shape
    block = rows // 10
    return call(
        square_kernel,
        4 * rows * width * width,
        4 * flat_one.size,
        grid=(10,),
        in_specs=[pl.BlockSpec((block, width), lambda i: (i, 0))],
        out_specs=pl.BlockSpec((width, width), lambda i: (0, 0)),
        out_shape=shape(width, width),
        scratch_shapes=[pltpu.VMEM((width, width), jnp.float32)] * 2,
    )(flat_one)


def loose_kernel(raw_ref, *refs):
    block_refs, out_ref = refs[:-1], refs[-1]
    count, local_rows, columns = block_refs[0].shape
    raw = both_parts(raw_ref[...], 1)
    for n in range(count):
        high, low = split(jnp.concatenate([ref[n] for ref in block_refs], axis=0))
        out_ref[n] = fold(mxu(raw, high, TN) + mxu(raw, low, TN), 0)


def loosen(raw, blocks):
    count, local_rows, columns = blocks[0].shape
    return call(
        loose_kernel,
        8 * raw.size * count * columns,
        4 * raw.size + 4 * len(blocks) * blocks[0].size,
        out_shape=shape(count, raw.shape[1], columns),
    )(raw, *blocks)


def carry_kernel(everyone_ref, weight_ref, core_ref, raw_ref, middle_ref, rows_ref, sum_ref):
    step = pl.program_id(0)
    block, columns, _ = everyone_ref.shape
    local_rows = core_ref.shape[0]
    band = middle_ref.shape[0]
    weight_high, weight_low = split(weight_ref[...])
    everyone = jnp.concatenate([everyone_ref[n] for n in range(block)], axis=1)
    high, low = split(everyone)
    spread = mxu(weight_high, high, NN) + mxu(weight_high, low, NN) + mxu(weight_low, high, NN)
    middle_rows = rows_of(middle_ref)
    for n in range(block):
        piece = lax.slice_in_dim(spread, n * columns, (n + 1) * columns, axis=1)
        rows_ref[pl.ds(n, local_rows, stride=block), :] = piece[:local_rows]
        middle_rows[pl.ds(n, band, stride=block), :] = piece[local_rows:]
    rows = both_parts(rows_ref[...], 1)
    high, low = split(rows_of(core_ref)[...])

    @pl.when(step == 0)
    def _():
        sum_ref[...] = jnp.zeros_like(sum_ref)

    total = fold(mxu(rows, high, TN) + mxu(rows, low, TN), 0)
    sum_ref[...] += total

    @pl.when(step == pl.num_programs(0) - 1)
    def _():
        raw_ref[...] = sum_ref[...].T


def carry_rows(everyone, weight, core_two, band):
    local_rows, slices, width = core_two.shape
    columns = everyone.shape[2]
    return call(
        carry_kernel,
        2 * core_two.size * columns * 4,
        4 * core_two.size + 4 * everyone.size,
        grid=(slices // BLOCK,),
        in_specs=[
            pl.BlockSpec((BLOCK, columns, columns), lambda i: (i, 0, 0)),
            pl.BlockSpec((local_rows + band, columns), lambda i: (0, 0)),
            pl.BlockSpec((local_rows, BLOCK, width), lambda i: (0, i, 0)),
        ],
        out_specs=[
            pl.BlockSpec((width, columns), lambda i: (0, 0)),
            pl.BlockSpec((band, BLOCK, columns), lambda i: (0, i, 0)),
        ],
        out_shape=[shape(width, columns), shape(band, slices, columns)],
        scratch_shapes=[
            pltpu.VMEM((local_rows * BLOCK, columns), jnp.float32),
            pltpu.VMEM((columns, width), jnp.float32),
        ],
    )(everyone, weight, core_two)


def apply_kernel(rows_ref, weight_ref, out_ref):
    weight = both_parts(weight_ref[...], 1)
    high, low = split(rows_ref[...])
    out_ref[...] = fold(mxu(high, weight, NN) + mxu(low, weight, NN), 1)


def apply_to(rows, weight, steps):
    count, width = rows.shape
    columns = weight.shape[1]
    return call(
        apply_kernel,
        8 * rows.size * columns,
        4 * (rows.size + count * columns),
        grid=(steps,),
        in_specs=[
            pl.BlockSpec((count // steps, width), lambda i: (i, 0)),
            pl.BlockSpec((width, columns), lambda i: (0, 0)),
        ],
        out_specs=pl.BlockSpec((count // steps, columns), lambda i: (i, 0)),
        out_shape=shape(count, columns),
    )(rows, weight)


def axis_bits(axis):
    return [(axis, bit) for bit in range((lax.axis_size(axis) - 1).bit_length())]


def swap(value, step):
    axis, bit = step
    pairs = [(i, i ^ (1 << bit)) for i in range(lax.axis_size(axis))]
    return lax.ppermute(value, axis, pairs)


def side(step):
    axis, bit = step
    return lax.rem(lax.div(lax.axis_index(axis), 1 << bit), 2)


def halve(value, step):
    half = value.shape[0] // 2
    own = side(step)
    keep = lax.dynamic_slice_in_dim(value, own * half, half, 0)
    give = lax.dynamic_slice_in_dim(value, (1 - own) * half, half, 0)
    return keep + swap(give, step)


def double(value, step):
    other = swap(value, step)
    own = side(step) == 0
    return jnp.concatenate([jnp.where(own, value, other), jnp.where(own, other, value)], axis=0)


def scatter_sum(value, steps):
    for step in steps:
        value = halve(value, step)
    return value


def gather(value, steps):
    for step in reversed(steps):
        value = double(value, step)
    return value


def total(value, steps):
    for step in steps:
        value = value + swap(value, step)
    return value


def exchange(value, axes):
    return lax.all_to_all(value, axes, 0, 0, tiled=True)


def split_blocks(blocks, groups):
    return jnp.sum(lax.all_to_all(blocks, ("cuts", "rank"), 0, 0, axis_index_groups=groups, tiled=True), axis=0)


def split_sum(value, axes):
    parts = lax.axis_size(axes)
    blocks = value.reshape((parts, value.shape[0] // parts) + value.shape[1:])
    return jnp.sum(exchange(blocks, axes), axis=0)


def gather_all(value, axes):
    parts = lax.axis_size(axes)
    return exchange(jnp.broadcast_to(value[None], (parts,) + value.shape), axes)


def small_inverse(entry):
    size = len(entry)
    entry = [list(row) for row in entry]
    inverse = [[None] * size for _ in range(size)]
    for k in range(size):
        pivot = entry[k][k]
        root = lax.rsqrt(pivot)
        root = root * (1.5 - 0.5 * pivot * root * root)
        inverse[k][k] = root
        for i in range(k + 1, size):
            entry[i][k] = entry[i][k] * root
        for i in range(k + 1, size):
            for m in range(k + 1, i + 1):
                entry[i][m] = entry[i][m] - entry[i][k] * entry[m][k]
    for k in range(size):
        for i in range(k + 1, size):
            total = entry[i][k] * inverse[k][k]
            for m in range(k + 1, i):
                total = total + entry[i][m] * inverse[m][k]
            inverse[i][k] = -total * inverse[i][i]
    return inverse


def factor_kernel(gram_ref, inverse_ref):
    size, tile = gram_ref.shape[0], BLOCK
    count = size // tile
    left = [gram_ref[pl.ds(i * tile, tile), :] for i in range(count)]
    lane = lax.broadcasted_iota(jnp.int32, (tile, size), 1)
    sublane = lax.broadcasted_iota(jnp.int32, (tile, size), 0)
    right = [jnp.where(lane == sublane + i * tile, 1.0, 0.0) for i in range(count)]

    def spread(value, row, column):
        return jnp.broadcast_to(value[row:row + 1, column:column + 1], (tile, size))

    for j in range(count):
        corner = [[spread(left[j], i, j * tile + k) for k in range(i + 1)] for i in range(tile)]
        small = small_inverse(corner)
        columns = []
        for k in range(tile):
            column = jnp.where(sublane == k, small[k][k], 0.0)
            for i in range(k + 1, tile):
                column = jnp.where(sublane == i, small[i][k], column)
            columns.append(column)
        done_left = sum(columns[k] * left[j][k:k + 1, :] for k in range(tile))
        done_right = sum(columns[k] * right[j][k:k + 1, :] for k in range(tile))
        inverse_ref[pl.ds(j * tile, tile), :] = done_right
        if j + 1 < count:
            turned = done_left.T
            for i in range(j + 1, count):
                for k in range(tile):
                    factor = jnp.broadcast_to(turned[i * tile:(i + 1) * tile, k:k + 1], (tile, size))
                    left[i] = left[i] - factor * done_left[k:k + 1, :]
                    right[i] = right[i] - factor * done_right[k:k + 1, :]


def invert_factor(gram):
    return call(
        factor_kernel,
        4 * gram.size * gram.shape[0],
        8 * gram.size,
        out_shape=shape(*gram.shape),
    )(gram)


def dot(a, b, contract, precision=HIGHEST):
    return lax.dot_general(
        a, b, (contract, ((), ())), precision=precision, preferred_element_type=jnp.float32
    )


def on_device(core_one, core_two, right_sketch, sketch_core):
    local_rows, slices, width = core_one.shape
    sketch_width = right_sketch.shape[1]
    ranks, cuts = lax.axis_size("rank"), lax.axis_size("cuts")
    rank = lax.axis_index("rank")
    band = sketch_width // ranks
    cut_steps, rank_steps = axis_bits("cuts"), axis_bits("rank")
    steps = cut_steps[:1] + rank_steps + cut_steps[1:]
    both = ("cuts", "rank")
    core_groups = [
        [cut * ranks + place for cut in range(core, cuts, 2) for place in range(ranks)] for core in range(2)
    ]
    share = -(-slices // ranks)

    filler = ((0, 0), (0, -slices % BLOCK), (0, 0))
    core_two, sketch_core = jnp.pad(core_two, filler), jnp.pad(sketch_core, filler)
    sketched, part = sketch(core_two, right_sketch, sketch_core)
    sketched = sketched[:slices]
    bridge = gather_all(split_sum(part, "cuts"), both)
    bridge = bridge.reshape(cuts, ranks, -1, sketch_width).swapaxes(0, 1).reshape(width, sketch_width)

    padded = jnp.pad(sketched, ((0, share * ranks - slices), (0, 0), (0, 0)))
    blocks = []
    for offset in range(ranks):
        block = lax.dynamic_slice_in_dim(padded, (rank ^ offset) * share, share, 0)
        if offset:
            block = lax.ppermute(block, "rank", [(i, i ^ offset) for i in range(ranks)])
        blocks.append(block)

    flat_one = core_one.reshape(local_rows * slices, width)
    square = square_of(flat_one)
    square = square.reshape(2, ranks * cuts // 2, -1, width)
    square = halve(square, cut_steps[0])[0]
    own_square = split_blocks(square, core_groups)
    raw_rows = dot(own_square, bridge, ((1,), (0,)))
    raw = gather_all(raw_rows, both).reshape(cuts // 2, 2, ranks, -1, sketch_width)
    raw = raw.transpose(1, 0, 2, 3, 4).reshape(width, sketch_width)
    gram = dot(bridge, raw, ((0,), (0,)))

    order = [lax.dynamic_slice_in_dim(raw, (rank ^ i) * local_rows, local_rows, 0) for i in range(ranks)]
    loose = loosen(jnp.concatenate(order, axis=0), blocks)
    gram, loose = lax.optimization_barrier((gram, loose))
    first = share // 2
    pieces = []
    for piece, order in ((loose[:first], rank_steps), (loose[first:], rank_steps[::-1])):
        if piece.shape[0]:
            count = piece.shape[0]
            piece = piece[None]
            for step in order:
                piece = double(piece, step)
            if order is not rank_steps:
                bits = len(rank_steps)
                piece = piece.reshape((2,) * bits + piece.shape[1:])
                piece = piece.transpose(tuple(range(bits))[::-1] + tuple(range(bits, bits + 3)))
                piece = piece.reshape((ranks, count) + piece.shape[bits + 1:])
            pieces.append(piece)
    everyone = jnp.concatenate(pieces, axis=1)
    everyone = everyone.reshape((ranks * share,) + everyone.shape[2:])[:slices]

    inverse = invert_factor(gram)
    tight = jnp.einsum("bd,ndc->nbc", inverse, loose, precision=HIGHEST)
    flat_tight = tight.reshape(share * sketch_width, sketch_width)
    second_gram = total(dot(flat_tight, flat_tight, ((0,), (0,))), steps)
    second_inverse = invert_factor(second_gram)

    scale = jnp.sqrt(jnp.float32(local_rows * ranks * slices * cuts))
    solve = scale * dot(bridge, inverse, ((1,), (1,)))
    left_core = apply_to(flat_one, solve, 5).reshape(local_rows, slices, sketch_width)

    own_raw = lax.dynamic_slice_in_dim(raw, rank * local_rows, local_rows, 0)
    weight = dot(dot(own_raw, inverse, ((1,), (1,))), inverse, ((1,), (0,)))
    own_inverse = lax.dynamic_slice_in_dim(inverse, rank * band, band, 0)
    weight = jnp.concatenate([weight, own_inverse], axis=0)
    everyone = jnp.pad(everyone, ((0, -slices % BLOCK), (0, 0), (0, 0)))
    second_raw, rows = carry_rows(everyone, weight, core_two, band)
    second_raw = split_sum(second_raw, both)
    second_raw = gather_all(second_raw, both).reshape(width, sketch_width)
    carry = dot(second_inverse, second_raw, ((1,), (1,)))

    scale = jnp.sqrt(jnp.float32(sketch_width * slices * cuts))
    rows = rows[:, :slices].reshape(band * slices, sketch_width)
    middle_core = scale * dot(rows, second_inverse, ((1,), (1,)))
    middle_core = middle_core.reshape(band, slices, sketch_width)
    return (left_core, middle_core, carry)


def solution(mesh):
    placed = (P("rank", "cuts", None), P("rank", "cuts", None), P(), P(None, "cuts", None))
    return jax.shard_map(
        on_device,
        mesh=mesh,
        in_specs=placed,
        out_specs=(P("rank", "cuts", None), P("rank", "cuts", None), P()),
        check_vma=False,
    )
```

```python
import functools
import math

import jax
import jax.numpy as jnp
from jax import lax
from jax.experimental import pallas as pl
from jax.experimental.pallas import tpu as pltpu
from jax.sharding import PartitionSpec as P

NT = (((1,), (1,)), ((), ()))
NN = (((1,), (0,)), ((), ()))
TN = (((0,), (0,)), ((), ()))
VMEM_LIMIT = 56 * 1024 * 1024
BLOCK = 8


def call(kernel, flops, size, **more):
    return pl.pallas_call(
        kernel,
        compiler_params=pltpu.CompilerParams(vmem_limit_bytes=VMEM_LIMIT),
        cost_estimate=pl.CostEstimate(flops=flops, bytes_accessed=size, transcendentals=0),
        **more,
    )


def shape(*extent):
    return jax.ShapeDtypeStruct(extent, jnp.float32)


def split(value):
    high = value.astype(jnp.bfloat16)
    return high, (value - high.astype(jnp.float32)).astype(jnp.bfloat16)


def mxu(a, b, form):
    return lax.dot_general(a, b, form, preferred_element_type=jnp.float32)


def exact(a, b, form):
    return lax.dot_general(a, b, form, precision=lax.Precision.HIGHEST, preferred_element_type=jnp.float32)


def both_parts(value, axis):
    return jnp.concatenate(split(value), axis=axis)


def fold(value, axis):
    half = value.shape[axis] // 2
    return lax.slice_in_dim(value, 0, half, axis=axis) + lax.slice_in_dim(value, half, 2 * half, axis=axis)


def rows_of(ref):
    return ref.reshape(ref.shape[0] * ref.shape[1], ref.shape[2])


def sketch_kernel(core_ref, right_ref, left_ref, sketched_ref, part_ref, rows_ref):
    local_rows, block, _ = core_ref.shape
    columns = right_ref.shape[1]
    right = both_parts(right_ref[...], 1)
    product = mxu(both_parts(rows_of(core_ref)[...], 0), right, NN)
    rows_ref[...] = fold(fold(product, 0), 1)
    left_rows = rows_of(left_ref)

    @pl.when(pl.program_id(0) == 0)
    def _():
        part_ref[...] = jnp.zeros_like(part_ref)

    total = jnp.zeros(part_ref.shape, jnp.float32)
    for pair in range(0, block, 2):
        sides, lefts = [], []
        for n in (pair, pair + 1):
            rows = rows_ref[pl.ds(n, local_rows, stride=block), :]
            sketched_ref[n] = rows
            sides.append(rows)
            lefts.append(left_rows[pl.ds(n, columns, stride=block), :])
        side = both_parts(jnp.concatenate(sides, axis=1), 0)
        left = both_parts(jnp.concatenate(lefts, axis=1), 0)
        total = total + fold(fold(mxu(side, left, NT), 0), 1)
    part_ref[...] += total


def sketch(core_two, right_sketch, sketch_core):
    local_rows, slices, width = core_two.shape
    columns = right_sketch.shape[1]
    return call(
        sketch_kernel,
        2 * core_two.size * columns * 4,
        4 * (core_two.size + 2 * sketch_core.size),
        grid=(slices // BLOCK,),
        in_specs=[
            pl.BlockSpec((local_rows, BLOCK, width), lambda i: (0, i, 0)),
            pl.BlockSpec((width, columns), lambda i: (0, 0)),
            pl.BlockSpec((columns, BLOCK, columns), lambda i: (0, i, 0)),
        ],
        out_specs=[
            pl.BlockSpec((BLOCK, local_rows, columns), lambda i: (i, 0, 0)),
            pl.BlockSpec((local_rows, columns), lambda i: (0, 0)),
        ],
        out_shape=[shape(slices, local_rows, columns), shape(local_rows, columns)],
        scratch_shapes=[pltpu.VMEM((local_rows * BLOCK, columns), jnp.float32)],
    )(core_two, right_sketch, sketch_core)


def block_of(rows):
    block = 1024
    while rows % block:
        block //= 2
    return block


def square_kernel(core_ref, core_index_ref, keep_ref, give_ref, sum_ref):
    step = pl.program_id(0)
    width = core_ref.shape[1]
    high, low = split(core_ref[...])

    @pl.when(step == 0)
    def _():
        sum_ref[...] = jnp.zeros_like(sum_ref)

    sum_ref[...] += mxu(high, jnp.concatenate([high, low], axis=1), TN)

    @pl.when(step == pl.num_programs(0) - 1)
    def _():
        cross = sum_ref[:, width:]
        sum_ref[:, :width] = sum_ref[:, :width] + cross + cross.T
        half = width // 2
        own = core_index_ref[0]
        keep_ref[...] = sum_ref[pl.ds(pl.multiple_of(own * half, half), half), :width]
        give_ref[...] = sum_ref[pl.ds(pl.multiple_of((1 - own) * half, half), half), :width]


def square_of(flat_one, core_index):
    rows, width = flat_one.shape
    block = block_of(rows)
    half = pl.BlockSpec((width // 2, width), lambda i: (0, 0))
    return call(
        square_kernel,
        4 * rows * width * width,
        4 * flat_one.size,
        grid=(rows // block,),
        in_specs=[
            pl.BlockSpec((block, width), lambda i: (i, 0)),
            pl.BlockSpec(memory_space=pltpu.SMEM),
        ],
        out_specs=[half, half],
        out_shape=[shape(width // 2, width)] * 2,
        scratch_shapes=[pltpu.VMEM((width, 2 * width), jnp.float32)],
    )(flat_one, core_index)


def loose_kernel(halves, rank_ref, raw_ref, *refs):
    piece_refs, out_refs = refs[:-len(halves)], refs[-len(halves):]
    ranks = len(piece_refs) // len(halves)
    local_rows = piece_refs[0].shape[1]
    rows = []
    for offset in range(ranks):
        start = pl.multiple_of((rank_ref[0] ^ offset) * local_rows, local_rows)
        rows.append(raw_ref[pl.ds(start, local_rows), :])
    raw = both_parts(jnp.concatenate(rows, axis=0), 1).T
    for half, count in enumerate(halves):
        refs = piece_refs[half * ranks:(half + 1) * ranks]
        for n in range(count):
            value = jnp.concatenate([ref[n] for ref in refs], axis=0)
            product = mxu(raw, jnp.concatenate(split(value), axis=1), NN)
            out_refs[half][n] = fold(fold(product, 0), 1)


def loosen(rank_index, raw, pieces, halves):
    columns = raw.shape[1]
    size = sum(piece.size for piece in pieces)
    whole = pl.BlockSpec(memory_space=pltpu.VMEM)
    return call(
        functools.partial(loose_kernel, halves),
        8 * size * columns,
        4 * raw.size + 4 * size,
        in_specs=[pl.BlockSpec(memory_space=pltpu.SMEM)] + [whole] * (len(pieces) + 1),
        out_specs=[whole] * len(halves),
        out_shape=[shape(count, columns, columns) for count in halves],
    )(rank_index, raw, *pieces)


def carry_kernel(halves, share, rank_ref, weight_ref, core_ref, *refs):
    piece_refs = refs[:-4]
    joined_ref, middle_ref, rows_ref, sum_ref = refs[-4:]
    step = pl.program_id(0)
    block, width = core_ref.shape
    columns = weight_ref.shape[1]
    ranks = len(piece_refs) // len(halves)
    room = share * ranks
    local_rows = rows_ref.shape[0] // room
    band = middle_ref.shape[0] // room

    @pl.when(step == 0)
    def _():
        sum_ref[...] = jnp.zeros_like(sum_ref)
        weight_high, weight_low = split(weight_ref[...])
        weight = jnp.concatenate([weight_high, weight_low], axis=0)
        for half, count in enumerate(halves):
            for offset in range(ranks):
                ref = piece_refs[half * ranks + offset]
                first = (rank_ref[0] ^ offset) * share + sum(halves[:half])
                high, low = split(jnp.concatenate([ref[n] for n in range(count)], axis=1))
                spread = fold(mxu(weight, high, NN), 0) + mxu(weight_high, low, NN)
                for n in range(count):
                    piece = lax.slice_in_dim(spread, n * columns, (n + 1) * columns, axis=1)
                    rows_ref[pl.ds(first + n, local_rows, stride=room), :] = piece[:local_rows]
                    middle_ref[pl.ds(first + n, band, stride=room), :] = piece[local_rows:]

    rows = both_parts(rows_ref[pl.ds(pl.multiple_of(step * block, block), block), :], 1)
    product = mxu(rows, both_parts(core_ref[...], 1), TN)
    product = fold(fold(product, 0), 1)
    sum_ref[...] += product

    @pl.when(step == pl.num_programs(0) - 1)
    def _():
        joined_ref[:width, :] = sum_ref[...].T
        middle = both_parts(middle_ref[...], 1)
        joined_ref[width:, :] = fold(fold(mxu(middle, middle, TN), 0), 1)


def carry_rows(rank_index, weight, flat_two, pieces, halves, share, band):
    rows, width = flat_two.shape
    columns = weight.shape[1]
    block = block_of(rows)
    ranks = len(pieces) // len(halves)
    whole = pl.BlockSpec(memory_space=pltpu.VMEM)
    return call(
        functools.partial(carry_kernel, halves, share),
        8 * flat_two.size * columns,
        4 * flat_two.size + 4 * sum(piece.size for piece in pieces),
        grid=(rows // block,),
        in_specs=[
            pl.BlockSpec(memory_space=pltpu.SMEM),
            pl.BlockSpec((weight.shape[0], columns), lambda i: (0, 0)),
            pl.BlockSpec((block, width), lambda i: (i, 0)),
        ]
        + [pl.BlockSpec(piece.shape, lambda i: (0, 0, 0)) for piece in pieces],
        out_specs=[
            pl.BlockSpec((width + columns, columns), lambda i: (0, 0)),
            pl.BlockSpec((band * share * ranks, columns), lambda i: (0, 0)),
        ],
        out_shape=[shape(width + columns, columns), shape(band * share * ranks, columns)],
        scratch_shapes=[pltpu.VMEM((rows, columns), jnp.float32), pltpu.VMEM((columns, width), jnp.float32)],
    )(rank_index, weight, flat_two, *pieces)


def apply_kernel(rows_ref, weight_ref, out_ref):
    weight = both_parts(weight_ref[...], 1)
    product = mxu(both_parts(rows_ref[...], 0), weight, NN)
    out_ref[...] = fold(fold(product, 0), 1)


def apply_to(rows, weight):
    count, width = rows.shape
    columns = weight.shape[1]
    block = block_of(count)
    return call(
        apply_kernel,
        8 * rows.size * columns,
        4 * (rows.size + count * columns),
        grid=(count // block,),
        in_specs=[
            pl.BlockSpec((block, width), lambda i: (i, 0)),
            pl.BlockSpec((width, columns), lambda i: (0, 0)),
        ],
        out_specs=pl.BlockSpec((block, columns), lambda i: (i, 0)),
        out_shape=shape(count, columns),
    )(rows, weight)


def small_inverse(entry):
    size = len(entry)
    entry = [list(row) for row in entry]
    inverse = [[None] * size for _ in range(size)]
    for k in range(size):
        pivot = entry[k][k]
        root = lax.rsqrt(pivot)
        root = root * (1.5 - 0.5 * pivot * root * root)
        inverse[k][k] = root
        for i in range(k + 1, size):
            entry[i][k] = entry[i][k] * root
        for i in range(k + 1, size):
            for m in range(k + 1, i + 1):
                entry[i][m] = entry[i][m] - entry[i][k] * entry[m][k]
    for k in range(size):
        for i in range(k + 1, size):
            total = entry[i][k] * inverse[k][k]
            for m in range(k + 1, i):
                total = total + entry[i][m] * inverse[m][k]
            inverse[i][k] = -total * inverse[i][i]
    return inverse


def factor(gram, inverse_ref):
    size, tile = gram.shape[0], BLOCK
    count = size // tile
    left = [gram[i * tile:(i + 1) * tile, :] for i in range(count)]
    lane = lax.broadcasted_iota(jnp.int32, (tile, size), 1)
    sublane = lax.broadcasted_iota(jnp.int32, (tile, size), 0)
    right = [jnp.where(lane == sublane + i * tile, 1.0, 0.0) for i in range(count)]

    def spread(value, row, column):
        return jnp.broadcast_to(value[row:row + 1, column:column + 1], (tile, size))

    for j in range(count):
        corner = [[spread(left[j], i, j * tile + k) for k in range(i + 1)] for i in range(tile)]
        small = small_inverse(corner)
        columns = []
        for k in range(tile):
            column = jnp.where(sublane == k, small[k][k], 0.0)
            for i in range(k + 1, tile):
                column = jnp.where(sublane == i, small[i][k], column)
            columns.append(column)
        done_left = sum(columns[k] * left[j][k:k + 1, :] for k in range(tile))
        done_right = sum(columns[k] * right[j][k:k + 1, :] for k in range(tile))
        inverse_ref[pl.ds(j * tile, tile), :] = done_right
        if j + 1 < count:
            turned = done_left.T
            for i in range(j + 1, count):
                for k in range(tile):
                    factor = jnp.broadcast_to(turned[i * tile:(i + 1) * tile, k:k + 1], (tile, size))
                    left[i] = left[i] - factor * done_left[k:k + 1, :]
                    right[i] = right[i] - factor * done_right[k:k + 1, :]


def first_kernel(scale, band, rank_ref, bridge_ref, raw_ref, weight_ref, solve_ref, inverse_ref):
    local_rows = weight_ref.shape[0] - band
    factor(exact(bridge_ref[...], raw_ref[...], TN), inverse_ref)
    inverse = inverse_ref[...]
    start = pl.multiple_of(rank_ref[0] * local_rows, local_rows)
    own = exact(raw_ref[pl.ds(start, local_rows), :], inverse, NT)
    weight_ref[:local_rows, :] = exact(own, inverse, NN)
    weight_ref[local_rows:, :] = inverse_ref[pl.ds(pl.multiple_of(rank_ref[0] * band, band), band), :]
    solve_ref[...] = scale * exact(bridge_ref[...], inverse, NT)


def first_factor(rank_index, bridge, raw, scale, local_rows, band):
    columns = raw.shape[1]
    whole = pl.BlockSpec(memory_space=pltpu.VMEM)
    return call(
        functools.partial(first_kernel, scale, band),
        8 * raw.size * columns,
        16 * raw.size,
        in_specs=[pl.BlockSpec(memory_space=pltpu.SMEM), whole, whole],
        out_specs=[whole, whole],
        out_shape=[shape(local_rows + band, columns), shape(*raw.shape)],
        scratch_shapes=[pltpu.VMEM((columns, columns), jnp.float32)],
    )(rank_index, bridge, raw)


def last_kernel(scale, joined_ref, middle_ref, carry_ref, out_ref, inverse_ref):
    columns = inverse_ref.shape[0]
    width = carry_ref.shape[1]
    factor(joined_ref[pl.ds(width, columns), :], inverse_ref)
    inverse = inverse_ref[...]
    carry_ref[...] = exact(inverse, joined_ref[pl.ds(0, width), :], NT)
    out_ref[...] = exact(middle_ref[...], scale * inverse, NT)


def last_factor(joined, middle, scale, width):
    columns = joined.shape[1]
    whole = pl.BlockSpec(memory_space=pltpu.VMEM)
    return call(
        functools.partial(last_kernel, scale),
        8 * middle.size * columns,
        8 * middle.size,
        in_specs=[whole, whole],
        out_specs=[whole, whole],
        out_shape=[shape(columns, width), shape(*middle.shape)],
        scratch_shapes=[pltpu.VMEM((columns, columns), jnp.float32)],
    )(joined, middle)


def swap(value, axis, offset):
    return lax.ppermute(value, axis, [(i, i ^ offset) for i in range(lax.axis_size(axis))])


def exchange(value, axes, groups=None):
    return lax.all_to_all(value, axes, 0, 0, axis_index_groups=groups, tiled=True)


def gather_all(value, axes):
    parts = lax.axis_size(axes)
    return exchange(jnp.broadcast_to(value[None], (parts,) + value.shape), axes)


def after(value, others):
    return lax.optimization_barrier((value, others))


def on_device(core_one, core_two, right_sketch, sketch_core):
    local_rows, slices, width = core_one.shape
    columns = right_sketch.shape[1]
    ranks, cuts = lax.axis_size("rank"), lax.axis_size("cuts")
    rank, cut = lax.axis_index("rank"), lax.axis_index("cuts")
    rank_index = rank.astype(jnp.int32).reshape(1)
    core_index = lax.rem(cut, 2).astype(jnp.int32).reshape(1)
    both = ("cuts", "rank")
    parts = ranks * cuts
    band = columns // ranks
    share = -(-slices // ranks)
    room = share * ranks
    halves = [share // 2, share - share // 2]
    core_groups = [
        [z * ranks + place for z in range(core, cuts, 2) for place in range(ranks)] for core in range(2)
    ]
    filler = ((0, 0), (0, room - slices), (0, 0))
    core_two, sketch_core = jnp.pad(core_two, filler), jnp.pad(sketch_core, filler)
    flat_one = core_one.reshape(local_rows * slices, width)
    flat_two = core_two.reshape(local_rows * room, width)

    sketched, part = sketch(core_two, right_sketch, sketch_core)

    def piece(half, offset):
        start = (rank ^ offset) * share + half * halves[0]
        return lax.dynamic_slice_in_dim(sketched, start, halves[half], 0)

    def send(names, behind):
        found = [piece(*name) for name in names]
        if behind is not None:
            found, _ = after(found, behind)
        return {name: swap(value, "rank", name[1]) for name, value in zip(names, found)}

    far = ranks - 1
    pieces = {(half, 0): piece(half, 0) for half in range(2)}
    near = [[(half, offset) for offset in range(1, far)] for half in range(2)]

    moved = send(near[0], None)
    bridge_rows = jnp.sum(exchange(part.reshape(cuts, local_rows // cuts, columns), "cuts"), axis=0)
    flat_late, part = after(flat_one, part)
    keep, give = square_of(flat_late, core_index)
    bridge_rows, moved = after(bridge_rows, moved)
    pieces.update(moved)

    moved = send(near[1], bridge_rows)
    bridge = gather_all(bridge_rows, both)
    bridge = bridge.reshape(cuts, ranks, -1, columns).swapaxes(0, 1).reshape(width, columns)
    square = keep + swap(give, "cuts", 1)
    square, moved = after(square, moved)
    pieces.update(moved)

    moved = send([(0, far)], square)
    square = exchange(square.reshape(parts // 2, -1, width), both, core_groups)
    raw_rows = exact(jnp.sum(square, axis=0), bridge, NN)
    raw_rows, moved = after(raw_rows, moved)
    pieces.update(moved)

    pieces.update(send([(1, far)], raw_rows))
    raw = gather_all(raw_rows, both).reshape(cuts // 2, 2, ranks, -1, columns)
    raw = raw.transpose(1, 0, 2, 3, 4).reshape(width, columns)

    ordered = [pieces[(half, offset)] for half in range(2) for offset in range(ranks)]
    loose = loosen(rank_index, raw, ordered, halves)
    loose, (bridge, raw) = after(loose, (bridge, raw))

    bits = [1 << bit for bit in range((ranks - 1).bit_length())]
    everyone = []
    for value, order in zip(loose, (bits, bits[::-1])):
        found = {0: value}
        for bit in order:
            found.update({offset ^ bit: swap(held, "rank", bit) for offset, held in list(found.items())})
        everyone += [found[offset] for offset in range(ranks)]

    scale = math.sqrt(local_rows * ranks * slices * cuts)
    weight, solve = first_factor(rank_index, bridge, raw, scale, local_rows, band)
    joined, middle = carry_rows(rank_index, weight, flat_two, everyone, halves, share, band)
    total = joined.shape[0]
    joined = jnp.pad(joined, ((0, -total % parts), (0, 0))).reshape(parts, -1, columns)
    joined = jnp.sum(exchange(joined, both), axis=0)
    joined = lax.all_gather(joined, both, axis=0, tiled=True)[:total]
    left_core = apply_to(flat_one, solve).reshape(local_rows, slices, columns)
    scale = math.sqrt(columns * slices * cuts)
    carry, middle = last_factor(joined, middle, scale, width)
    middle_core = middle.reshape(band, room, columns)[:, :slices]
    return (left_core, middle_core, carry)


def solution(mesh):
    placed = (P("rank", "cuts", None), P("rank", "cuts", None), P(), P(None, "cuts", None))
    return jax.shard_map(
        on_device,
        mesh=mesh,
        in_specs=placed,
        out_specs=(P("rank", "cuts", None), P("rank", "cuts", None), P()),
        check_vma=False,
    )
```

```python
import functools
import math

import jax
import jax.numpy as jnp
from jax import lax
from jax.experimental import pallas as pl
from jax.experimental.pallas import tpu as pltpu
from jax.sharding import PartitionSpec as P

NT = (((1,), (1,)), ((), ()))
NN = (((1,), (0,)), ((), ()))
TN = (((0,), (0,)), ((), ()))
VMEM_LIMIT = 56 * 1024 * 1024
BLOCK = 8


def call(kernel, flops, size, **more):
    return pl.pallas_call(
        kernel,
        compiler_params=pltpu.CompilerParams(vmem_limit_bytes=VMEM_LIMIT),
        cost_estimate=pl.CostEstimate(flops=flops, bytes_accessed=size, transcendentals=0),
        **more,
    )


def shape(*extent):
    return jax.ShapeDtypeStruct(extent, jnp.float32)


def split(value):
    high = value.astype(jnp.bfloat16)
    return high, (value - high.astype(jnp.float32)).astype(jnp.bfloat16)


def mxu(a, b, form):
    return lax.dot_general(a, b, form, preferred_element_type=jnp.float32)


def exact(a, b, form):
    return lax.dot_general(a, b, form, precision=lax.Precision.HIGHEST, preferred_element_type=jnp.float32)


def both_parts(value, axis):
    return jnp.concatenate(split(value), axis=axis)


def twice(value, axis):
    return jnp.concatenate([value, value], axis=axis)


def fold(value, axis):
    half = value.shape[axis] // 2
    return lax.slice_in_dim(value, 0, half, axis=axis) + lax.slice_in_dim(value, half, 2 * half, axis=axis)


def rows_of(ref):
    return ref.reshape(ref.shape[0] * ref.shape[1], ref.shape[2])


def sketch_kernel(core_ref, right_ref, left_ref, sketched_ref, part_ref, rows_ref):
    local_rows, block, _ = core_ref.shape
    columns = right_ref.shape[1]
    right = twice(both_parts(right_ref[...], 1), 0)
    rows_ref[...] = fold(mxu(both_parts(rows_of(core_ref)[...], 1), right, NN), 1)
    left_rows = rows_of(left_ref)

    @pl.when(pl.program_id(0) == 0)
    def _():
        part_ref[...] = jnp.zeros_like(part_ref)

    sides, lefts = [], []
    for n in range(block):
        rows = rows_ref[pl.ds(n, local_rows, stride=block), :]
        sketched_ref[n] = rows
        sides.append(rows)
        lefts.append(left_rows[pl.ds(n, columns, stride=block), :])
    side = both_parts(jnp.concatenate(sides, axis=1), 1)
    left = twice(both_parts(jnp.concatenate(lefts, axis=1), 0), 1)
    part_ref[...] += fold(mxu(side, left, NT), 1)


def sketch(core_two, right_sketch, sketch_core):
    local_rows, slices, width = core_two.shape
    columns = right_sketch.shape[1]
    return call(
        sketch_kernel,
        2 * core_two.size * columns * 4,
        4 * (core_two.size + 2 * sketch_core.size),
        grid=(slices // BLOCK,),
        in_specs=[
            pl.BlockSpec((local_rows, BLOCK, width), lambda i: (0, i, 0)),
            pl.BlockSpec((width, columns), lambda i: (0, 0)),
            pl.BlockSpec((columns, BLOCK, columns), lambda i: (0, i, 0)),
        ],
        out_specs=[
            pl.BlockSpec((BLOCK, local_rows, columns), lambda i: (i, 0, 0)),
            pl.BlockSpec((local_rows, columns), lambda i: (0, 0)),
        ],
        out_shape=[shape(slices, local_rows, columns), shape(local_rows, columns)],
        scratch_shapes=[pltpu.VMEM((local_rows * BLOCK, columns), jnp.float32)],
    )(core_two, right_sketch, sketch_core)


def block_of(rows):
    block = 1024
    while rows % block:
        block //= 2
    return block


def square_kernel(core_ref, core_index_ref, keep_ref, give_ref, sum_ref):
    step = pl.program_id(0)
    width = core_ref.shape[1]
    high, low = split(core_ref[...])

    @pl.when(step == 0)
    def _():
        sum_ref[...] = jnp.zeros_like(sum_ref)

    sum_ref[...] += mxu(high, jnp.concatenate([high, low], axis=1), TN)

    @pl.when(step == pl.num_programs(0) - 1)
    def _():
        cross = sum_ref[:, width:]
        sum_ref[:, :width] = sum_ref[:, :width] + cross + cross.T
        half = width // 2
        own = core_index_ref[0]
        keep_ref[...] = sum_ref[pl.ds(pl.multiple_of(own * half, half), half), :width]
        give_ref[...] = sum_ref[pl.ds(pl.multiple_of((1 - own) * half, half), half), :width]


def square_of(flat_one, core_index):
    rows, width = flat_one.shape
    block = block_of(rows)
    half = pl.BlockSpec((width // 2, width), lambda i: (0, 0))
    return call(
        square_kernel,
        4 * rows * width * width,
        4 * flat_one.size,
        grid=(rows // block,),
        in_specs=[
            pl.BlockSpec((block, width), lambda i: (i, 0)),
            pl.BlockSpec(memory_space=pltpu.SMEM),
        ],
        out_specs=[half, half],
        out_shape=[shape(width // 2, width)] * 2,
        scratch_shapes=[pltpu.VMEM((width, 2 * width), jnp.float32)],
    )(flat_one, core_index)


def loose_kernel(halves, rank_ref, raw_ref, *refs):
    piece_refs, out_refs = refs[:-len(halves)], refs[-len(halves):]
    ranks = len(piece_refs) // len(halves)
    local_rows = piece_refs[0].shape[1]
    rows = []
    for offset in range(ranks):
        start = pl.multiple_of((rank_ref[0] ^ offset) * local_rows, local_rows)
        rows.append(raw_ref[pl.ds(start, local_rows), :])
    raw = twice(both_parts(jnp.concatenate(rows, axis=0), 1).T, 1)
    columns = raw_ref.shape[1]
    for half, count in enumerate(halves):
        refs = piece_refs[half * ranks:(half + 1) * ranks]
        value = [jnp.concatenate([ref[n] for n in range(count)], axis=1) for ref in refs]
        product = fold(mxu(raw, both_parts(jnp.concatenate(value, axis=0), 0), NN), 0)
        for n in range(count):
            out_refs[half][n] = product[:, n * columns:(n + 1) * columns]


def loosen(rank_index, raw, pieces, halves):
    columns = raw.shape[1]
    size = sum(piece.size for piece in pieces)
    whole = pl.BlockSpec(memory_space=pltpu.VMEM)
    return call(
        functools.partial(loose_kernel, halves),
        8 * size * columns,
        4 * raw.size + 4 * size,
        in_specs=[pl.BlockSpec(memory_space=pltpu.SMEM)] + [whole] * (len(pieces) + 1),
        out_specs=[whole] * len(halves),
        out_shape=[shape(count, columns, columns) for count in halves],
    )(rank_index, raw, *pieces)


def carry_kernel(halves, share, rank_ref, weight_ref, core_ref, *refs):
    piece_refs = refs[:-4]
    joined_ref, middle_ref, rows_ref, sum_ref = refs[-4:]
    step = pl.program_id(0)
    block, width = core_ref.shape
    columns = weight_ref.shape[1]
    ranks = len(piece_refs) // len(halves)
    room = share * ranks
    local_rows = rows_ref.shape[0] // room
    band = middle_ref.shape[0] // room

    @pl.when(step == 0)
    def _():
        sum_ref[...] = jnp.zeros_like(sum_ref)
        weight = twice(both_parts(weight_ref[...], 0), 1)
        for half, count in enumerate(halves):
            for offset in range(ranks):
                ref = piece_refs[half * ranks + offset]
                first = (rank_ref[0] ^ offset) * share + sum(halves[:half])
                value = both_parts(jnp.concatenate([ref[n] for n in range(count)], axis=1), 0)
                spread = fold(mxu(weight, value, NN), 0)
                for n in range(count):
                    piece = lax.slice_in_dim(spread, n * columns, (n + 1) * columns, axis=1)
                    rows_ref[pl.ds(first + n, local_rows, stride=room), :] = piece[:local_rows]
                    middle_ref[pl.ds(first + n, band, stride=room), :] = piece[local_rows:]

    rows = both_parts(rows_ref[pl.ds(pl.multiple_of(step * block, block), block), :], 1).T
    product = fold(mxu(twice(rows, 1), both_parts(core_ref[...], 0), NN), 0)
    sum_ref[...] += product

    @pl.when(step == pl.num_programs(0) - 1)
    def _():
        joined_ref[:width, :] = sum_ref[...].T
        middle = both_parts(middle_ref[...], 1)
        joined_ref[width:width + columns, :] = fold(fold(mxu(middle, middle, TN), 0), 1)
        joined_ref[width + columns:, :] = jnp.zeros_like(joined_ref[width + columns:, :])


def carry_rows(rank_index, weight, flat_two, pieces, halves, share, band, total):
    rows, width = flat_two.shape
    columns = weight.shape[1]
    block = block_of(rows)
    ranks = len(pieces) // len(halves)
    whole = pl.BlockSpec(memory_space=pltpu.VMEM)
    return call(
        functools.partial(carry_kernel, halves, share),
        8 * flat_two.size * columns,
        4 * flat_two.size + 4 * sum(piece.size for piece in pieces),
        grid=(rows // block,),
        in_specs=[
            pl.BlockSpec(memory_space=pltpu.SMEM),
            pl.BlockSpec((weight.shape[0], columns), lambda i: (0, 0)),
            pl.BlockSpec((block, width), lambda i: (i, 0)),
        ]
        + [pl.BlockSpec(piece.shape, lambda i: (0, 0, 0)) for piece in pieces],
        out_specs=[
            pl.BlockSpec((total, columns), lambda i: (0, 0)),
            pl.BlockSpec((band * share * ranks, columns), lambda i: (0, 0)),
        ],
        out_shape=[shape(total, columns), shape(band * share * ranks, columns)],
        scratch_shapes=[pltpu.VMEM((rows, columns), jnp.float32), pltpu.VMEM((columns, width), jnp.float32)],
    )(rank_index, weight, flat_two, *pieces)


def apply_kernel(rows_ref, weight_ref, out_ref):
    weight = twice(both_parts(weight_ref[...], 1), 0)
    out_ref[...] = fold(mxu(both_parts(rows_ref[...], 1), weight, NN), 1)


def apply_to(rows, weight):
    count, width = rows.shape
    columns = weight.shape[1]
    block = block_of(count)
    return call(
        apply_kernel,
        8 * rows.size * columns,
        4 * (rows.size + count * columns),
        grid=(count // block,),
        in_specs=[
            pl.BlockSpec((block, width), lambda i: (i, 0)),
            pl.BlockSpec((width, columns), lambda i: (0, 0)),
        ],
        out_specs=pl.BlockSpec((block, columns), lambda i: (i, 0)),
        out_shape=shape(count, columns),
    )(rows, weight)


def small_inverse(entry):
    size = len(entry)
    entry = [list(row) for row in entry]
    inverse = [[None] * size for _ in range(size)]
    for k in range(size):
        pivot = entry[k][k]
        root = lax.rsqrt(pivot)
        root = root * (1.5 - 0.5 * pivot * root * root)
        inverse[k][k] = root
        for i in range(k + 1, size):
            entry[i][k] = entry[i][k] * root
        for i in range(k + 1, size):
            for m in range(k + 1, i + 1):
                entry[i][m] = entry[i][m] - entry[i][k] * entry[m][k]
    for k in range(size):
        for i in range(k + 1, size):
            total = entry[i][k] * inverse[k][k]
            for m in range(k + 1, i):
                total = total + entry[i][m] * inverse[m][k]
            inverse[i][k] = -total * inverse[i][i]
    return inverse


def factor(gram, inverse_ref):
    size, tile = gram.shape[0], BLOCK
    count = size // tile
    left = [gram[i * tile:(i + 1) * tile, :] for i in range(count)]
    lane = lax.broadcasted_iota(jnp.int32, (tile, size), 1)
    sublane = lax.broadcasted_iota(jnp.int32, (tile, size), 0)
    right = [jnp.where(lane == sublane + i * tile, 1.0, 0.0) for i in range(count)]

    def spread(value, row, column):
        return jnp.broadcast_to(value[row:row + 1, column:column + 1], (tile, size))

    for j in range(count):
        corner = [[spread(left[j], i, j * tile + k) for k in range(i + 1)] for i in range(tile)]
        small = small_inverse(corner)
        columns = []
        for k in range(tile):
            column = jnp.where(sublane == k, small[k][k], 0.0)
            for i in range(k + 1, tile):
                column = jnp.where(sublane == i, small[i][k], column)
            columns.append(column)
        done_left = sum(columns[k] * left[j][k:k + 1, :] for k in range(tile))
        done_right = sum(columns[k] * right[j][k:k + 1, :] for k in range(tile))
        inverse_ref[pl.ds(j * tile, tile), :] = done_right
        if j + 1 < count:
            turned = done_left.T
            for i in range(j + 1, count):
                for k in range(tile):
                    factor = jnp.broadcast_to(turned[i * tile:(i + 1) * tile, k:k + 1], (tile, size))
                    left[i] = left[i] - factor * done_left[k:k + 1, :]
                    right[i] = right[i] - factor * done_right[k:k + 1, :]


def first_kernel(scale, band, rank_ref, bridge_ref, raw_ref, weight_ref, solve_ref, inverse_ref):
    local_rows = weight_ref.shape[0] - band
    factor(exact(bridge_ref[...], raw_ref[...], TN), inverse_ref)
    inverse = inverse_ref[...]
    start = pl.multiple_of(rank_ref[0] * local_rows, local_rows)
    own = exact(raw_ref[pl.ds(start, local_rows), :], inverse, NT)
    weight_ref[:local_rows, :] = exact(own, inverse, NN)
    weight_ref[local_rows:, :] = inverse_ref[pl.ds(pl.multiple_of(rank_ref[0] * band, band), band), :]
    solve_ref[...] = scale * exact(bridge_ref[...], inverse, NT)


def first_factor(rank_index, bridge, raw, scale, local_rows, band):
    columns = raw.shape[1]
    whole = pl.BlockSpec(memory_space=pltpu.VMEM)
    return call(
        functools.partial(first_kernel, scale, band),
        8 * raw.size * columns,
        16 * raw.size,
        in_specs=[pl.BlockSpec(memory_space=pltpu.SMEM), whole, whole],
        out_specs=[whole, whole],
        out_shape=[shape(local_rows + band, columns), shape(*raw.shape)],
        scratch_shapes=[pltpu.VMEM((columns, columns), jnp.float32)],
    )(rank_index, bridge, raw)


def last_kernel(scale, joined_ref, middle_ref, carry_ref, out_ref, inverse_ref):
    columns = inverse_ref.shape[0]
    width = carry_ref.shape[1]
    factor(joined_ref[pl.ds(width, columns), :], inverse_ref)
    inverse = inverse_ref[...]
    carry_ref[...] = exact(inverse, joined_ref[pl.ds(0, width), :], NT)
    out_ref[...] = exact(middle_ref[...], scale * inverse, NT)


def last_factor(joined, middle, scale, width):
    columns = joined.shape[1]
    whole = pl.BlockSpec(memory_space=pltpu.VMEM)
    return call(
        functools.partial(last_kernel, scale),
        8 * middle.size * columns,
        8 * middle.size,
        in_specs=[whole, whole],
        out_specs=[whole, whole],
        out_shape=[shape(columns, width), shape(*middle.shape)],
        scratch_shapes=[pltpu.VMEM((columns, columns), jnp.float32)],
    )(joined, middle)


def swap(value, axis, offset):
    return lax.ppermute(value, axis, [(i, i ^ offset) for i in range(lax.axis_size(axis))])


def exchange(value, axes, groups=None):
    return lax.all_to_all(value, axes, 0, 0, axis_index_groups=groups, tiled=True)


def gather_all(value, axes):
    parts = lax.axis_size(axes)
    return exchange(jnp.broadcast_to(value[None], (parts,) + value.shape), axes)


def after(value, others):
    return lax.optimization_barrier((value, others))


def on_device(core_one, core_two, right_sketch, sketch_core):
    local_rows, slices, width = core_one.shape
    columns = right_sketch.shape[1]
    ranks, cuts = lax.axis_size("rank"), lax.axis_size("cuts")
    rank, cut = lax.axis_index("rank"), lax.axis_index("cuts")
    rank_index = rank.astype(jnp.int32).reshape(1)
    core_index = lax.rem(cut, 2).astype(jnp.int32).reshape(1)
    both = ("cuts", "rank")
    parts = ranks * cuts
    band = columns // ranks
    share = -(-slices // ranks)
    room = share * ranks
    halves = [share // 2, share - share // 2]
    core_groups = [
        [z * ranks + place for z in range(core, cuts, 2) for place in range(ranks)] for core in range(2)
    ]
    filler = ((0, 0), (0, room - slices), (0, 0))
    core_two, sketch_core = jnp.pad(core_two, filler), jnp.pad(sketch_core, filler)
    flat_one = core_one.reshape(local_rows * slices, width)
    flat_two = core_two.reshape(local_rows * room, width)

    sketched, part = sketch(core_two, right_sketch, sketch_core)

    def send(names, source, behind):
        found = []
        for half, offset in names:
            start = (rank ^ offset) * share + half * halves[0]
            found.append(lax.dynamic_slice_in_dim(source, start, halves[half], 0))
        if behind is not None:
            found, _ = after(found, behind)
        return {name: swap(value, "rank", name[1]) if name[1] else value for name, value in zip(names, found)}

    far = ranks - 1
    near = [[(half, offset) for offset in range(1, far)] for half in range(2)]

    moved = send(near[0], sketched, None)
    bridge_rows = jnp.sum(exchange(part.reshape(cuts, local_rows // cuts, columns), "cuts"), axis=0)
    flat_late, part = after(flat_one, part)
    keep, give = square_of(flat_late, core_index)
    bridge_rows, pieces = after(bridge_rows, moved)
    sketched, bridge_rows = after(sketched, bridge_rows)
    pieces.update(send([(0, 0), (1, 0)], sketched, None))

    bridge = gather_all(bridge_rows, both)
    bridge = bridge.reshape(cuts, ranks, -1, columns).swapaxes(0, 1).reshape(width, columns)
    square = keep + swap(give, "cuts", 1)
    moved = send(near[1] + [(0, far)], sketched, square)
    square = exchange(square.reshape(parts // 2, -1, width), both, core_groups)
    raw_rows = exact(jnp.sum(square, axis=0), bridge, NN)
    raw_rows, moved = after(raw_rows, moved)
    pieces.update(moved)

    pieces.update(send([(1, far)], sketched, raw_rows))
    raw = gather_all(raw_rows, both).reshape(cuts // 2, 2, ranks, -1, columns)
    raw = raw.transpose(1, 0, 2, 3, 4).reshape(width, columns)

    ordered = [pieces[(half, offset)] for half in range(2) for offset in range(ranks)]
    loose = loosen(rank_index, raw, ordered, halves)
    loose, (bridge, raw) = after(loose, (bridge, raw))

    bits = [1 << bit for bit in range((ranks - 1).bit_length())]
    everyone = []
    for value, order in zip(loose, (bits, bits[::-1])):
        found = {0: value}
        for bit in order:
            found.update({offset ^ bit: swap(held, "rank", bit) for offset, held in list(found.items())})
        everyone += [found[offset] for offset in range(ranks)]

    scale = math.sqrt(local_rows * ranks * slices * cuts)
    weight, solve = first_factor(rank_index, bridge, raw, scale, local_rows, band)
    total = -(-(width + columns) // (BLOCK * parts)) * BLOCK * parts
    joined, middle = carry_rows(rank_index, weight, flat_two, everyone, halves, share, band, total)
    joined = jnp.sum(exchange(joined.reshape(parts, -1, columns), both), axis=0)
    joined = gather_all(joined, both).reshape(total, columns)
    left_core = apply_to(flat_one, solve).reshape(local_rows, slices, columns)
    scale = math.sqrt(columns * slices * cuts)
    carry, middle = last_factor(joined, middle, scale, width)
    middle_core = middle.reshape(band, room, columns)[:, :slices]
    return (left_core, middle_core, carry)


def solution(mesh):
    placed = (P("rank", "cuts", None), P("rank", "cuts", None), P(), P(None, "cuts", None))
    return jax.shard_map(
        on_device,
        mesh=mesh,
        in_specs=placed,
        out_specs=(P("rank", "cuts", None), P("rank", "cuts", None), P()),
        check_vma=False,
    )
```

```python
import functools
import math

import jax
import jax.numpy as jnp
from jax import lax
from jax.experimental import pallas as pl
from jax.experimental.pallas import tpu as pltpu
from jax.sharding import PartitionSpec as P

NT = (((1,), (1,)), ((), ()))
NN = (((1,), (0,)), ((), ()))
TN = (((0,), (0,)), ((), ()))
VMEM_LIMIT = 56 * 1024 * 1024
BLOCK = 8


PARTS = 4


def tiles(block, width):
    size = block // PARTS
    return [pl.BlockSpec((size, width), lambda i, q=q: (i * PARTS + q, 0)) for q in range(PARTS)]


def joined_rows(refs):
    return jnp.concatenate([ref[...] for ref in refs], axis=0)


def call(kernel, flops, size, **more):
    return pl.pallas_call(
        kernel,
        compiler_params=pltpu.CompilerParams(vmem_limit_bytes=VMEM_LIMIT),
        cost_estimate=pl.CostEstimate(flops=flops, bytes_accessed=size, transcendentals=0),
        **more,
    )


def shape(*extent):
    return jax.ShapeDtypeStruct(extent, jnp.float32)


def split(value):
    high = value.astype(jnp.bfloat16)
    return high, (value - high.astype(jnp.float32)).astype(jnp.bfloat16)


def mxu(a, b, form):
    return lax.dot_general(a, b, form, preferred_element_type=jnp.float32)


def exact(a, b, form):
    return lax.dot_general(a, b, form, precision=lax.Precision.HIGHEST, preferred_element_type=jnp.float32)


def both_parts(value, axis):
    return jnp.concatenate(split(value), axis=axis)


def twice(value, axis):
    return jnp.concatenate([value, value], axis=axis)


def fold(value, axis):
    half = value.shape[axis] // 2
    return lax.slice_in_dim(value, 0, half, axis=axis) + lax.slice_in_dim(value, half, 2 * half, axis=axis)


def rows_of(ref):
    return ref.reshape(ref.shape[0] * ref.shape[1], ref.shape[2])


def sketch_kernel(*refs):
    core_refs, (right_ref, left_ref, sketched_ref, part_ref, rows_ref) = refs[:PARTS], refs[PARTS:]
    block = left_ref.shape[1]
    local_rows = rows_ref.shape[0] // block
    columns = right_ref.shape[1]
    right = twice(both_parts(right_ref[...], 1), 0)
    rows_ref[...] = fold(mxu(both_parts(jnp.concatenate([rows_of(ref)[...] for ref in core_refs], axis=0), 1), right, NN), 1)
    left_rows = rows_of(left_ref)

    @pl.when(pl.program_id(0) == 0)
    def _():
        part_ref[...] = jnp.zeros_like(part_ref)

    sides, lefts = [], []
    for n in range(block):
        rows = rows_ref[pl.ds(n, local_rows, stride=block), :]
        sketched_ref[n] = rows
        sides.append(rows)
        lefts.append(left_rows[pl.ds(n, columns, stride=block), :])
    side = both_parts(jnp.concatenate(sides, axis=1), 1)
    left = twice(both_parts(jnp.concatenate(lefts, axis=1), 0), 1)
    part_ref[...] += fold(mxu(side, left, NT), 1)


def sketch(core_two, right_sketch, sketch_core):
    local_rows, slices, width = core_two.shape
    columns = right_sketch.shape[1]
    return call(
        sketch_kernel,
        2 * core_two.size * columns * 4,
        4 * (core_two.size + 2 * sketch_core.size),
        grid=(slices // BLOCK,),
        in_specs=[
            *[pl.BlockSpec((local_rows // PARTS, BLOCK, width), lambda i, q=q: (q, i, 0)) for q in range(PARTS)],
            pl.BlockSpec((width, columns), lambda i: (0, 0)),
            pl.BlockSpec((columns, BLOCK, columns), lambda i: (0, i, 0)),
        ],
        out_specs=[
            pl.BlockSpec((BLOCK, local_rows, columns), lambda i: (i, 0, 0)),
            pl.BlockSpec((local_rows, columns), lambda i: (0, 0)),
        ],
        out_shape=[shape(slices, local_rows, columns), shape(local_rows, columns)],
        scratch_shapes=[pltpu.VMEM((local_rows * BLOCK, columns), jnp.float32)],
    )(*[core_two] * PARTS, right_sketch, sketch_core)


def block_of(rows):
    block = 1024
    while rows % block:
        block //= 2
    return block


def rows_kernel(*refs):
    core_refs, (bridge_ref, raw_ref, rows_ref, sum_ref) = refs[:PARTS], refs[PARTS:]
    step = pl.program_id(0)

    @pl.when(step == 0)
    def _():
        sum_ref[...] = jnp.zeros_like(sum_ref)

    high, low = split(joined_rows(core_refs))
    bridge = twice(both_parts(bridge_ref[...], 1), 0)
    rows = fold(mxu(jnp.concatenate([high, low], axis=1), bridge, NN), 1)
    rows_ref[...] = rows
    turned = twice(both_parts(rows, 1).T, 1)
    product = fold(mxu(turned, jnp.concatenate([high, low], axis=0), NN), 0)
    sum_ref[...] += product

    @pl.when(step == pl.num_programs(0) - 1)
    def _():
        raw_ref[...] = sum_ref[...].T


def first_rows_of(flat_one, bridge):
    rows, width = flat_one.shape
    columns = bridge.shape[1]
    block = block_of(rows)
    return call(
        rows_kernel,
        16 * flat_one.size * columns,
        4 * flat_one.size,
        grid=(rows // block,),
        in_specs=[
            *tiles(block, width),
            pl.BlockSpec((width, columns), lambda i: (0, 0)),
        ],
        out_specs=[
            pl.BlockSpec((width, columns), lambda i: (0, 0)),
            pl.BlockSpec((block, columns), lambda i: (i, 0)),
        ],
        out_shape=[shape(width, columns), shape(rows, columns)],
        scratch_shapes=[pltpu.VMEM((columns, width), jnp.float32)],
    )(*[flat_one] * PARTS, bridge)


def loose_kernel(halves, rank_ref, raw_ref, *refs):
    piece_refs, out_refs = refs[:-len(halves)], refs[-len(halves):]
    ranks = len(piece_refs) // len(halves)
    local_rows = piece_refs[0].shape[1]
    rows = []
    for offset in range(ranks):
        start = pl.multiple_of((rank_ref[0] ^ offset) * local_rows, local_rows)
        rows.append(raw_ref[pl.ds(start, local_rows), :])
    raw = twice(both_parts(jnp.concatenate(rows, axis=0), 1).T, 1)
    columns = raw_ref.shape[1]
    for half, count in enumerate(halves):
        refs = piece_refs[half * ranks:(half + 1) * ranks]
        value = [jnp.concatenate([ref[n] for n in range(count)], axis=1) for ref in refs]
        product = fold(mxu(raw, both_parts(jnp.concatenate(value, axis=0), 0), NN), 0)
        for n in range(count):
            out_refs[half][n] = product[:, n * columns:(n + 1) * columns]


def loosen(rank_index, raw, pieces, halves):
    columns = raw.shape[1]
    size = sum(piece.size for piece in pieces)
    whole = pl.BlockSpec(memory_space=pltpu.VMEM)
    return call(
        functools.partial(loose_kernel, halves),
        8 * size * columns,
        4 * raw.size + 4 * size,
        in_specs=[pl.BlockSpec(memory_space=pltpu.SMEM)] + [whole] * (len(pieces) + 1),
        out_specs=[whole] * len(halves),
        out_shape=[shape(count, columns, columns) for count in halves],
    )(rank_index, raw, *pieces)


def carry_kernel(halves, share, rank_ref, weight_ref, *refs):
    core_refs, piece_refs = refs[:PARTS], refs[PARTS:-4]
    joined_ref, middle_ref, rows_ref, sum_ref = refs[-4:]
    step = pl.program_id(0)
    block, width = core_refs[0].shape[0] * PARTS, core_refs[0].shape[1]
    columns = weight_ref.shape[1]
    ranks = len(piece_refs) // len(halves)
    room = share * ranks
    local_rows = rows_ref.shape[0] // room
    band = middle_ref.shape[0] // room

    @pl.when(step == 0)
    def _():
        sum_ref[...] = jnp.zeros_like(sum_ref)
        weight = twice(both_parts(weight_ref[...], 0), 1)
        for half, count in enumerate(halves):
            for offset in range(ranks):
                ref = piece_refs[half * ranks + offset]
                first = (rank_ref[0] ^ offset) * share + sum(halves[:half])
                value = both_parts(jnp.concatenate([ref[n] for n in range(count)], axis=1), 0)
                spread = fold(mxu(weight, value, NN), 0)
                for n in range(count):
                    piece = lax.slice_in_dim(spread, n * columns, (n + 1) * columns, axis=1)
                    rows_ref[pl.ds(first + n, local_rows, stride=room), :] = piece[:local_rows]
                    middle_ref[pl.ds(first + n, band, stride=room), :] = piece[local_rows:]

    rows = both_parts(rows_ref[pl.ds(pl.multiple_of(step * block, block), block), :], 1).T
    product = fold(mxu(twice(rows, 1), both_parts(joined_rows(core_refs), 0), NN), 0)
    sum_ref[...] += product

    @pl.when(step == pl.num_programs(0) - 1)
    def _():
        joined_ref[:width, :] = sum_ref[...].T
        middle = both_parts(middle_ref[...], 1)
        joined_ref[width:width + columns, :] = fold(fold(mxu(middle, middle, TN), 0), 1)
        joined_ref[width + columns:, :] = jnp.zeros_like(joined_ref[width + columns:, :])


def carry_rows(rank_index, weight, flat_two, pieces, halves, share, band, total):
    rows, width = flat_two.shape
    columns = weight.shape[1]
    block = block_of(rows)
    ranks = len(pieces) // len(halves)
    whole = pl.BlockSpec(memory_space=pltpu.VMEM)
    return call(
        functools.partial(carry_kernel, halves, share),
        8 * flat_two.size * columns,
        4 * flat_two.size + 4 * sum(piece.size for piece in pieces),
        grid=(rows // block,),
        in_specs=[
            pl.BlockSpec(memory_space=pltpu.SMEM),
            pl.BlockSpec((weight.shape[0], columns), lambda i: (0, 0)),
            *tiles(block, width),
        ]
        + [pl.BlockSpec(piece.shape, lambda i: (0, 0, 0)) for piece in pieces],
        out_specs=[
            pl.BlockSpec((total, columns), lambda i: (0, 0)),
            pl.BlockSpec((band * share * ranks, columns), lambda i: (0, 0)),
        ],
        out_shape=[shape(total, columns), shape(band * share * ranks, columns)],
        scratch_shapes=[pltpu.VMEM((rows, columns), jnp.float32), pltpu.VMEM((columns, width), jnp.float32)],
    )(rank_index, weight, *[flat_two] * PARTS, *pieces)


def apply_kernel(rows_ref, weight_ref, out_ref):
    weight = twice(both_parts(weight_ref[...], 0), 1)
    out_ref[...] = fold(mxu(both_parts(rows_ref[...], 1), weight, NT), 1)


def apply_to(rows, weight):
    count, columns = rows.shape
    block = block_of(count)
    tile = pl.BlockSpec((block, columns), lambda i: (i, 0))
    return call(
        apply_kernel,
        8 * rows.size * columns,
        8 * rows.size,
        grid=(count // block,),
        in_specs=[tile, pl.BlockSpec((columns, columns), lambda i: (0, 0))],
        out_specs=pl.BlockSpec((block, columns), lambda i: (i, 0)),
        out_shape=shape(count, columns),
    )(rows, weight)


def small_inverse(entry):
    size = len(entry)
    entry = [list(row) for row in entry]
    inverse = [[None] * size for _ in range(size)]
    for k in range(size):
        pivot = entry[k][k]
        root = lax.rsqrt(pivot)
        root = root * (1.5 - 0.5 * pivot * root * root)
        inverse[k][k] = root
        for i in range(k + 1, size):
            entry[i][k] = entry[i][k] * root
        for i in range(k + 1, size):
            for m in range(k + 1, i + 1):
                entry[i][m] = entry[i][m] - entry[i][k] * entry[m][k]
    for k in range(size):
        for i in range(k + 1, size):
            total = entry[i][k] * inverse[k][k]
            for m in range(k + 1, i):
                total = total + entry[i][m] * inverse[m][k]
            inverse[i][k] = -total * inverse[i][i]
    return inverse


def factor(gram, inverse_ref):
    size, tile = gram.shape[0], BLOCK
    count = size // tile
    left = [gram[i * tile:(i + 1) * tile, :] for i in range(count)]
    lane = lax.broadcasted_iota(jnp.int32, (tile, size), 1)
    sublane = lax.broadcasted_iota(jnp.int32, (tile, size), 0)
    right = [jnp.where(lane == sublane + i * tile, 1.0, 0.0) for i in range(count)]

    def spread(value, row, column):
        return jnp.broadcast_to(value[row:row + 1, column:column + 1], (tile, size))

    for j in range(count):
        corner = [[spread(left[j], i, j * tile + k) for k in range(i + 1)] for i in range(tile)]
        small = small_inverse(corner)
        columns = []
        for k in range(tile):
            column = jnp.where(sublane == k, small[k][k], 0.0)
            for i in range(k + 1, tile):
                column = jnp.where(sublane == i, small[i][k], column)
            columns.append(column)
        done_left = sum(columns[k] * left[j][k:k + 1, :] for k in range(tile))
        done_right = sum(columns[k] * right[j][k:k + 1, :] for k in range(tile))
        inverse_ref[pl.ds(j * tile, tile), :] = done_right
        if j + 1 < count:
            turned = done_left.T
            for i in range(j + 1, count):
                for k in range(tile):
                    factor = jnp.broadcast_to(turned[i * tile:(i + 1) * tile, k:k + 1], (tile, size))
                    left[i] = left[i] - factor * done_left[k:k + 1, :]
                    right[i] = right[i] - factor * done_right[k:k + 1, :]


def first_kernel(scale, band, rank_ref, bridge_ref, raw_ref, weight_ref, solve_ref, inverse_ref):
    local_rows = weight_ref.shape[0] - band
    factor(exact(bridge_ref[...], raw_ref[...], TN), inverse_ref)
    inverse = inverse_ref[...]
    start = pl.multiple_of(rank_ref[0] * local_rows, local_rows)
    own = exact(raw_ref[pl.ds(start, local_rows), :], inverse, NT)
    weight_ref[:local_rows, :] = exact(own, inverse, NN)
    weight_ref[local_rows:, :] = inverse_ref[pl.ds(pl.multiple_of(rank_ref[0] * band, band), band), :]
    solve_ref[...] = scale * inverse


def first_factor(rank_index, bridge, raw, scale, local_rows, band):
    columns = raw.shape[1]
    whole = pl.BlockSpec(memory_space=pltpu.VMEM)
    return call(
        functools.partial(first_kernel, scale, band),
        8 * raw.size * columns,
        16 * raw.size,
        in_specs=[pl.BlockSpec(memory_space=pltpu.SMEM), whole, whole],
        out_specs=[whole, whole],
        out_shape=[shape(local_rows + band, columns), shape(columns, columns)],
        scratch_shapes=[pltpu.VMEM((columns, columns), jnp.float32)],
    )(rank_index, bridge, raw)


def last_kernel(scale, joined_ref, middle_ref, carry_ref, out_ref, inverse_ref):
    columns = inverse_ref.shape[0]
    width = carry_ref.shape[1]
    factor(joined_ref[pl.ds(width, columns), :], inverse_ref)
    inverse = inverse_ref[...]
    carry_ref[...] = exact(inverse, joined_ref[pl.ds(0, width), :], NT)
    out_ref[...] = exact(middle_ref[...], scale * inverse, NT)


def last_factor(joined, middle, scale, width):
    columns = joined.shape[1]
    whole = pl.BlockSpec(memory_space=pltpu.VMEM)
    return call(
        functools.partial(last_kernel, scale),
        8 * middle.size * columns,
        8 * middle.size,
        in_specs=[whole, whole],
        out_specs=[whole, whole],
        out_shape=[shape(columns, width), shape(*middle.shape)],
        scratch_shapes=[pltpu.VMEM((columns, columns), jnp.float32)],
    )(joined, middle)


def swap(value, axis, offset):
    return lax.ppermute(value, axis, [(i, i ^ offset) for i in range(lax.axis_size(axis))])


def exchange(value, axes):
    return lax.all_to_all(value, axes, 0, 0, tiled=True)


def gather_all(value, axes):
    parts = lax.axis_size(axes)
    return exchange(jnp.broadcast_to(value[None], (parts,) + value.shape), axes)


def after(value, others):
    return lax.optimization_barrier((value, others))


def on_device(core_one, core_two, right_sketch, sketch_core):
    local_rows, slices, width = core_one.shape
    columns = right_sketch.shape[1]
    ranks, cuts = lax.axis_size("rank"), lax.axis_size("cuts")
    rank = lax.axis_index("rank")
    rank_index = rank.astype(jnp.int32).reshape(1)
    both = ("cuts", "rank")
    parts = ranks * cuts
    band = columns // ranks
    share = -(-slices // ranks)
    room = share * ranks
    halves = [share // 2, share - share // 2]
    filler = ((0, 0), (0, room - slices), (0, 0))
    core_two, sketch_core = jnp.pad(core_two, filler), jnp.pad(sketch_core, filler)
    flat_one = core_one.reshape(local_rows * slices, width)
    flat_two = core_two.reshape(local_rows * room, width)

    sketched, part = sketch(core_two, right_sketch, sketch_core)

    def send(names, source, behind):
        found = []
        for half, offset in names:
            start = (rank ^ offset) * share + half * halves[0]
            found.append(lax.dynamic_slice_in_dim(source, start, halves[half], 0))
        if behind is not None:
            found, _ = after(found, behind)
        return {name: swap(value, "rank", name[1]) if name[1] else value for name, value in zip(names, found)}

    far = ranks - 1
    near = [[(half, offset) for offset in range(1, far)] for half in range(2)]

    cut_bits = [1 << bit for bit in range((cuts - 1).bit_length())]
    bits = [1 << bit for bit in range((ranks - 1).bit_length())]
    for bit in cut_bits:
        part = part + swap(part, "cuts", bit)
    bridge = {0: part}
    for bit in bits:
        bridge.update({offset ^ bit: swap(held, "rank", bit) for offset, held in list(bridge.items())})
    bridge = jnp.stack([bridge[offset] for offset in range(ranks)])
    bridge = bridge[rank ^ jnp.arange(ranks)].reshape(width, columns)
    sketched, bridge = after(sketched, bridge)
    pieces = send([(0, 0), (1, 0)] + near[0] + near[1], sketched, None)
    raw, first_rows = first_rows_of(flat_one, bridge)
    raw, moved = after(raw, pieces)
    pieces.update(moved)
    moved = send([(0, far)], sketched, raw)
    raw = jnp.sum(exchange(raw.reshape(parts, -1, columns), both), axis=0)
    raw, moved = after(raw, moved)
    pieces.update(moved)
    pieces.update(send([(1, far)], sketched, raw))
    raw = gather_all(raw, both).reshape(width, columns)

    ordered = [pieces[(half, offset)] for half in range(2) for offset in range(ranks)]
    loose = loosen(rank_index, raw, ordered, halves)
    loose, (bridge, raw) = after(loose, (bridge, raw))

    everyone = []
    for value, order in zip(loose, (bits, bits[::-1])):
        found = {0: value}
        for bit in order:
            found.update({offset ^ bit: swap(held, "rank", bit) for offset, held in list(found.items())})
        everyone += [found[offset] for offset in range(ranks)]

    scale = math.sqrt(local_rows * ranks * slices * cuts)
    weight, solve = first_factor(rank_index, bridge, raw, scale, local_rows, band)
    total = -(-(width + columns) // (BLOCK * parts)) * BLOCK * parts
    joined, middle = carry_rows(rank_index, weight, flat_two, everyone, halves, share, band, total)
    joined = jnp.sum(exchange(joined.reshape(parts, -1, columns), both), axis=0)
    joined = gather_all(joined, both).reshape(total, columns)
    left_core = apply_to(first_rows, solve).reshape(local_rows, slices, columns)
    scale = math.sqrt(columns * slices * cuts)
    carry, middle = last_factor(joined, middle, scale, width)
    middle_core = middle.reshape(band, room, columns)[:, :slices]
    return (left_core, middle_core, carry)


def solution(mesh):
    placed = (P("rank", "cuts", None), P("rank", "cuts", None), P(), P(None, "cuts", None))
    return jax.shard_map(
        on_device,
        mesh=mesh,
        in_specs=placed,
        out_specs=(P("rank", "cuts", None), P("rank", "cuts", None), P()),
        check_vma=False,
    )
```

```python
import functools
import math

import jax
import jax.numpy as jnp
from jax import lax
from jax.experimental import pallas as pl
from jax.experimental.pallas import tpu as pltpu
from jax.sharding import PartitionSpec as P

NT = (((1,), (1,)), ((), ()))
NN = (((1,), (0,)), ((), ()))
TN = (((0,), (0,)), ((), ()))
VMEM_LIMIT = 56 * 1024 * 1024
BLOCK = 8


PARTS = 4


def tiles(block, width):
    size = block // PARTS
    return [pl.BlockSpec((size, width), lambda i, q=q: (i * PARTS + q, 0)) for q in range(PARTS)]


def joined_rows(refs):
    return jnp.concatenate([ref[...] for ref in refs], axis=0)


def call(kernel, flops, size, **more):
    return pl.pallas_call(
        kernel,
        compiler_params=pltpu.CompilerParams(vmem_limit_bytes=VMEM_LIMIT),
        cost_estimate=pl.CostEstimate(flops=flops, bytes_accessed=size, transcendentals=0),
        **more,
    )


def shape(*extent):
    return jax.ShapeDtypeStruct(extent, jnp.float32)


def split(value):
    high = value.astype(jnp.bfloat16)
    return high, (value - high.astype(jnp.float32)).astype(jnp.bfloat16)


def mxu(a, b, form):
    return lax.dot_general(a, b, form, preferred_element_type=jnp.float32)


def exact(a, b, form):
    return lax.dot_general(a, b, form, precision=lax.Precision.HIGHEST, preferred_element_type=jnp.float32)


def both_parts(value, axis):
    return jnp.concatenate(split(value), axis=axis)


def twice(value, axis):
    return jnp.concatenate([value, value], axis=axis)


def fold(value, axis):
    half = value.shape[axis] // 2
    return lax.slice_in_dim(value, 0, half, axis=axis) + lax.slice_in_dim(value, half, 2 * half, axis=axis)


def rows_of(ref):
    return ref.reshape(ref.shape[0] * ref.shape[1], ref.shape[2])


def sketch_kernel(*refs):
    core_refs, (right_ref, left_ref, sketched_ref, part_ref, rows_ref) = refs[:PARTS], refs[PARTS:]
    block = left_ref.shape[1]
    local_rows = rows_ref.shape[0] // block
    columns = right_ref.shape[1]
    right = twice(both_parts(right_ref[...], 1), 0)
    rows_ref[...] = fold(mxu(both_parts(jnp.concatenate([rows_of(ref)[...] for ref in core_refs], axis=0), 1), right, NN), 1)
    left_rows = rows_of(left_ref)

    @pl.when(pl.program_id(0) == 0)
    def _():
        part_ref[...] = jnp.zeros_like(part_ref)

    sides, lefts = [], []
    for n in range(block):
        rows = rows_ref[pl.ds(n, local_rows, stride=block), :]
        sketched_ref[n] = rows
        sides.append(rows)
        lefts.append(left_rows[pl.ds(n, columns, stride=block), :])
    side = both_parts(jnp.concatenate(sides, axis=1), 1)
    left = twice(both_parts(jnp.concatenate(lefts, axis=1), 0), 1)
    part_ref[...] += fold(mxu(side, left, NT), 1)


def sketch(core_two, right_sketch, sketch_core):
    local_rows, slices, width = core_two.shape
    columns = right_sketch.shape[1]
    return call(
        sketch_kernel,
        2 * core_two.size * columns * 4,
        4 * (core_two.size + 2 * sketch_core.size),
        grid=(slices // BLOCK,),
        in_specs=[
            *[pl.BlockSpec((local_rows // PARTS, BLOCK, width), lambda i, q=q: (q, i, 0)) for q in range(PARTS)],
            pl.BlockSpec((width, columns), lambda i: (0, 0)),
            pl.BlockSpec((columns, BLOCK, columns), lambda i: (0, i, 0)),
        ],
        out_specs=[
            pl.BlockSpec((BLOCK, local_rows, columns), lambda i: (i, 0, 0)),
            pl.BlockSpec((local_rows, columns), lambda i: (0, 0)),
        ],
        out_shape=[shape(slices, local_rows, columns), shape(local_rows, columns)],
        scratch_shapes=[pltpu.VMEM((local_rows * BLOCK, columns), jnp.float32)],
    )(*[core_two] * PARTS, right_sketch, sketch_core)


def block_of(rows):
    block = 1024
    while rows % block:
        block //= 2
    return block


def square_kernel(core_ref, square_ref, sum_ref):
    step = pl.program_id(0)
    width = core_ref.shape[1]
    high, low = split(core_ref[...])

    @pl.when(step == 0)
    def _():
        sum_ref[...] = jnp.zeros_like(sum_ref)

    sum_ref[...] += mxu(high, jnp.concatenate([high, low], axis=1), TN)

    @pl.when(step == pl.num_programs(0) - 1)
    def _():
        cross = sum_ref[:, width:]
        square_ref[...] = sum_ref[:, :width] + cross + cross.T


def square_of(flat_one):
    rows, width = flat_one.shape
    block = block_of(rows)
    return call(
        square_kernel,
        4 * rows * width * width,
        4 * flat_one.size,
        grid=(rows // block,),
        in_specs=[pl.BlockSpec((block, width), lambda i: (i, 0))],
        out_specs=pl.BlockSpec((width, width), lambda i: (0, 0)),
        out_shape=shape(width, width),
        scratch_shapes=[pltpu.VMEM((width, 2 * width), jnp.float32)],
    )(flat_one)


def loose_kernel(rank_ref, raw_ref, *refs):
    piece_refs, out_ref = refs[:-1], refs[-1]
    count, local_rows, columns = piece_refs[0].shape
    rows = []
    for offset in range(len(piece_refs)):
        start = pl.multiple_of((rank_ref[0] ^ offset) * local_rows, local_rows)
        rows.append(raw_ref[pl.ds(start, local_rows), :])
    raw = twice(both_parts(jnp.concatenate(rows, axis=0), 1).T, 1)
    value = [jnp.concatenate([ref[n] for n in range(count)], axis=1) for ref in piece_refs]
    product = fold(mxu(raw, both_parts(jnp.concatenate(value, axis=0), 0), NN), 0)
    for n in range(count):
        out_ref[n] = product[:, n * columns:(n + 1) * columns]


def loosen(rank_index, raw, pieces):
    columns = raw.shape[1]
    size = len(pieces) * pieces[0].size
    whole = pl.BlockSpec(memory_space=pltpu.VMEM)
    return call(
        loose_kernel,
        8 * size * columns,
        4 * raw.size + 4 * size,
        in_specs=[pl.BlockSpec(memory_space=pltpu.SMEM)] + [whole] * (len(pieces) + 1),
        out_specs=whole,
        out_shape=shape(pieces[0].shape[0], columns, columns),
    )(rank_index, raw, *pieces)


def carry_kernel(halves, share, rank_ref, weight_ref, *refs):
    core_refs, piece_refs = refs[:PARTS], refs[PARTS:-4]
    joined_ref, middle_ref, rows_ref, sum_ref = refs[-4:]
    step = pl.program_id(0)
    block, width = core_refs[0].shape[0] * PARTS, core_refs[0].shape[1]
    columns = weight_ref.shape[1]
    ranks = len(piece_refs) // len(halves)
    room = share * ranks
    local_rows = rows_ref.shape[0] // room
    band = middle_ref.shape[0] // room

    @pl.when(step == 0)
    def _():
        sum_ref[...] = jnp.zeros_like(sum_ref)
        weight = twice(both_parts(weight_ref[...], 0), 1)
        for half, count in enumerate(halves):
            for offset in range(ranks):
                ref = piece_refs[half * ranks + offset]
                first = (rank_ref[0] ^ offset) * share + sum(halves[:half])
                value = both_parts(jnp.concatenate([ref[n] for n in range(count)], axis=1), 0)
                spread = fold(mxu(weight, value, NN), 0)
                for n in range(count):
                    piece = lax.slice_in_dim(spread, n * columns, (n + 1) * columns, axis=1)
                    rows_ref[pl.ds(first + n, local_rows, stride=room), :] = piece[:local_rows]
                    middle_ref[pl.ds(first + n, band, stride=room), :] = piece[local_rows:]

    rows = both_parts(rows_ref[pl.ds(pl.multiple_of(step * block, block), block), :], 1).T
    product = fold(mxu(twice(rows, 1), both_parts(joined_rows(core_refs), 0), NN), 0)
    sum_ref[...] += product

    @pl.when(step == pl.num_programs(0) - 1)
    def _():
        joined_ref[:width, :] = sum_ref[...].T
        middle = both_parts(middle_ref[...], 1)
        joined_ref[width:width + columns, :] = fold(fold(mxu(middle, middle, TN), 0), 1)
        joined_ref[width + columns:, :] = jnp.zeros_like(joined_ref[width + columns:, :])


def carry_rows(rank_index, weight, flat_two, pieces, halves, share, band, total):
    rows, width = flat_two.shape
    columns = weight.shape[1]
    block = block_of(rows)
    ranks = len(pieces) // len(halves)
    whole = pl.BlockSpec(memory_space=pltpu.VMEM)
    return call(
        functools.partial(carry_kernel, halves, share),
        8 * flat_two.size * columns,
        4 * flat_two.size + 4 * sum(piece.size for piece in pieces),
        grid=(rows // block,),
        in_specs=[
            pl.BlockSpec(memory_space=pltpu.SMEM),
            pl.BlockSpec((weight.shape[0], columns), lambda i: (0, 0)),
            *tiles(block, width),
        ]
        + [pl.BlockSpec(piece.shape, lambda i: (0, 0, 0)) for piece in pieces],
        out_specs=[
            pl.BlockSpec((total, columns), lambda i: (0, 0)),
            pl.BlockSpec((band * share * ranks, columns), lambda i: (0, 0)),
        ],
        out_shape=[shape(total, columns), shape(band * share * ranks, columns)],
        scratch_shapes=[pltpu.VMEM((rows, columns), jnp.float32), pltpu.VMEM((columns, width), jnp.float32)],
    )(rank_index, weight, *[flat_two] * PARTS, *pieces)


def apply_kernel(rows_ref, weight_ref, out_ref):
    weight = twice(both_parts(weight_ref[...], 1), 0)
    out_ref[...] = fold(mxu(both_parts(rows_ref[...], 1), weight, NN), 1)


def apply_to(rows, weight):
    count, width = rows.shape
    columns = weight.shape[1]
    block = block_of(count)
    return call(
        apply_kernel,
        8 * rows.size * columns,
        4 * (rows.size + count * columns),
        grid=(count // block,),
        in_specs=[
            pl.BlockSpec((block, width), lambda i: (i, 0)),
            pl.BlockSpec((width, columns), lambda i: (0, 0)),
        ],
        out_specs=pl.BlockSpec((block, columns), lambda i: (i, 0)),
        out_shape=shape(count, columns),
    )(rows, weight)


def small_inverse(entry):
    size = len(entry)
    entry = [list(row) for row in entry]
    inverse = [[None] * size for _ in range(size)]
    for k in range(size):
        pivot = entry[k][k]
        root = lax.rsqrt(pivot)
        root = root * (1.5 - 0.5 * pivot * root * root)
        inverse[k][k] = root
        for i in range(k + 1, size):
            entry[i][k] = entry[i][k] * root
        for i in range(k + 1, size):
            for m in range(k + 1, i + 1):
                entry[i][m] = entry[i][m] - entry[i][k] * entry[m][k]
    for k in range(size):
        for i in range(k + 1, size):
            total = entry[i][k] * inverse[k][k]
            for m in range(k + 1, i):
                total = total + entry[i][m] * inverse[m][k]
            inverse[i][k] = -total * inverse[i][i]
    return inverse


def factor(gram, inverse_ref):
    size, tile = gram.shape[0], BLOCK
    count = size // tile
    left = [gram[i * tile:(i + 1) * tile, :] for i in range(count)]
    lane = lax.broadcasted_iota(jnp.int32, (tile, size), 1)
    sublane = lax.broadcasted_iota(jnp.int32, (tile, size), 0)
    right = [jnp.where(lane == sublane + i * tile, 1.0, 0.0) for i in range(count)]

    def spread(value, row, column):
        return jnp.broadcast_to(value[row:row + 1, column:column + 1], (tile, size))

    for j in range(count):
        corner = [[spread(left[j], i, j * tile + k) for k in range(i + 1)] for i in range(tile)]
        small = small_inverse(corner)
        columns = []
        for k in range(tile):
            column = jnp.where(sublane == k, small[k][k], 0.0)
            for i in range(k + 1, tile):
                column = jnp.where(sublane == i, small[i][k], column)
            columns.append(column)
        done_left = sum(columns[k] * left[j][k:k + 1, :] for k in range(tile))
        done_right = sum(columns[k] * right[j][k:k + 1, :] for k in range(tile))
        inverse_ref[pl.ds(j * tile, tile), :] = done_right
        if j + 1 < count:
            turned = done_left.T
            for i in range(j + 1, count):
                for k in range(tile):
                    factor = jnp.broadcast_to(turned[i * tile:(i + 1) * tile, k:k + 1], (tile, size))
                    left[i] = left[i] - factor * done_left[k:k + 1, :]
                    right[i] = right[i] - factor * done_right[k:k + 1, :]


def first_kernel(scale, band, rank_ref, bridge_ref, raw_ref, weight_ref, solve_ref, inverse_ref):
    local_rows = weight_ref.shape[0] - band
    factor(exact(bridge_ref[...], raw_ref[...], TN), inverse_ref)
    inverse = inverse_ref[...]
    start = pl.multiple_of(rank_ref[0] * local_rows, local_rows)
    own = exact(raw_ref[pl.ds(start, local_rows), :], inverse, NT)
    weight_ref[:local_rows, :] = exact(own, inverse, NN)
    weight_ref[local_rows:, :] = inverse_ref[pl.ds(pl.multiple_of(rank_ref[0] * band, band), band), :]
    solve_ref[...] = scale * exact(bridge_ref[...], inverse, NT)


def first_factor(rank_index, bridge, raw, scale, local_rows, band):
    columns = raw.shape[1]
    whole = pl.BlockSpec(memory_space=pltpu.VMEM)
    return call(
        functools.partial(first_kernel, scale, band),
        8 * raw.size * columns,
        16 * raw.size,
        in_specs=[pl.BlockSpec(memory_space=pltpu.SMEM), whole, whole],
        out_specs=[whole, whole],
        out_shape=[shape(local_rows + band, columns), shape(*raw.shape)],
        scratch_shapes=[pltpu.VMEM((columns, columns), jnp.float32)],
    )(rank_index, bridge, raw)


def last_kernel(scale, joined_ref, middle_ref, carry_ref, out_ref, inverse_ref):
    columns = inverse_ref.shape[0]
    width = carry_ref.shape[1]
    factor(joined_ref[pl.ds(width, columns), :], inverse_ref)
    inverse = inverse_ref[...]
    carry_ref[...] = exact(inverse, joined_ref[pl.ds(0, width), :], NT)
    out_ref[...] = exact(middle_ref[...], scale * inverse, NT)


def last_factor(joined, middle, scale, width):
    columns = joined.shape[1]
    whole = pl.BlockSpec(memory_space=pltpu.VMEM)
    return call(
        functools.partial(last_kernel, scale),
        8 * middle.size * columns,
        8 * middle.size,
        in_specs=[whole, whole],
        out_specs=[whole, whole],
        out_shape=[shape(columns, width), shape(*middle.shape)],
        scratch_shapes=[pltpu.VMEM((columns, columns), jnp.float32)],
    )(joined, middle)


def swap(value, axis, offset):
    return lax.ppermute(value, axis, [(i, i ^ offset) for i in range(lax.axis_size(axis))])


def exchange(value, axes):
    return lax.all_to_all(value, axes, 0, 0, tiled=True)


def gather_all(value, axes):
    parts = lax.axis_size(axes)
    return exchange(jnp.broadcast_to(value[None], (parts,) + value.shape), axes)


def after(value, others):
    return lax.optimization_barrier((value, others))


def on_device(core_one, core_two, right_sketch, sketch_core):
    local_rows, slices, width = core_one.shape
    columns = right_sketch.shape[1]
    ranks, cuts = lax.axis_size("rank"), lax.axis_size("cuts")
    rank = lax.axis_index("rank")
    rank_index = rank.astype(jnp.int32).reshape(1)
    both = ("cuts", "rank")
    parts = ranks * cuts
    band = columns // ranks
    share = -(-slices // ranks)
    room = share * ranks
    halves = [share // 2, share - share // 2]
    filler = ((0, 0), (0, room - slices), (0, 0))
    core_two, sketch_core = jnp.pad(core_two, filler), jnp.pad(sketch_core, filler)
    flat_one = core_one.reshape(local_rows * slices, width)
    flat_two = core_two.reshape(local_rows * room, width)

    sketched, part = sketch(core_two, right_sketch, sketch_core)

    def send(names, source, behind):
        found = []
        for half, offset in names:
            start = (rank ^ offset) * share + half * halves[0]
            found.append(lax.dynamic_slice_in_dim(source, start, halves[half], 0))
        if behind is not None:
            found, _ = after(found, behind)
        return {name: swap(value, "rank", name[1]) if name[1] else value for name, value in zip(names, found)}

    far = ranks - 1
    near = [[(half, offset) for offset in range(1, far)] for half in range(2)]

    bits = [1 << bit for bit in range((ranks - 1).bit_length())]
    moved = send(near[0] + near[1], sketched, None)
    bridge_rows = jnp.sum(exchange(part.reshape(cuts, local_rows // cuts, columns), "cuts"), axis=0)
    flat_late, part = after(flat_one, part)
    square = square_of(flat_late)
    bridge_rows, (pieces, square) = after(bridge_rows, (moved, square))
    sketched, bridge_rows = after(sketched, bridge_rows)
    pieces.update(send([(0, 0), (1, 0)], sketched, None))
    bridge = gather_all(bridge_rows, both)
    bridge = bridge.reshape(cuts, ranks, -1, columns).swapaxes(0, 1).reshape(width, columns)

    raw = exact(square, bridge, NN)
    far_piece = send([(0, far)], sketched, raw)
    raw = jnp.sum(exchange(raw.reshape(parts, -1, columns), both), axis=0)
    raw, far_piece = after(raw, far_piece)
    pieces.update(far_piece)
    pieces.update(send([(1, far)], sketched, raw))
    raw = gather_all(raw, both).reshape(width, columns)

    loose = [loosen(rank_index, raw, [pieces[(half, offset)] for offset in range(ranks)]) for half in range(2)]
    loose[1], (bridge, raw) = after(loose[1], (bridge, raw))
    everyone = []
    for value, order in zip(loose, (bits, bits[::-1])):
        found = {0: value}
        for bit in order:
            found.update({offset ^ bit: swap(held, "rank", bit) for offset, held in list(found.items())})
        everyone += [found[offset] for offset in range(ranks)]

    scale = math.sqrt(local_rows * ranks * slices * cuts)
    weight, solve = first_factor(rank_index, bridge, raw, scale, local_rows, band)
    total = -(-(width + columns) // (BLOCK * parts)) * BLOCK * parts
    joined, middle = carry_rows(rank_index, weight, flat_two, everyone, halves, share, band, total)
    joined = jnp.sum(exchange(joined.reshape(parts, -1, columns), both), axis=0)
    joined = gather_all(joined, both).reshape(total, columns)
    left_core = apply_to(flat_one, solve).reshape(local_rows, slices, columns)
    scale = math.sqrt(columns * slices * cuts)
    carry, middle = last_factor(joined, middle, scale, width)
    middle_core = middle.reshape(band, room, columns)[:, :slices]
    return (left_core, middle_core, carry)


def solution(mesh):
    placed = (P("rank", "cuts", None), P("rank", "cuts", None), P(), P(None, "cuts", None))
    return jax.shard_map(
        on_device,
        mesh=mesh,
        in_specs=placed,
        out_specs=(P("rank", "cuts", None), P("rank", "cuts", None), P()),
        check_vma=False,
    )
```

```python
import functools
import math

import jax
import jax.numpy as jnp
from jax import lax
from jax.experimental import pallas as pl
from jax.experimental.pallas import tpu as pltpu
from jax.sharding import PartitionSpec as P

NT = (((1,), (1,)), ((), ()))
NN = (((1,), (0,)), ((), ()))
TN = (((0,), (0,)), ((), ()))
VMEM_LIMIT = 56 * 1024 * 1024
BLOCK = 8


PARTS = 4


def tiles(block, width):
    size = block // PARTS
    return [pl.BlockSpec((size, width), lambda i, q=q: (i * PARTS + q, 0)) for q in range(PARTS)]


def joined_rows(refs):
    return jnp.concatenate([ref[...] for ref in refs], axis=0)


def call(kernel, flops, size, **more):
    return pl.pallas_call(
        kernel,
        compiler_params=pltpu.CompilerParams(vmem_limit_bytes=VMEM_LIMIT),
        cost_estimate=pl.CostEstimate(flops=flops, bytes_accessed=size, transcendentals=0),
        **more,
    )


def shape(*extent):
    return jax.ShapeDtypeStruct(extent, jnp.float32)


def split(value):
    high = value.astype(jnp.bfloat16)
    return high, (value - high.astype(jnp.float32)).astype(jnp.bfloat16)


def mxu(a, b, form):
    return lax.dot_general(a, b, form, preferred_element_type=jnp.float32)


def exact(a, b, form):
    return lax.dot_general(a, b, form, precision=lax.Precision.HIGHEST, preferred_element_type=jnp.float32)


def both_parts(value, axis):
    return jnp.concatenate(split(value), axis=axis)


def twice(value, axis):
    return jnp.concatenate([value, value], axis=axis)


def fold(value, axis):
    half = value.shape[axis] // 2
    return lax.slice_in_dim(value, 0, half, axis=axis) + lax.slice_in_dim(value, half, 2 * half, axis=axis)


def rows_of(ref):
    return ref.reshape(ref.shape[0] * ref.shape[1], ref.shape[2])


def sketch_kernel(*refs):
    core_refs, (right_ref, left_ref, sketched_ref, part_ref, rows_ref) = refs[:PARTS], refs[PARTS:]
    block = left_ref.shape[1]
    local_rows = rows_ref.shape[0] // block
    columns = right_ref.shape[1]
    right = twice(both_parts(right_ref[...], 1), 0)
    rows_ref[...] = fold(mxu(both_parts(jnp.concatenate([rows_of(ref)[...] for ref in core_refs], axis=0), 1), right, NN), 1)
    left_rows = rows_of(left_ref)

    @pl.when(pl.program_id(0) == 0)
    def _():
        part_ref[...] = jnp.zeros_like(part_ref)

    sides, lefts = [], []
    for n in range(block):
        rows = rows_ref[pl.ds(n, local_rows, stride=block), :]
        sketched_ref[n] = rows
        sides.append(rows)
        lefts.append(left_rows[pl.ds(n, columns, stride=block), :])
    side = both_parts(jnp.concatenate(sides, axis=1), 1)
    left = twice(both_parts(jnp.concatenate(lefts, axis=1), 0), 1)
    part_ref[...] += fold(mxu(side, left, NT), 1)


def sketch(core_two, right_sketch, sketch_core):
    local_rows, slices, width = core_two.shape
    columns = right_sketch.shape[1]
    return call(
        sketch_kernel,
        2 * core_two.size * columns * 4,
        4 * (core_two.size + 2 * sketch_core.size),
        grid=(slices // BLOCK,),
        in_specs=[
            *[pl.BlockSpec((local_rows // PARTS, BLOCK, width), lambda i, q=q: (q, i, 0)) for q in range(PARTS)],
            pl.BlockSpec((width, columns), lambda i: (0, 0)),
            pl.BlockSpec((columns, BLOCK, columns), lambda i: (0, i, 0)),
        ],
        out_specs=[
            pl.BlockSpec((BLOCK, local_rows, columns), lambda i: (i, 0, 0)),
            pl.BlockSpec((local_rows, columns), lambda i: (0, 0)),
        ],
        out_shape=[shape(slices, local_rows, columns), shape(local_rows, columns)],
        scratch_shapes=[pltpu.VMEM((local_rows * BLOCK, columns), jnp.float32)],
    )(*[core_two] * PARTS, right_sketch, sketch_core)


def block_of(rows):
    block = 1024
    while rows % block:
        block //= 2
    return block


def square_kernel(core_ref, square_ref, sum_ref):
    step = pl.program_id(0)
    width = core_ref.shape[1]
    high, low = split(core_ref[...])

    @pl.when(step == 0)
    def _():
        sum_ref[...] = jnp.zeros_like(sum_ref)

    sum_ref[...] += mxu(high, jnp.concatenate([high, low], axis=1), TN)

    @pl.when(step == pl.num_programs(0) - 1)
    def _():
        cross = sum_ref[:, width:]
        square_ref[...] = sum_ref[:, :width] + cross + cross.T


def square_of(flat_one):
    rows, width = flat_one.shape
    block = block_of(rows)
    return call(
        square_kernel,
        4 * rows * width * width,
        4 * flat_one.size,
        grid=(rows // block,),
        in_specs=[pl.BlockSpec((block, width), lambda i: (i, 0))],
        out_specs=pl.BlockSpec((width, width), lambda i: (0, 0)),
        out_shape=shape(width, width),
        scratch_shapes=[pltpu.VMEM((width, 2 * width), jnp.float32)],
    )(flat_one)


def product_kernel(square_ref, bridge_ref, out_ref):
    bridge = twice(both_parts(bridge_ref[...], 1), 0)
    out_ref[...] = fold(mxu(both_parts(square_ref[...], 1), bridge, NN), 1)


def product_of(square, bridge):
    return call(
        product_kernel,
        8 * square.size * bridge.shape[1],
        4 * square.size + 8 * bridge.size,
        out_shape=shape(*bridge.shape),
    )(square, bridge)


def loose_kernel(rank_ref, raw_ref, *refs):
    piece_refs, out_ref = refs[:-1], refs[-1]
    count, local_rows, columns = piece_refs[0].shape
    rows = []
    for offset in range(len(piece_refs)):
        start = pl.multiple_of((rank_ref[0] ^ offset) * local_rows, local_rows)
        rows.append(raw_ref[pl.ds(start, local_rows), :])
    raw = twice(both_parts(jnp.concatenate(rows, axis=0), 1).T, 1)
    value = [jnp.concatenate([ref[n] for n in range(count)], axis=1) for ref in piece_refs]
    product = fold(mxu(raw, both_parts(jnp.concatenate(value, axis=0), 0), NN), 0)
    for n in range(count):
        out_ref[n] = product[:, n * columns:(n + 1) * columns]


def loosen(rank_index, raw, pieces):
    columns = raw.shape[1]
    size = len(pieces) * pieces[0].size
    whole = pl.BlockSpec(memory_space=pltpu.VMEM)
    return call(
        loose_kernel,
        8 * size * columns,
        4 * raw.size + 4 * size,
        in_specs=[pl.BlockSpec(memory_space=pltpu.SMEM)] + [whole] * (len(pieces) + 1),
        out_specs=whole,
        out_shape=shape(pieces[0].shape[0], columns, columns),
    )(rank_index, raw, *pieces)


def carry_kernel(halves, share, rank_ref, weight_ref, *refs):
    core_refs, piece_refs = refs[:PARTS], refs[PARTS:-4]
    joined_ref, middle_ref, rows_ref, sum_ref = refs[-4:]
    step = pl.program_id(0)
    block, width = core_refs[0].shape[0] * PARTS, core_refs[0].shape[1]
    columns = weight_ref.shape[1]
    ranks = len(piece_refs) // len(halves)
    room = share * ranks
    local_rows = rows_ref.shape[0] // room
    band = middle_ref.shape[0] // room

    @pl.when(step == 0)
    def _():
        sum_ref[...] = jnp.zeros_like(sum_ref)
        weight = twice(both_parts(weight_ref[...], 0), 1)
        for half, count in enumerate(halves):
            for offset in range(ranks):
                ref = piece_refs[half * ranks + offset]
                first = (rank_ref[0] ^ offset) * share + sum(halves[:half])
                value = both_parts(jnp.concatenate([ref[n] for n in range(count)], axis=1), 0)
                spread = fold(mxu(weight, value, NN), 0)
                for n in range(count):
                    piece = lax.slice_in_dim(spread, n * columns, (n + 1) * columns, axis=1)
                    rows_ref[pl.ds(first + n, local_rows, stride=room), :] = piece[:local_rows]
                    middle_ref[pl.ds(first + n, band, stride=room), :] = piece[local_rows:]

    rows = both_parts(rows_ref[pl.ds(pl.multiple_of(step * block, block), block), :], 1).T
    product = fold(mxu(twice(rows, 1), both_parts(joined_rows(core_refs), 0), NN), 0)
    sum_ref[...] += product

    @pl.when(step == pl.num_programs(0) - 1)
    def _():
        joined_ref[:width, :] = sum_ref[...].T
        middle = both_parts(middle_ref[...], 1)
        joined_ref[width:width + columns, :] = fold(fold(mxu(middle, middle, TN), 0), 1)
        joined_ref[width + columns:, :] = jnp.zeros_like(joined_ref[width + columns:, :])


def carry_rows(rank_index, weight, flat_two, pieces, halves, share, band, total):
    rows, width = flat_two.shape
    columns = weight.shape[1]
    block = block_of(rows)
    ranks = len(pieces) // len(halves)
    whole = pl.BlockSpec(memory_space=pltpu.VMEM)
    return call(
        functools.partial(carry_kernel, halves, share),
        8 * flat_two.size * columns,
        4 * flat_two.size + 4 * sum(piece.size for piece in pieces),
        grid=(rows // block,),
        in_specs=[
            pl.BlockSpec(memory_space=pltpu.SMEM),
            pl.BlockSpec((weight.shape[0], columns), lambda i: (0, 0)),
            *tiles(block, width),
        ]
        + [pl.BlockSpec(piece.shape, lambda i: (0, 0, 0)) for piece in pieces],
        out_specs=[
            pl.BlockSpec((total, columns), lambda i: (0, 0)),
            pl.BlockSpec((band * share * ranks, columns), lambda i: (0, 0)),
        ],
        out_shape=[shape(total, columns), shape(band * share * ranks, columns)],
        scratch_shapes=[pltpu.VMEM((rows, columns), jnp.float32), pltpu.VMEM((columns, width), jnp.float32)],
    )(rank_index, weight, *[flat_two] * PARTS, *pieces)


def apply_kernel(rows_ref, weight_ref, out_ref):
    weight = twice(both_parts(weight_ref[...], 1), 0)
    out_ref[...] = fold(mxu(both_parts(rows_ref[...], 1), weight, NN), 1)


def apply_to(rows, weight):
    count, width = rows.shape
    columns = weight.shape[1]
    block = block_of(count)
    return call(
        apply_kernel,
        8 * rows.size * columns,
        4 * (rows.size + count * columns),
        grid=(count // block,),
        in_specs=[
            pl.BlockSpec((block, width), lambda i: (i, 0)),
            pl.BlockSpec((width, columns), lambda i: (0, 0)),
        ],
        out_specs=pl.BlockSpec((block, columns), lambda i: (i, 0)),
        out_shape=shape(count, columns),
    )(rows, weight)


def small_inverse(entry):
    size = len(entry)
    entry = [list(row) for row in entry]
    inverse = [[None] * size for _ in range(size)]
    for k in range(size):
        pivot = entry[k][k]
        root = lax.rsqrt(pivot)
        inverse[k][k] = root
        for i in range(k + 1, size):
            entry[i][k] = entry[i][k] * root
        for i in range(k + 1, size):
            for m in range(k + 1, i + 1):
                entry[i][m] = entry[i][m] - entry[i][k] * entry[m][k]
    for k in range(size):
        for i in range(k + 1, size):
            total = entry[i][k] * inverse[k][k]
            for m in range(k + 1, i):
                total = total + entry[i][m] * inverse[m][k]
            inverse[i][k] = -total * inverse[i][i]
    return inverse


def factor(gram, inverse_ref):
    size, tile = gram.shape[0], BLOCK
    count = size // tile
    left = [gram[i * tile:(i + 1) * tile, :] for i in range(count)]
    lane = lax.broadcasted_iota(jnp.int32, (tile, size), 1)
    sublane = lax.broadcasted_iota(jnp.int32, (tile, size), 0)
    right = [jnp.where(lane == sublane + i * tile, 1.0, 0.0) for i in range(count)]

    def spread(value, row, column):
        return jnp.broadcast_to(value[row:row + 1, column:column + 1], (tile, size))

    for j in range(count):
        corner = [[spread(left[j], i, j * tile + k) for k in range(i + 1)] for i in range(tile)]
        small = small_inverse(corner)
        columns = []
        for k in range(tile):
            column = jnp.where(sublane == k, small[k][k], 0.0)
            for i in range(k + 1, tile):
                column = jnp.where(sublane == i, small[i][k], column)
            columns.append(column)
        done_left = sum(columns[k] * left[j][k:k + 1, :] for k in range(tile))
        done_right = sum(columns[k] * right[j][k:k + 1, :] for k in range(tile))
        inverse_ref[pl.ds(j * tile, tile), :] = done_right
        if j + 1 < count:
            turned = done_left.T
            for i in range(j + 1, count):
                for k in range(tile):
                    factor = jnp.broadcast_to(turned[i * tile:(i + 1) * tile, k:k + 1], (tile, size))
                    left[i] = left[i] - factor * done_left[k:k + 1, :]
                    right[i] = right[i] - factor * done_right[k:k + 1, :]


def first_kernel(scale, band, rank_ref, bridge_ref, raw_ref, weight_ref, solve_ref, inverse_ref):
    local_rows = weight_ref.shape[0] - band
    factor(exact(bridge_ref[...], raw_ref[...], TN), inverse_ref)
    inverse = inverse_ref[...]
    start = pl.multiple_of(rank_ref[0] * local_rows, local_rows)
    own = exact(raw_ref[pl.ds(start, local_rows), :], inverse, NT)
    weight_ref[:local_rows, :] = exact(own, inverse, NN)
    weight_ref[local_rows:, :] = inverse_ref[pl.ds(pl.multiple_of(rank_ref[0] * band, band), band), :]
    solve_ref[...] = scale * exact(bridge_ref[...], inverse, NT)


def first_factor(rank_index, bridge, raw, scale, local_rows, band):
    columns = raw.shape[1]
    whole = pl.BlockSpec(memory_space=pltpu.VMEM)
    return call(
        functools.partial(first_kernel, scale, band),
        8 * raw.size * columns,
        16 * raw.size,
        in_specs=[pl.BlockSpec(memory_space=pltpu.SMEM), whole, whole],
        out_specs=[whole, whole],
        out_shape=[shape(local_rows + band, columns), shape(*raw.shape)],
        scratch_shapes=[pltpu.VMEM((columns, columns), jnp.float32)],
    )(rank_index, bridge, raw)


def last_kernel(scale, joined_ref, middle_ref, carry_ref, out_ref, inverse_ref):
    columns = inverse_ref.shape[0]
    width = carry_ref.shape[1]
    factor(joined_ref[pl.ds(width, columns), :], inverse_ref)
    inverse = inverse_ref[...]
    carry_ref[...] = exact(inverse, joined_ref[pl.ds(0, width), :], NT)
    out_ref[...] = exact(middle_ref[...], scale * inverse, NT)


def last_factor(joined, middle, scale, width):
    columns = joined.shape[1]
    whole = pl.BlockSpec(memory_space=pltpu.VMEM)
    return call(
        functools.partial(last_kernel, scale),
        8 * middle.size * columns,
        8 * middle.size,
        in_specs=[whole, whole],
        out_specs=[whole, whole],
        out_shape=[shape(columns, width), shape(*middle.shape)],
        scratch_shapes=[pltpu.VMEM((columns, columns), jnp.float32)],
    )(joined, middle)


def swap(value, axis, offset):
    return lax.ppermute(value, axis, [(i, i ^ offset) for i in range(lax.axis_size(axis))])


def exchange(value, axes):
    return lax.all_to_all(value, axes, 0, 0, tiled=True)


def gather_all(value, axes):
    parts = lax.axis_size(axes)
    return exchange(jnp.broadcast_to(value[None], (parts,) + value.shape), axes)


def after(value, others):
    return lax.optimization_barrier((value, others))


def on_device(core_one, core_two, right_sketch, sketch_core):
    local_rows, slices, width = core_one.shape
    columns = right_sketch.shape[1]
    ranks, cuts = lax.axis_size("rank"), lax.axis_size("cuts")
    rank = lax.axis_index("rank")
    rank_index = rank.astype(jnp.int32).reshape(1)
    both = ("cuts", "rank")
    parts = ranks * cuts
    band = columns // ranks
    share = -(-slices // ranks)
    room = share * ranks
    halves = [share // 2, share - share // 2]
    filler = ((0, 0), (0, room - slices), (0, 0))
    core_two, sketch_core = jnp.pad(core_two, filler), jnp.pad(sketch_core, filler)
    flat_one = core_one.reshape(local_rows * slices, width)
    flat_two = core_two.reshape(local_rows * room, width)

    sketched, part = sketch(core_two, right_sketch, sketch_core)

    def send(names, source, behind):
        found = []
        for half, offset in names:
            start = (rank ^ offset) * share + half * halves[0]
            found.append(lax.dynamic_slice_in_dim(source, start, halves[half], 0))
        if behind is not None:
            found, _ = after(found, behind)
        return {name: swap(value, "rank", name[1]) if name[1] else value for name, value in zip(names, found)}

    far = ranks - 1
    near = [[(half, offset) for offset in range(1, far)] for half in range(2)]

    bits = [1 << bit for bit in range((ranks - 1).bit_length())]
    moved = send(near[0], sketched, None)
    bridge_rows = jnp.sum(exchange(part.reshape(cuts, local_rows // cuts, columns), "cuts"), axis=0)
    bridge_rows, pieces = after(bridge_rows, moved)
    flat_late, bridge_rows = after(flat_one, bridge_rows)
    sketched, bridge_rows = after(sketched, bridge_rows)
    moved = send(near[1] + [(0, far)], sketched, None)
    bridge = gather_all(bridge_rows, ("rank", "cuts")).reshape(width, columns)
    square = square_of(flat_late)
    pieces.update(send([(0, 0), (1, 0)], sketched, None))

    raw = product_of(square, bridge)
    raw, moved = after(raw, moved)
    pieces.update(moved)
    far_piece = send([(1, far)], sketched, raw)
    raw = jnp.sum(exchange(raw.reshape(parts, -1, columns), both), axis=0)
    raw, far_piece = after(raw, far_piece)
    pieces.update(far_piece)
    raw = gather_all(raw, both).reshape(width, columns)

    loose = [loosen(rank_index, raw, [pieces[(half, offset)] for offset in range(ranks)]) for half in range(2)]
    loose[1], (bridge, raw) = after(loose[1], (bridge, raw))
    everyone = []
    for value, order in zip(loose, (bits, bits[::-1])):
        found = {0: value}
        for bit in order:
            found.update({offset ^ bit: swap(held, "rank", bit) for offset, held in list(found.items())})
        everyone += [found[offset] for offset in range(ranks)]

    scale = math.sqrt(local_rows * ranks * slices * cuts)
    weight, solve = first_factor(rank_index, bridge, raw, scale, local_rows, band)
    total = -(-(width + columns) // (BLOCK * parts)) * BLOCK * parts
    joined, middle = carry_rows(rank_index, weight, flat_two, everyone, halves, share, band, total)
    joined = jnp.sum(exchange(joined.reshape(parts, -1, columns), both), axis=0)
    joined = gather_all(joined, both).reshape(total, columns)
    left_core = apply_to(flat_one, solve).reshape(local_rows, slices, columns)
    scale = math.sqrt(columns * slices * cuts)
    carry, middle = last_factor(joined, middle, scale, width)
    middle_core = middle.reshape(band, room, columns)[:, :slices]
    return (left_core, middle_core, carry)


def solution(mesh):
    placed = (P("rank", "cuts", None), P("rank", "cuts", None), P(), P(None, "cuts", None))
    return jax.shard_map(
        on_device,
        mesh=mesh,
        in_specs=placed,
        out_specs=(P("rank", "cuts", None), P("rank", "cuts", None), P()),
        check_vma=False,
    )
```

```python
import functools
import math

import jax
import jax.numpy as jnp
from jax import lax
from jax.experimental import pallas as pl
from jax.experimental.pallas import tpu as pltpu
from jax.sharding import PartitionSpec as P

NT = (((1,), (1,)), ((), ()))
NN = (((1,), (0,)), ((), ()))
TN = (((0,), (0,)), ((), ()))
VMEM_LIMIT = 56 * 1024 * 1024
BLOCK = 8


PARTS = 4


def call(kernel, flops, size, **more):
    return pl.pallas_call(
        kernel,
        compiler_params=pltpu.CompilerParams(vmem_limit_bytes=VMEM_LIMIT),
        cost_estimate=pl.CostEstimate(flops=flops, bytes_accessed=size, transcendentals=0),
        **more,
    )


def shape(*extent):
    return jax.ShapeDtypeStruct(extent, jnp.float32)


def split(value):
    high = value.astype(jnp.bfloat16)
    return high, (value - high.astype(jnp.float32)).astype(jnp.bfloat16)


def mxu(a, b, form):
    return lax.dot_general(a, b, form, preferred_element_type=jnp.float32)


def exact(a, b, form):
    return lax.dot_general(a, b, form, precision=lax.Precision.HIGHEST, preferred_element_type=jnp.float32)


def both_parts(value, axis):
    return jnp.concatenate(split(value), axis=axis)


def twice(value, axis):
    return jnp.concatenate([value, value], axis=axis)


def fold(value, axis):
    half = value.shape[axis] // 2
    return lax.slice_in_dim(value, 0, half, axis=axis) + lax.slice_in_dim(value, half, 2 * half, axis=axis)


def rows_of(ref):
    return ref.reshape(ref.shape[0] * ref.shape[1], ref.shape[2])


def sketch_kernel(*refs):
    core_refs, (right_ref, left_ref, sketched_ref, part_ref, rows_ref) = refs[:PARTS], refs[PARTS:]
    block = left_ref.shape[1]
    local_rows = rows_ref.shape[0] // block
    columns = right_ref.shape[1]
    right = twice(both_parts(right_ref[...], 1), 0)
    rows_ref[...] = fold(mxu(both_parts(jnp.concatenate([rows_of(ref)[...] for ref in core_refs], axis=0), 1), right, NN), 1)
    left_rows = rows_of(left_ref)

    @pl.when(pl.program_id(0) == 0)
    def _():
        part_ref[...] = jnp.zeros_like(part_ref)

    sides, lefts = [], []
    for n in range(block):
        rows = rows_ref[pl.ds(n, local_rows, stride=block), :]
        sketched_ref[n] = rows
        sides.append(rows)
        lefts.append(left_rows[pl.ds(n, columns, stride=block), :])
    side = both_parts(jnp.concatenate(sides, axis=1), 1)
    left = twice(both_parts(jnp.concatenate(lefts, axis=1), 0), 1)
    part_ref[...] += fold(mxu(side, left, NT), 1)


def sketch(core_two, right_sketch, sketch_core):
    local_rows, slices, width = core_two.shape
    columns = right_sketch.shape[1]
    return call(
        sketch_kernel,
        2 * core_two.size * columns * 4,
        4 * (core_two.size + 2 * sketch_core.size),
        grid=(slices // BLOCK,),
        in_specs=[
            *[pl.BlockSpec((local_rows // PARTS, BLOCK, width), lambda i, q=q: (q, i, 0)) for q in range(PARTS)],
            pl.BlockSpec((width, columns), lambda i: (0, 0)),
            pl.BlockSpec((columns, BLOCK, columns), lambda i: (0, i, 0)),
        ],
        out_specs=[
            pl.BlockSpec((BLOCK, local_rows, columns), lambda i: (i, 0, 0)),
            pl.BlockSpec((local_rows, columns), lambda i: (0, 0)),
        ],
        out_shape=[shape(slices, local_rows, columns), shape(local_rows, columns)],
        scratch_shapes=[pltpu.VMEM((local_rows * BLOCK, columns), jnp.float32)],
    )(*[core_two] * PARTS, right_sketch, sketch_core)


def block_of(rows):
    block = 1024
    while rows % block:
        block //= 2
    return block


def square_kernel(core_ref, square_ref, sum_ref):
    step = pl.program_id(0)
    width = core_ref.shape[1]
    high, low = split(core_ref[...])

    @pl.when(step == 0)
    def _():
        sum_ref[...] = jnp.zeros_like(sum_ref)

    sum_ref[...] += mxu(high, jnp.concatenate([high, low], axis=1), TN)

    @pl.when(step == pl.num_programs(0) - 1)
    def _():
        cross = sum_ref[:, width:]
        square_ref[...] = both_parts(sum_ref[:, :width] + cross + cross.T, 1)


def square_of(flat_one):
    rows, width = flat_one.shape
    block = block_of(rows)
    return call(
        square_kernel,
        4 * rows * width * width,
        4 * flat_one.size,
        grid=(rows // block,),
        in_specs=[pl.BlockSpec((block, width), lambda i: (i, 0))],
        out_specs=pl.BlockSpec((width, 2 * width), lambda i: (0, 0)),
        out_shape=jax.ShapeDtypeStruct((width, 2 * width), jnp.bfloat16),
        scratch_shapes=[pltpu.VMEM((width, 2 * width), jnp.float32)],
    )(flat_one)


def product_kernel(square_ref, bridge_ref, out_ref):
    bridge = twice(both_parts(bridge_ref[...], 1), 0)
    out_ref[...] = fold(mxu(square_ref[...], bridge, NN), 1)


def product_of(square, bridge):
    return call(
        product_kernel,
        4 * square.size * bridge.shape[1],
        2 * square.size + 8 * bridge.size,
        out_shape=shape(*bridge.shape),
    )(square, bridge)


def loose_kernel(rank_ref, raw_ref, *refs):
    piece_refs, out_refs = refs[:-2], refs[-2:]
    ranks = len(piece_refs) // 2
    local_rows, columns = piece_refs[0].shape[1:]
    rows = []
    for offset in range(ranks):
        start = pl.multiple_of((rank_ref[0] ^ offset) * local_rows, local_rows)
        rows.append(raw_ref[pl.ds(start, local_rows), :])
    raw = twice(both_parts(jnp.concatenate(rows, axis=0), 1).T, 1)
    for half, out_ref in enumerate(out_refs):
        refs = piece_refs[half * ranks:(half + 1) * ranks]
        count = out_ref.shape[0]
        value = [jnp.concatenate([ref[n] for n in range(count)], axis=1) for ref in refs]
        product = fold(mxu(raw, both_parts(jnp.concatenate(value, axis=0), 0), NN), 0)
        for n in range(count):
            out_ref[n] = product[:, n * columns:(n + 1) * columns]


def loosen(rank_index, raw, pieces, halves):
    columns = raw.shape[1]
    size = sum(piece.size for piece in pieces)
    whole = pl.BlockSpec(memory_space=pltpu.VMEM)
    return call(
        loose_kernel,
        8 * size * columns,
        4 * raw.size + 4 * size,
        in_specs=[pl.BlockSpec(memory_space=pltpu.SMEM)] + [whole] * (len(pieces) + 1),
        out_specs=[whole] * 2,
        out_shape=[shape(count, columns, columns) for count in halves],
    )(rank_index, raw, *pieces)


def slot_places(rank, places, pieces):
    return [
        (rank ^ offset) * stride + n
        for (offset, stride, first), piece in zip(places, pieces)
        for n in range(first, first + piece.shape[0])
    ]


def carry_kernel(places, room, last, tiles, rank_ref, weight_ref, *refs):
    core_refs, refs = refs[:tiles], refs[tiles:]
    piece_refs = refs[:len(places)]
    if last:
        before_ref, before_gram_ref, out_ref, middle_ref, spread_ref, sum_ref = refs[len(places):]
    else:
        out_ref, gram_ref, middle_ref, spread_ref, sum_ref = refs[len(places):]
    step = pl.program_id(0)
    columns = weight_ref.shape[1]
    local_rows = spread_ref.shape[1]
    width = sum_ref.shape[1]
    block = core_refs[0].shape[0] // room
    slots = slot_places(rank_ref[0], places, piece_refs)

    @pl.when(step == 0)
    def _():
        sum_ref[...] = before_ref[...] if last else jnp.zeros_like(sum_ref)
        weight = twice(both_parts(weight_ref[...], 0), 1)
        slot = 0
        for ref in piece_refs:
            count = ref.shape[0]
            value = both_parts(jnp.concatenate([ref[n] for n in range(count)], axis=1), 0)
            spread = fold(mxu(weight, value, NN), 0)
            for n in range(count):
                piece = lax.slice_in_dim(spread, n * columns, (n + 1) * columns, axis=1)
                spread_ref[slot] = piece[:local_rows]
                middle_ref[slot] = piece[local_rows:]
                slot += 1

    start = pl.multiple_of(step * block, block)
    rows = jnp.concatenate([spread_ref[slot, pl.ds(start, block), :] for slot in range(len(slots))], axis=0)
    core = [[ref[pl.ds(place, block, stride=room), :] for ref in core_refs] for place in slots]
    core = jnp.concatenate([jnp.concatenate(row, axis=1) for row in core], axis=0)
    product = fold(mxu(twice(both_parts(rows, 1).T, 1), both_parts(core, 0), NN), 0)
    sum_ref[...] += product

    @pl.when(step == pl.num_programs(0) - 1)
    def _():
        middle = jnp.concatenate([middle_ref[slot] for slot in range(len(slots))], axis=0)
        middle = both_parts(middle, 1)
        gram = fold(fold(mxu(middle, middle, TN), 0), 1)
        if last:
            out_ref[:width, :] = sum_ref[...].T
            out_ref[width:width + columns, :] = gram + before_gram_ref[...]
            out_ref[width + columns:, :] = jnp.zeros_like(out_ref[width + columns:, :])
        else:
            out_ref[...] = sum_ref[...]
            gram_ref[...] = gram


def carry_rows(rank_index, weight, flat_two, pieces, places, room, band, before, total):
    rows, width = flat_two.shape
    columns = weight.shape[1]
    local_rows = rows // room
    block = math.gcd(local_rows, 32)
    tiles = max(width // 128, 1)
    slots = sum(piece.shape[0] for piece in pieces)
    last = before is not None
    fixed = [pl.BlockSpec(piece.shape, lambda i: (0, 0, 0)) for piece in pieces]
    outs = [shape(columns, width), shape(columns, columns)]
    if last:
        fixed += [pl.BlockSpec(value.shape, lambda i: (0, 0)) for value in before]
        outs = [shape(total, columns)]
    return call(
        functools.partial(carry_kernel, places, room, last, tiles),
        8 * slots * local_rows * width * columns,
        4 * flat_two.size + 4 * sum(piece.size for piece in pieces),
        grid=(local_rows // block,),
        in_specs=[
            pl.BlockSpec(memory_space=pltpu.SMEM),
            pl.BlockSpec((weight.shape[0], columns), lambda i: (0, 0)),
            *[pl.BlockSpec((block * room, width // tiles), lambda i, q=q: (i, q)) for q in range(tiles)],
        ]
        + fixed,
        out_specs=[pl.BlockSpec(out.shape, lambda i: (0, 0)) for out in outs]
        + [pl.BlockSpec((slots, band, columns), lambda i: (0, 0, 0))],
        out_shape=outs + [shape(slots, band, columns)],
        scratch_shapes=[pltpu.VMEM((slots, local_rows, columns), jnp.float32), pltpu.VMEM((columns, width), jnp.float32)],
    )(rank_index, weight, *[flat_two] * tiles, *pieces, *(before or ()))


def apply_kernel(rows_ref, weight_ref, out_ref):
    weight = twice(both_parts(weight_ref[...], 1), 0)
    out_ref[...] = fold(mxu(both_parts(rows_ref[...], 1), weight, NN), 1)


def apply_to(rows, weight):
    count, width = rows.shape
    columns = weight.shape[1]
    block = block_of(count)
    return call(
        apply_kernel,
        8 * rows.size * columns,
        4 * (rows.size + count * columns),
        grid=(count // block,),
        in_specs=[
            pl.BlockSpec((block, width), lambda i: (i, 0)),
            pl.BlockSpec((width, columns), lambda i: (0, 0)),
        ],
        out_specs=pl.BlockSpec((block, columns), lambda i: (i, 0)),
        out_shape=shape(count, columns),
    )(rows, weight)


def small_inverse(entry):
    size = len(entry)
    entry = [list(row) for row in entry]
    unit = [[None] * size for _ in range(size)]
    for k in range(size):
        scaled = 1.0 / entry[k][k]
        for i in range(k + 1, size):
            unit[i][k] = entry[i][k] * scaled
        for i in range(k + 1, size):
            for m in range(k + 1, i + 1):
                entry[i][m] = entry[i][m] - unit[i][k] * entry[m][k]
    roots = [lax.rsqrt(entry[k][k]) for k in range(size)]
    inverse = [[None] * size for _ in range(size)]
    for k in range(size):
        inverse[k][k] = 1.0
        for i in range(k + 1, size):
            total = unit[i][k]
            for m in range(k + 1, i):
                total = total + unit[i][m] * inverse[m][k]
            inverse[i][k] = -total
    return [[inverse[i][k] * roots[i] for k in range(i + 1)] for i in range(size)]


def factor(gram, inverse_ref):
    size, tile = gram.shape[0], BLOCK
    count = size // tile
    left = [gram[i * tile:(i + 1) * tile, :] for i in range(count)]
    lane = lax.broadcasted_iota(jnp.int32, (tile, size), 1)
    sublane = lax.broadcasted_iota(jnp.int32, (tile, size), 0)
    right = [jnp.where(lane == sublane + i * tile, 1.0, 0.0) for i in range(count)]

    def spread(value, row, column):
        return jnp.broadcast_to(value[row:row + 1, column:column + 1], (tile, size))

    for j in range(count):
        corner = [[spread(left[j], i, j * tile + k) for k in range(i + 1)] for i in range(tile)]
        small = small_inverse(corner)
        columns = []
        for k in range(tile):
            column = jnp.where(sublane == k, small[k][k], 0.0)
            for i in range(k + 1, tile):
                column = jnp.where(sublane == i, small[i][k], column)
            columns.append(column)
        done_left = sum(columns[k] * left[j][k:k + 1, :] for k in range(tile))
        done_right = sum(columns[k] * right[j][k:k + 1, :] for k in range(tile))
        inverse_ref[pl.ds(j * tile, tile), :] = done_right
        if j + 1 < count:
            turned = done_left.T
            for i in range(j + 1, count):
                for k in range(tile):
                    factor = jnp.broadcast_to(turned[i * tile:(i + 1) * tile, k:k + 1], (tile, size))
                    left[i] = left[i] - factor * done_left[k:k + 1, :]
                    right[i] = right[i] - factor * done_right[k:k + 1, :]


def first_kernel(scale, band, rank_ref, bridge_ref, raw_ref, weight_ref, solve_ref, inverse_ref):
    local_rows = weight_ref.shape[0] - band
    factor(exact(bridge_ref[...], raw_ref[...], TN), inverse_ref)
    inverse = inverse_ref[...]
    start = pl.multiple_of(rank_ref[0] * local_rows, local_rows)
    own = exact(raw_ref[pl.ds(start, local_rows), :], inverse, NT)
    weight_ref[:local_rows, :] = exact(own, inverse, NN)
    weight_ref[local_rows:, :] = inverse_ref[pl.ds(pl.multiple_of(rank_ref[0] * band, band), band), :]
    solve_ref[...] = scale * exact(bridge_ref[...], inverse, NT)


def first_factor(rank_index, bridge, raw, scale, local_rows, band):
    columns = raw.shape[1]
    whole = pl.BlockSpec(memory_space=pltpu.VMEM)
    return call(
        functools.partial(first_kernel, scale, band),
        8 * raw.size * columns,
        16 * raw.size,
        in_specs=[pl.BlockSpec(memory_space=pltpu.SMEM), whole, whole],
        out_specs=[whole, whole],
        out_shape=[shape(local_rows + band, columns), shape(*raw.shape)],
        scratch_shapes=[pltpu.VMEM((columns, columns), jnp.float32)],
    )(rank_index, bridge, raw)


def last_kernel(scale, places, room, rank_ref, joined_ref, *refs):
    middle_refs = refs[:len(places)]
    carry_ref, out_ref, inverse_ref = refs[len(places):]
    columns = inverse_ref.shape[0]
    width = carry_ref.shape[1]
    factor(joined_ref[pl.ds(width, columns), :], inverse_ref)
    inverse = inverse_ref[...]
    carry_ref[...] = exact(inverse, joined_ref[pl.ds(0, width), :], NT)
    inverse = scale * inverse
    for ref, group in zip(middle_refs, places):
        count, band, _ = ref.shape
        rows = jnp.concatenate([ref[slot] for slot in range(count)], axis=0)
        rows = exact(rows, inverse, NT)
        slot = 0
        for offset, stride, first, pieces in group:
            for n in range(first, first + pieces):
                place = (rank_ref[0] ^ offset) * stride + n
                out_ref[pl.ds(place, band, stride=room), :] = rows[slot * band:(slot + 1) * band]
                slot += 1


def last_factor(rank_index, joined, middles, scale, width, places, room):
    columns = joined.shape[1]
    band = middles[0].shape[1]
    whole = pl.BlockSpec(memory_space=pltpu.VMEM)
    return call(
        functools.partial(last_kernel, scale, places, room),
        8 * room * band * columns * columns,
        8 * room * band * columns,
        in_specs=[pl.BlockSpec(memory_space=pltpu.SMEM), whole] + [whole] * len(middles),
        out_specs=[whole, whole],
        out_shape=[shape(columns, width), shape(room * band, columns)],
        scratch_shapes=[pltpu.VMEM((columns, columns), jnp.float32)],
    )(rank_index, joined, *middles)


def swap(value, axis, offset):
    return lax.ppermute(value, axis, [(i, i ^ offset) for i in range(lax.axis_size(axis))])


def exchange(value, axes):
    return lax.all_to_all(value, axes, 0, 0, tiled=True)


def gather_all(value, axes):
    parts = lax.axis_size(axes)
    return exchange(jnp.broadcast_to(value[None], (parts,) + value.shape), axes)


def after(value, others):
    return lax.optimization_barrier((value, others))


def on_device(core_one, core_two, right_sketch, sketch_core):
    local_rows, slices, width = core_one.shape
    columns = right_sketch.shape[1]
    ranks, cuts = lax.axis_size("rank"), lax.axis_size("cuts")
    rank = lax.axis_index("rank")
    rank_index = rank.astype(jnp.int32).reshape(1)
    both = ("cuts", "rank")
    parts = ranks * cuts
    band = columns // ranks
    share = -(-slices // ranks)
    room = share * ranks
    halves = [share // 2, share - share // 2]
    filler = ((0, 0), (0, room - slices), (0, 0))
    core_two, sketch_core = jnp.pad(core_two, filler), jnp.pad(sketch_core, filler)
    flat_one = core_one.reshape(local_rows * slices, width)
    flat_two = core_two.reshape(local_rows * room, width)

    sketched, part = sketch(core_two, right_sketch, sketch_core)

    def send(names, source, behind):
        found = []
        for half, offset in names:
            start = (rank ^ offset) * share + half * halves[0]
            found.append(lax.dynamic_slice_in_dim(source, start, halves[half], 0))
        if behind is not None:
            found, _ = after(found, behind)
        return {name: swap(value, "rank", name[1]) if name[1] else value for name, value in zip(names, found)}

    far = ranks - 1
    near = [[(half, offset) for offset in range(1, far)] for half in range(2)]

    bits = [1 << bit for bit in range((ranks - 1).bit_length())]
    moved = send(near[0], sketched, None)
    bridge_rows = jnp.sum(exchange(part.reshape(cuts, local_rows // cuts, columns), "cuts"), axis=0)
    bridge_rows, pieces = after(bridge_rows, moved)
    flat_late, bridge_rows = after(flat_one, bridge_rows)
    sketched, bridge_rows = after(sketched, bridge_rows)
    moved = send(near[1] + [(0, far)], sketched, None)
    bridge = gather_all(bridge_rows, ("rank", "cuts")).reshape(width, columns)
    square = square_of(flat_late)
    pieces.update(send([(0, 0), (1, 0)], sketched, None))

    raw = product_of(square, bridge)
    raw, moved = after(raw, moved)
    pieces.update(moved)
    far_piece = send([(1, far)], sketched, raw)
    raw = jnp.sum(exchange(raw.reshape(parts, -1, columns), both), axis=0)
    raw, far_piece = after(raw, far_piece)
    pieces.update(far_piece)
    raw = gather_all(raw, both).reshape(width, columns)

    ordered = [pieces[(half, offset)] for half in range(2) for offset in range(ranks)]
    loose = loosen(rank_index, raw, ordered, halves)
    loose, (bridge, raw) = after(loose, (bridge, raw))
    groups = [[], []]
    for half, order in enumerate((bits, bits[::-1])):
        found = {0: loose[half]}
        for bit in order:
            found.update({offset ^ bit: swap(held, "rank", bit) for offset, held in list(found.items())})
        for offset, held in found.items():
            late = offset not in (0, *order[:1])
            groups[late].append((held, (offset, share, half * halves[0])))
    groups = [group for group in groups if group]

    scale = math.sqrt(local_rows * ranks * slices * cuts)
    weight, solve = first_factor(rank_index, bridge, raw, scale, local_rows, band)
    total = -(-(width + columns) // (BLOCK * parts)) * BLOCK * parts
    joined, middles = None, []
    for group in groups:
        held, places = zip(*group)
        *joined, middle = carry_rows(rank_index, weight, flat_two, held, places, room, band, joined, total)
        middles.append(middle)
    joined = joined[0]
    joined = jnp.sum(exchange(joined.reshape(parts, -1, columns), both), axis=0)
    joined = gather_all(joined, both).reshape(total, columns)
    left_core = apply_to(flat_one, solve).reshape(local_rows, slices, columns)
    scale = math.sqrt(columns * slices * cuts)
    places = [[(*place, held.shape[0]) for held, place in group] for group in groups]
    carry, middle = last_factor(rank_index, joined, middles, scale, width, places, room)
    middle_core = middle.reshape(band, room, columns)[:, :slices]
    return (left_core, middle_core, carry)


def solution(mesh):
    placed = (P("rank", "cuts", None), P("rank", "cuts", None), P(), P(None, "cuts", None))
    return jax.shard_map(
        on_device,
        mesh=mesh,
        in_specs=placed,
        out_specs=(P("rank", "cuts", None), P("rank", "cuts", None), P()),
        check_vma=False,
    )
```

```python
import functools
import math

import jax
import jax.numpy as jnp
from jax import lax
from jax.experimental import pallas as pl
from jax.experimental.pallas import tpu as pltpu
from jax.sharding import PartitionSpec as P

NT = (((1,), (1,)), ((), ()))
NN = (((1,), (0,)), ((), ()))
TN = (((0,), (0,)), ((), ()))
VMEM_LIMIT = 56 * 1024 * 1024
BLOCK = 8


PARTS = 4


def tiles(block, width):
    size = block // PARTS
    return [pl.BlockSpec((size, width), lambda i, q=q: (i * PARTS + q, 0)) for q in range(PARTS)]


def joined_rows(refs):
    return jnp.concatenate([ref[...] for ref in refs], axis=0)


def call(kernel, flops, size, **more):
    return pl.pallas_call(
        kernel,
        compiler_params=pltpu.CompilerParams(vmem_limit_bytes=VMEM_LIMIT),
        cost_estimate=pl.CostEstimate(flops=flops, bytes_accessed=size, transcendentals=0),
        **more,
    )


def shape(*extent):
    return jax.ShapeDtypeStruct(extent, jnp.float32)


def split(value):
    high = value.astype(jnp.bfloat16)
    return high, (value - high.astype(jnp.float32)).astype(jnp.bfloat16)


def mxu(a, b, form):
    return lax.dot_general(a, b, form, preferred_element_type=jnp.float32)


def exact(a, b, form):
    return lax.dot_general(a, b, form, precision=lax.Precision.HIGHEST, preferred_element_type=jnp.float32)


def both_parts(value, axis):
    return jnp.concatenate(split(value), axis=axis)


def twice(value, axis):
    return jnp.concatenate([value, value], axis=axis)


def fold(value, axis):
    half = value.shape[axis] // 2
    return lax.slice_in_dim(value, 0, half, axis=axis) + lax.slice_in_dim(value, half, 2 * half, axis=axis)


def rows_of(ref):
    return ref.reshape(ref.shape[0] * ref.shape[1], ref.shape[2])


def sketch_kernel(*refs):
    core_refs, (right_ref, left_ref, sketched_ref, part_ref, rows_ref) = refs[:PARTS], refs[PARTS:]
    block = left_ref.shape[1]
    local_rows = rows_ref.shape[0] // block
    columns = right_ref.shape[1]
    right = twice(both_parts(right_ref[...], 1), 0)
    rows_ref[...] = fold(mxu(both_parts(jnp.concatenate([rows_of(ref)[...] for ref in core_refs], axis=0), 1), right, NN), 1)
    left_rows = rows_of(left_ref)

    @pl.when(pl.program_id(0) == 0)
    def _():
        part_ref[...] = jnp.zeros_like(part_ref)

    sides, lefts = [], []
    for n in range(block):
        rows = rows_ref[pl.ds(n, local_rows, stride=block), :]
        sketched_ref[n] = rows
        sides.append(rows)
        lefts.append(left_rows[pl.ds(n, columns, stride=block), :])
    side = both_parts(jnp.concatenate(sides, axis=1), 1)
    left = twice(both_parts(jnp.concatenate(lefts, axis=1), 0), 1)
    part_ref[...] += fold(mxu(side, left, NT), 1)


def sketch(core_two, right_sketch, sketch_core):
    local_rows, slices, width = core_two.shape
    columns = right_sketch.shape[1]
    return call(
        sketch_kernel,
        2 * core_two.size * columns * 4,
        4 * (core_two.size + 2 * sketch_core.size),
        grid=(slices // BLOCK,),
        in_specs=[
            *[pl.BlockSpec((local_rows // PARTS, BLOCK, width), lambda i, q=q: (q, i, 0)) for q in range(PARTS)],
            pl.BlockSpec((width, columns), lambda i: (0, 0)),
            pl.BlockSpec((columns, BLOCK, columns), lambda i: (0, i, 0)),
        ],
        out_specs=[
            pl.BlockSpec((BLOCK, local_rows, columns), lambda i: (i, 0, 0)),
            pl.BlockSpec((local_rows, columns), lambda i: (0, 0)),
        ],
        out_shape=[shape(slices, local_rows, columns), shape(local_rows, columns)],
        scratch_shapes=[pltpu.VMEM((local_rows * BLOCK, columns), jnp.float32)],
    )(*[core_two] * PARTS, right_sketch, sketch_core)


def block_of(rows):
    block = 1024
    while rows % block:
        block //= 2
    return block


def square_kernel(core_ref, square_ref, sum_ref):
    step = pl.program_id(0)
    width = core_ref.shape[1]
    high, low = split(core_ref[...])

    @pl.when(step == 0)
    def _():
        sum_ref[...] = jnp.zeros_like(sum_ref)

    sum_ref[...] += mxu(high, jnp.concatenate([high, low], axis=1), TN)

    @pl.when(step == pl.num_programs(0) - 1)
    def _():
        cross = sum_ref[:, width:]
        square_ref[...] = both_parts(sum_ref[:, :width] + cross + cross.T, 1)


def square_of(flat_one):
    rows, width = flat_one.shape
    block = block_of(rows)
    return call(
        square_kernel,
        4 * rows * width * width,
        4 * flat_one.size,
        grid=(rows // block,),
        in_specs=[pl.BlockSpec((block, width), lambda i: (i, 0))],
        out_specs=pl.BlockSpec((width, 2 * width), lambda i: (0, 0)),
        out_shape=jax.ShapeDtypeStruct((width, 2 * width), jnp.bfloat16),
        scratch_shapes=[pltpu.VMEM((width, 2 * width), jnp.float32)],
    )(flat_one)


def product_kernel(square_ref, bridge_ref, out_ref):
    bridge = twice(both_parts(bridge_ref[...], 1), 0)
    out_ref[...] = fold(mxu(square_ref[...], bridge, NN), 1)


def product_of(square, bridge):
    return call(
        product_kernel,
        4 * square.size * bridge.shape[1],
        2 * square.size + 8 * bridge.size,
        out_shape=shape(*bridge.shape),
    )(square, bridge)


def loose_kernel(rank_ref, raw_ref, *refs):
    piece_refs, out_refs = refs[:-2], refs[-2:]
    ranks = len(piece_refs) // 2
    local_rows, columns = piece_refs[0].shape[1:]
    rows = []
    for offset in range(ranks):
        start = pl.multiple_of((rank_ref[0] ^ offset) * local_rows, local_rows)
        rows.append(raw_ref[pl.ds(start, local_rows), :])
    raw = twice(both_parts(jnp.concatenate(rows, axis=0), 1).T, 1)
    for half, out_ref in enumerate(out_refs):
        refs = piece_refs[half * ranks:(half + 1) * ranks]
        count = out_ref.shape[0]
        value = [jnp.concatenate([ref[n] for n in range(count)], axis=1) for ref in refs]
        product = fold(mxu(raw, both_parts(jnp.concatenate(value, axis=0), 0), NN), 0)
        for n in range(count):
            out_ref[n] = product[:, n * columns:(n + 1) * columns]


def loosen(rank_index, raw, pieces, halves):
    columns = raw.shape[1]
    size = sum(piece.size for piece in pieces)
    whole = pl.BlockSpec(memory_space=pltpu.VMEM)
    return call(
        loose_kernel,
        8 * size * columns,
        4 * raw.size + 4 * size,
        in_specs=[pl.BlockSpec(memory_space=pltpu.SMEM)] + [whole] * (len(pieces) + 1),
        out_specs=[whole] * 2,
        out_shape=[shape(count, columns, columns) for count in halves],
    )(rank_index, raw, *pieces)


def carry_kernel(halves, share, rank_ref, weight_ref, *refs):
    core_refs, piece_refs = refs[:PARTS], refs[PARTS:-5]
    raw_ref, gram_ref, middle_ref, rows_ref, sum_ref = refs[-5:]
    step = pl.program_id(0)
    block, width = core_refs[0].shape[0] * PARTS, core_refs[0].shape[1]
    columns = weight_ref.shape[1]
    ranks = len(piece_refs) // len(halves)
    room = share * ranks
    local_rows = rows_ref.shape[0] // room
    band = middle_ref.shape[0] // room

    @pl.when(step == 0)
    def _():
        sum_ref[...] = jnp.zeros_like(sum_ref)
        weight = twice(both_parts(weight_ref[...], 0), 1)
        for half, count in enumerate(halves):
            for offset in range(ranks):
                ref = piece_refs[half * ranks + offset]
                first = (rank_ref[0] ^ offset) * share + sum(halves[:half])
                value = both_parts(jnp.concatenate([ref[n] for n in range(count)], axis=1), 0)
                spread = fold(mxu(weight, value, NN), 0)
                for n in range(count):
                    piece = lax.slice_in_dim(spread, n * columns, (n + 1) * columns, axis=1)
                    rows_ref[pl.ds(first + n, local_rows, stride=room), :] = piece[:local_rows]
                    middle_ref[pl.ds(first + n, band, stride=room), :] = piece[local_rows:]

    rows = both_parts(rows_ref[pl.ds(pl.multiple_of(step * block, block), block), :], 1).T
    product = fold(mxu(twice(rows, 1), both_parts(joined_rows(core_refs), 0), NN), 0)
    sum_ref[...] += product

    @pl.when(step == pl.num_programs(0) - 1)
    def _():
        raw_ref[...] = sum_ref[...].T
        middle = both_parts(middle_ref[...], 1)
        gram_ref[...] = fold(fold(mxu(middle, middle, TN), 0), 1)


def carry_rows(rank_index, weight, flat_two, pieces, halves, share, band):
    rows, width = flat_two.shape
    columns = weight.shape[1]
    block = block_of(rows)
    ranks = len(pieces) // len(halves)
    whole = pl.BlockSpec(memory_space=pltpu.VMEM)
    return call(
        functools.partial(carry_kernel, halves, share),
        8 * flat_two.size * columns,
        4 * flat_two.size + 4 * sum(piece.size for piece in pieces),
        grid=(rows // block,),
        in_specs=[
            pl.BlockSpec(memory_space=pltpu.SMEM),
            pl.BlockSpec((weight.shape[0], columns), lambda i: (0, 0)),
            *tiles(block, width),
        ]
        + [pl.BlockSpec(piece.shape, lambda i: (0, 0, 0)) for piece in pieces],
        out_specs=[
            pl.BlockSpec((width, columns), lambda i: (0, 0)),
            pl.BlockSpec((columns, columns), lambda i: (0, 0)),
            pl.BlockSpec((band * share * ranks, columns), lambda i: (0, 0)),
        ],
        out_shape=[shape(width, columns), shape(columns, columns), shape(band * share * ranks, columns)],
        scratch_shapes=[pltpu.VMEM((rows, columns), jnp.float32), pltpu.VMEM((columns, width), jnp.float32)],
    )(rank_index, weight, *[flat_two] * PARTS, *pieces)


def apply_kernel(rows_ref, weight_ref, out_ref):
    weight = twice(both_parts(weight_ref[...], 1), 0)
    out_ref[...] = fold(mxu(both_parts(rows_ref[...], 1), weight, NN), 1)


def apply_to(rows, weight):
    count, width = rows.shape
    columns = weight.shape[1]
    block = block_of(count)
    return call(
        apply_kernel,
        8 * rows.size * columns,
        4 * (rows.size + count * columns),
        grid=(count // block,),
        in_specs=[
            pl.BlockSpec((block, width), lambda i: (i, 0)),
            pl.BlockSpec((width, columns), lambda i: (0, 0)),
        ],
        out_specs=pl.BlockSpec((block, columns), lambda i: (i, 0)),
        out_shape=shape(count, columns),
    )(rows, weight)


def small_inverse(entry):
    size = len(entry)
    entry = [list(row) for row in entry]
    inverse = [[None] * size for _ in range(size)]
    for k in range(size):
        pivot = entry[k][k]
        root = lax.rsqrt(pivot)
        inverse[k][k] = root
        for i in range(k + 1, size):
            entry[i][k] = entry[i][k] * root
        for i in range(k + 1, size):
            for m in range(k + 1, i + 1):
                entry[i][m] = entry[i][m] - entry[i][k] * entry[m][k]
    for k in range(size):
        for i in range(k + 1, size):
            total = entry[i][k] * inverse[k][k]
            for m in range(k + 1, i):
                total = total + entry[i][m] * inverse[m][k]
            inverse[i][k] = -total * inverse[i][i]
    return inverse


def factor(gram, inverse_ref):
    size, tile = gram.shape[0], BLOCK
    count = size // tile
    left = [gram[i * tile:(i + 1) * tile, :] for i in range(count)]
    lane = lax.broadcasted_iota(jnp.int32, (tile, size), 1)
    sublane = lax.broadcasted_iota(jnp.int32, (tile, size), 0)
    right = [jnp.where(lane == sublane + i * tile, 1.0, 0.0) for i in range(count)]

    def spread(value, row, column):
        return jnp.broadcast_to(value[row:row + 1, column:column + 1], (tile, size))

    for j in range(count):
        corner = [[spread(left[j], i, j * tile + k) for k in range(i + 1)] for i in range(tile)]
        small = small_inverse(corner)
        columns = []
        for k in range(tile):
            column = jnp.where(sublane == k, small[k][k], 0.0)
            for i in range(k + 1, tile):
                column = jnp.where(sublane == i, small[i][k], column)
            columns.append(column)
        done_left = sum(columns[k] * left[j][k:k + 1, :] for k in range(tile))
        done_right = sum(columns[k] * right[j][k:k + 1, :] for k in range(tile))
        inverse_ref[pl.ds(j * tile, tile), :] = done_right
        if j + 1 < count:
            turned = done_left.T
            for i in range(j + 1, count):
                for k in range(tile):
                    factor = jnp.broadcast_to(turned[i * tile:(i + 1) * tile, k:k + 1], (tile, size))
                    left[i] = left[i] - factor * done_left[k:k + 1, :]
                    right[i] = right[i] - factor * done_right[k:k + 1, :]


def first_kernel(scale, band, rank_ref, bridge_ref, raw_ref, weight_ref, solve_ref, inverse_ref):
    local_rows = weight_ref.shape[0] - band
    factor(exact(bridge_ref[...], raw_ref[...], TN), inverse_ref)
    inverse = inverse_ref[...]
    start = pl.multiple_of(rank_ref[0] * local_rows, local_rows)
    own = exact(raw_ref[pl.ds(start, local_rows), :], inverse, NT)
    weight_ref[:local_rows, :] = exact(own, inverse, NN)
    weight_ref[local_rows:, :] = inverse_ref[pl.ds(pl.multiple_of(rank_ref[0] * band, band), band), :]
    solve_ref[...] = scale * exact(bridge_ref[...], inverse, NT)


def first_factor(rank_index, bridge, raw, scale, local_rows, band):
    columns = raw.shape[1]
    whole = pl.BlockSpec(memory_space=pltpu.VMEM)
    return call(
        functools.partial(first_kernel, scale, band),
        8 * raw.size * columns,
        16 * raw.size,
        in_specs=[pl.BlockSpec(memory_space=pltpu.SMEM), whole, whole],
        out_specs=[whole, whole],
        out_shape=[shape(local_rows + band, columns), shape(*raw.shape)],
        scratch_shapes=[pltpu.VMEM((columns, columns), jnp.float32)],
    )(rank_index, bridge, raw)


def last_kernel(scale, gram_ref, middle_ref, inverse_ref, out_ref):
    factor(gram_ref[...], inverse_ref)
    out_ref[...] = exact(middle_ref[...], scale * inverse_ref[...], NT)


def last_factor(gram, middle, scale):
    columns = gram.shape[0]
    whole = pl.BlockSpec(memory_space=pltpu.VMEM)
    return call(
        functools.partial(last_kernel, scale),
        8 * middle.size * columns,
        8 * middle.size,
        in_specs=[whole, whole],
        out_specs=[whole, whole],
        out_shape=[shape(columns, columns), shape(*middle.shape)],
    )(gram, middle)


def swap(value, axis, offset):
    return lax.ppermute(value, axis, [(i, i ^ offset) for i in range(lax.axis_size(axis))])


def exchange(value, axes):
    return lax.all_to_all(value, axes, 0, 0, tiled=True)


def gather_all(value, axes):
    parts = lax.axis_size(axes)
    return exchange(jnp.broadcast_to(value[None], (parts,) + value.shape), axes)


def after(value, others):
    return lax.optimization_barrier((value, others))


def on_device(core_one, core_two, right_sketch, sketch_core):
    local_rows, slices, width = core_one.shape
    columns = right_sketch.shape[1]
    ranks, cuts = lax.axis_size("rank"), lax.axis_size("cuts")
    rank = lax.axis_index("rank")
    rank_index = rank.astype(jnp.int32).reshape(1)
    both = ("cuts", "rank")
    parts = ranks * cuts
    band = columns // ranks
    share = -(-slices // ranks)
    room = share * ranks
    halves = [share // 2, share - share // 2]
    filler = ((0, 0), (0, room - slices), (0, 0))
    core_two, sketch_core = jnp.pad(core_two, filler), jnp.pad(sketch_core, filler)
    flat_one = core_one.reshape(local_rows * slices, width)
    flat_two = core_two.reshape(local_rows * room, width)

    sketched, part = sketch(core_two, right_sketch, sketch_core)

    def send(names, source, behind):
        found = []
        for half, offset in names:
            start = (rank ^ offset) * share + half * halves[0]
            found.append(lax.dynamic_slice_in_dim(source, start, halves[half], 0))
        if behind is not None:
            found, _ = after(found, behind)
        return {name: swap(value, "rank", name[1]) if name[1] else value for name, value in zip(names, found)}

    far = ranks - 1
    near = [[(half, offset) for offset in range(1, far)] for half in range(2)]

    cut_bits = [1 << bit for bit in range((cuts - 1).bit_length())]
    bits = [1 << bit for bit in range((ranks - 1).bit_length())]
    first = send(near[0], sketched, None)
    bridge_rows = jnp.sum(exchange(part.reshape(cuts, local_rows // cuts, columns), "cuts"), axis=0)
    flat_late, (bridge_rows, pieces) = after(flat_one, (bridge_rows, first))
    sketched, bridge_rows = after(sketched, bridge_rows)
    moved = send(near[1] + [(0, far)], sketched, None)
    bridge = gather_all(bridge_rows, ("rank", "cuts")).reshape(width, columns)
    square = square_of(flat_late)

    raw = product_of(square, bridge)
    raw, moved = after(raw, moved)
    pieces.update(moved)
    sketched, raw = after(sketched, raw)
    pieces.update(send([(0, 0), (1, 0)], sketched, None))
    raw = jnp.sum(exchange(raw.reshape(parts, -1, columns), both), axis=0)
    pieces.update(send([(1, far)], sketched, raw))
    raw = gather_all(raw, both).reshape(width, columns)

    ordered = [pieces[(half, offset)] for half in range(2) for offset in range(ranks)]
    loose = loosen(rank_index, raw, ordered, halves)
    loose, (bridge, raw) = after(loose, (bridge, raw))
    scale = math.sqrt(local_rows * ranks * slices * cuts)
    weight, solve = first_factor(rank_index, bridge, raw, scale, local_rows, band)
    everyone = []
    for half, order in enumerate((bits, bits[::-1])):
        found = {0: loose[half]}
        for bit in order:
            moved = {bit: swap(found[0], "rank", bit)}
            if len(found) > 1:
                late, weight = after({offset: found[offset] for offset in found if offset}, weight)
                moved.update({offset ^ bit: swap(held, "rank", bit) for offset, held in late.items()})
            found.update(moved)
        everyone += [found[offset] for offset in range(ranks)]

    left_core = apply_to(flat_one, solve).reshape(local_rows, slices, columns)
    weight, left_core = after(weight, left_core)
    raw, gram, middle = carry_rows(rank_index, weight, flat_two, everyone, halves, share, band)
    raw = jnp.sum(exchange(raw.reshape(parts, -1, columns), both), axis=0)
    for axis, bit in [("cuts", 1)] + [("rank", bit) for bit in bits] + [("cuts", bit) for bit in cut_bits[1:]]:
        gram = gram + swap(gram, axis, bit)
    raw, gram = after(raw, gram)
    raw = gather_all(raw, both).reshape(width, columns)
    scale = math.sqrt(columns * slices * cuts)
    inverse, middle = last_factor(gram, middle, scale)
    carry = exact(inverse, raw, NT)
    middle_core = middle.reshape(band, room, columns)[:, :slices]
    return (left_core, middle_core, carry)


def solution(mesh):
    placed = (P("rank", "cuts", None), P("rank", "cuts", None), P(), P(None, "cuts", None))
    return jax.shard_map(
        on_device,
        mesh=mesh,
        in_specs=placed,
        out_specs=(P("rank", "cuts", None), P("rank", "cuts", None), P()),
        check_vma=False,
    )
```

```python
import functools
import math

import jax
import jax.numpy as jnp
from jax import lax
from jax.experimental import pallas as pl
from jax.experimental.pallas import tpu as pltpu
from jax.sharding import PartitionSpec as P

NT = (((1,), (1,)), ((), ()))
NN = (((1,), (0,)), ((), ()))
TN = (((0,), (0,)), ((), ()))
VMEM_LIMIT = 56 * 1024 * 1024
BLOCK = 8


PARTS = 4


def tiles(block, width):
    size = block // PARTS
    return [pl.BlockSpec((size, width), lambda i, q=q: (i * PARTS + q, 0)) for q in range(PARTS)]


def joined_rows(refs):
    return jnp.concatenate([ref[...] for ref in refs], axis=0)


def call(kernel, flops, size, **more):
    return pl.pallas_call(
        kernel,
        compiler_params=pltpu.CompilerParams(vmem_limit_bytes=VMEM_LIMIT),
        cost_estimate=pl.CostEstimate(flops=flops, bytes_accessed=size, transcendentals=0),
        **more,
    )


def shape(*extent):
    return jax.ShapeDtypeStruct(extent, jnp.float32)


def split(value):
    high = value.astype(jnp.bfloat16)
    return high, (value - high.astype(jnp.float32)).astype(jnp.bfloat16)


def mxu(a, b, form):
    return lax.dot_general(a, b, form, preferred_element_type=jnp.float32)


def exact(a, b, form):
    return lax.dot_general(a, b, form, precision=lax.Precision.HIGHEST, preferred_element_type=jnp.float32)


def both_parts(value, axis):
    return jnp.concatenate(split(value), axis=axis)


def twice(value, axis):
    return jnp.concatenate([value, value], axis=axis)


def fold(value, axis):
    half = value.shape[axis] // 2
    return lax.slice_in_dim(value, 0, half, axis=axis) + lax.slice_in_dim(value, half, 2 * half, axis=axis)


def rows_of(ref):
    return ref.reshape(ref.shape[0] * ref.shape[1], ref.shape[2])


def sketch_kernel(*refs):
    core_refs, (right_ref, left_ref, sketched_ref, part_ref, rows_ref) = refs[:PARTS], refs[PARTS:]
    block = left_ref.shape[1]
    local_rows = rows_ref.shape[0] // block
    columns = right_ref.shape[1]
    right = twice(both_parts(right_ref[...], 1), 0)
    rows_ref[...] = fold(mxu(both_parts(jnp.concatenate([rows_of(ref)[...] for ref in core_refs], axis=0), 1), right, NN), 1)
    left_rows = rows_of(left_ref)

    @pl.when(pl.program_id(0) == 0)
    def _():
        part_ref[...] = jnp.zeros_like(part_ref)

    sides, lefts = [], []
    for n in range(block):
        rows = rows_ref[pl.ds(n, local_rows, stride=block), :]
        sketched_ref[n] = rows
        sides.append(rows)
        lefts.append(left_rows[pl.ds(n, columns, stride=block), :])
    side = both_parts(jnp.concatenate(sides, axis=1), 1)
    left = twice(both_parts(jnp.concatenate(lefts, axis=1), 0), 1)
    part_ref[...] += fold(mxu(side, left, NT), 1)


def sketch(core_two, right_sketch, sketch_core):
    local_rows, slices, width = core_two.shape
    columns = right_sketch.shape[1]
    return call(
        sketch_kernel,
        2 * core_two.size * columns * 4,
        4 * (core_two.size + 2 * sketch_core.size),
        grid=(slices // BLOCK,),
        in_specs=[
            *[pl.BlockSpec((local_rows // PARTS, BLOCK, width), lambda i, q=q: (q, i, 0)) for q in range(PARTS)],
            pl.BlockSpec((width, columns), lambda i: (0, 0)),
            pl.BlockSpec((columns, BLOCK, columns), lambda i: (0, i, 0)),
        ],
        out_specs=[
            pl.BlockSpec((BLOCK, local_rows, columns), lambda i: (i, 0, 0)),
            pl.BlockSpec((local_rows, columns), lambda i: (0, 0)),
        ],
        out_shape=[shape(slices, local_rows, columns), shape(local_rows, columns)],
        scratch_shapes=[pltpu.VMEM((local_rows * BLOCK, columns), jnp.float32)],
    )(*[core_two] * PARTS, right_sketch, sketch_core)


def block_of(rows):
    block = 1024
    while rows % block:
        block //= 2
    return block


def square_kernel(core_ref, square_ref, sum_ref):
    step = pl.program_id(0)
    width = core_ref.shape[1]
    high, low = split(core_ref[...])

    @pl.when(step == 0)
    def _():
        sum_ref[...] = jnp.zeros_like(sum_ref)

    sum_ref[...] += mxu(high, jnp.concatenate([high, low], axis=1), TN)

    @pl.when(step == pl.num_programs(0) - 1)
    def _():
        cross = sum_ref[:, width:]
        square_ref[...] = both_parts(sum_ref[:, :width] + cross + cross.T, 1)


def square_of(flat_one):
    rows, width = flat_one.shape
    block = block_of(rows)
    return call(
        square_kernel,
        4 * rows * width * width,
        4 * flat_one.size,
        grid=(rows // block,),
        in_specs=[pl.BlockSpec((block, width), lambda i: (i, 0))],
        out_specs=pl.BlockSpec((width, 2 * width), lambda i: (0, 0)),
        out_shape=jax.ShapeDtypeStruct((width, 2 * width), jnp.bfloat16),
        scratch_shapes=[pltpu.VMEM((width, 2 * width), jnp.float32)],
    )(flat_one)


def product_kernel(square_ref, bridge_ref, out_ref):
    bridge = twice(both_parts(bridge_ref[...], 1), 0)
    out_ref[...] = fold(mxu(square_ref[...], bridge, NN), 1)


def product_of(square, bridge):
    return call(
        product_kernel,
        4 * square.size * bridge.shape[1],
        2 * square.size + 8 * bridge.size,
        out_shape=shape(*bridge.shape),
    )(square, bridge)


def loose_kernel(rank_ref, raw_ref, *refs):
    piece_refs, out_refs = refs[:-2], refs[-2:]
    local_rows, columns = piece_refs[0].shape[1:]
    rows = []
    for offset in range(len(piece_refs)):
        start = pl.multiple_of((rank_ref[0] ^ offset) * local_rows, local_rows)
        rows.append(raw_ref[pl.ds(start, local_rows), :])
    raw = twice(both_parts(jnp.concatenate(rows, axis=0), 1).T, 1)
    first = 0
    for out_ref in out_refs:
        count = out_ref.shape[0]
        value = [jnp.concatenate([ref[first + n] for n in range(count)], axis=1) for ref in piece_refs]
        product = fold(mxu(raw, both_parts(jnp.concatenate(value, axis=0), 0), NN), 0)
        for n in range(count):
            out_ref[n] = product[:, n * columns:(n + 1) * columns]
        first += count


def loosen(rank_index, raw, pieces, halves):
    columns = raw.shape[1]
    size = sum(piece.size for piece in pieces)
    whole = pl.BlockSpec(memory_space=pltpu.VMEM)
    return call(
        loose_kernel,
        8 * size * columns,
        4 * raw.size + 4 * size,
        in_specs=[pl.BlockSpec(memory_space=pltpu.SMEM)] + [whole] * (len(pieces) + 1),
        out_specs=[whole] * 2,
        out_shape=[shape(count, columns, columns) for count in halves],
    )(rank_index, raw, *pieces)


def carry_kernel(halves, share, rank_ref, weight_ref, *refs):
    core_refs, piece_refs = refs[:PARTS], refs[PARTS:-5]
    raw_ref, gram_ref, middle_ref, rows_ref, sum_ref = refs[-5:]
    step = pl.program_id(0)
    block, width = core_refs[0].shape[0] * PARTS, core_refs[0].shape[1]
    columns = weight_ref.shape[1]
    ranks = len(piece_refs) // len(halves)
    room = share * ranks
    local_rows = rows_ref.shape[0] // room
    band = middle_ref.shape[0] // room

    @pl.when(step == 0)
    def _():
        sum_ref[...] = jnp.zeros_like(sum_ref)
        weight = twice(both_parts(weight_ref[...], 0), 1)
        for half, count in enumerate(halves):
            for offset in range(ranks):
                ref = piece_refs[half * ranks + offset]
                first = (rank_ref[0] ^ offset) * share + sum(halves[:half])
                value = both_parts(jnp.concatenate([ref[n] for n in range(count)], axis=1), 0)
                spread = fold(mxu(weight, value, NN), 0)
                for n in range(count):
                    piece = lax.slice_in_dim(spread, n * columns, (n + 1) * columns, axis=1)
                    rows_ref[pl.ds(first + n, local_rows, stride=room), :] = piece[:local_rows]
                    middle_ref[pl.ds(first + n, band, stride=room), :] = piece[local_rows:]

    rows = both_parts(rows_ref[pl.ds(pl.multiple_of(step * block, block), block), :], 1).T
    product = fold(mxu(twice(rows, 1), both_parts(joined_rows(core_refs), 0), NN), 0)
    sum_ref[...] += product

    @pl.when(step == pl.num_programs(0) - 1)
    def _():
        raw_ref[...] = sum_ref[...].T
        middle = both_parts(middle_ref[...], 1)
        gram_ref[...] = fold(fold(mxu(middle, middle, TN), 0), 1)


def carry_rows(rank_index, weight, flat_two, pieces, halves, share, band):
    rows, width = flat_two.shape
    columns = weight.shape[1]
    block = block_of(rows)
    ranks = len(pieces) // len(halves)
    whole = pl.BlockSpec(memory_space=pltpu.VMEM)
    return call(
        functools.partial(carry_kernel, halves, share),
        8 * flat_two.size * columns,
        4 * flat_two.size + 4 * sum(piece.size for piece in pieces),
        grid=(rows // block,),
        in_specs=[
            pl.BlockSpec(memory_space=pltpu.SMEM),
            pl.BlockSpec((weight.shape[0], columns), lambda i: (0, 0)),
            *tiles(block, width),
        ]
        + [pl.BlockSpec(piece.shape, lambda i: (0, 0, 0)) for piece in pieces],
        out_specs=[
            pl.BlockSpec((width, columns), lambda i: (0, 0)),
            pl.BlockSpec((columns, columns), lambda i: (0, 0)),
            pl.BlockSpec((band * share * ranks, columns), lambda i: (0, 0)),
        ],
        out_shape=[shape(width, columns), shape(columns, columns), shape(band * share * ranks, columns)],
        scratch_shapes=[pltpu.VMEM((rows, columns), jnp.float32), pltpu.VMEM((columns, width), jnp.float32)],
    )(rank_index, weight, *[flat_two] * PARTS, *pieces)


def apply_kernel(rows_ref, weight_ref, out_ref):
    weight = twice(both_parts(weight_ref[...], 1), 0)
    out_ref[...] = fold(mxu(both_parts(rows_ref[...], 1), weight, NN), 1)


def apply_to(rows, weight):
    count, width = rows.shape
    columns = weight.shape[1]
    block = block_of(count)
    return call(
        apply_kernel,
        8 * rows.size * columns,
        4 * (rows.size + count * columns),
        grid=(count // block,),
        in_specs=[
            pl.BlockSpec((block, width), lambda i: (i, 0)),
            pl.BlockSpec((width, columns), lambda i: (0, 0)),
        ],
        out_specs=pl.BlockSpec((block, columns), lambda i: (i, 0)),
        out_shape=shape(count, columns),
    )(rows, weight)


def small_inverse(entry):
    size = len(entry)
    entry = [list(row) for row in entry]
    inverse = [[None] * size for _ in range(size)]
    for k in range(size):
        pivot = entry[k][k]
        root = lax.rsqrt(pivot)
        inverse[k][k] = root
        for i in range(k + 1, size):
            entry[i][k] = entry[i][k] * root
        for i in range(k + 1, size):
            for m in range(k + 1, i + 1):
                entry[i][m] = entry[i][m] - entry[i][k] * entry[m][k]
    for k in range(size):
        for i in range(k + 1, size):
            total = entry[i][k] * inverse[k][k]
            for m in range(k + 1, i):
                total = total + entry[i][m] * inverse[m][k]
            inverse[i][k] = -total * inverse[i][i]
    return inverse


def factor(gram, inverse_ref):
    size, tile = gram.shape[0], BLOCK
    count = size // tile
    left = [gram[i * tile:(i + 1) * tile, :] for i in range(count)]
    lane = lax.broadcasted_iota(jnp.int32, (tile, size), 1)
    sublane = lax.broadcasted_iota(jnp.int32, (tile, size), 0)
    right = [jnp.where(lane == sublane + i * tile, 1.0, 0.0) for i in range(count)]

    def spread(value, row, column):
        return jnp.broadcast_to(value[row:row + 1, column:column + 1], (tile, size))

    for j in range(count):
        corner = [[spread(left[j], i, j * tile + k) for k in range(i + 1)] for i in range(tile)]
        small = small_inverse(corner)
        columns = []
        for k in range(tile):
            column = jnp.where(sublane == k, small[k][k], 0.0)
            for i in range(k + 1, tile):
                column = jnp.where(sublane == i, small[i][k], column)
            columns.append(column)
        done_left = sum(columns[k] * left[j][k:k + 1, :] for k in range(tile))
        done_right = sum(columns[k] * right[j][k:k + 1, :] for k in range(tile))
        inverse_ref[pl.ds(j * tile, tile), :] = done_right
        if j + 1 < count:
            turned = done_left.T
            for i in range(j + 1, count):
                for k in range(tile):
                    factor = jnp.broadcast_to(turned[i * tile:(i + 1) * tile, k:k + 1], (tile, size))
                    left[i] = left[i] - factor * done_left[k:k + 1, :]
                    right[i] = right[i] - factor * done_right[k:k + 1, :]


def first_kernel(scale, band, rank_ref, bridge_ref, raw_ref, weight_ref, solve_ref, inverse_ref):
    local_rows = weight_ref.shape[0] - band
    factor(exact(bridge_ref[...], raw_ref[...], TN), inverse_ref)
    inverse = inverse_ref[...]
    start = pl.multiple_of(rank_ref[0] * local_rows, local_rows)
    own = exact(raw_ref[pl.ds(start, local_rows), :], inverse, NT)
    weight_ref[:local_rows, :] = exact(own, inverse, NN)
    weight_ref[local_rows:, :] = inverse_ref[pl.ds(pl.multiple_of(rank_ref[0] * band, band), band), :]
    solve_ref[...] = scale * exact(bridge_ref[...], inverse, NT)


def first_factor(rank_index, bridge, raw, scale, local_rows, band):
    columns = raw.shape[1]
    whole = pl.BlockSpec(memory_space=pltpu.VMEM)
    return call(
        functools.partial(first_kernel, scale, band),
        8 * raw.size * columns,
        16 * raw.size,
        in_specs=[pl.BlockSpec(memory_space=pltpu.SMEM), whole, whole],
        out_specs=[whole, whole],
        out_shape=[shape(local_rows + band, columns), shape(*raw.shape)],
        scratch_shapes=[pltpu.VMEM((columns, columns), jnp.float32)],
    )(rank_index, bridge, raw)


def last_kernel(scale, gram_ref, middle_ref, inverse_ref, out_ref):
    factor(gram_ref[...], inverse_ref)
    out_ref[...] = exact(middle_ref[...], scale * inverse_ref[...], NT)


def last_factor(gram, middle, scale):
    columns = gram.shape[0]
    whole = pl.BlockSpec(memory_space=pltpu.VMEM)
    return call(
        functools.partial(last_kernel, scale),
        8 * middle.size * columns,
        8 * middle.size,
        in_specs=[whole, whole],
        out_specs=[whole, whole],
        out_shape=[shape(columns, columns), shape(*middle.shape)],
    )(gram, middle)


def swap(value, axis, offset):
    return lax.ppermute(value, axis, [(i, i ^ offset) for i in range(lax.axis_size(axis))])


def exchange(value, axes):
    return lax.all_to_all(value, axes, 0, 0, tiled=True)


def gather_all(value, axes):
    parts = lax.axis_size(axes)
    return exchange(jnp.broadcast_to(value[None], (parts,) + value.shape), axes)


def pairs_of(axis, bits):
    return [(axis, bits[start:start + 2]) for start in range(0, len(bits), 2)]


def after(value, others):
    return lax.optimization_barrier((value, others))


def on_device(core_one, core_two, right_sketch, sketch_core):
    local_rows, slices, width = core_one.shape
    columns = right_sketch.shape[1]
    ranks, cuts = lax.axis_size("rank"), lax.axis_size("cuts")
    rank = lax.axis_index("rank")
    rank_index = rank.astype(jnp.int32).reshape(1)
    both = ("cuts", "rank")
    parts = ranks * cuts
    band = columns // ranks
    share = -(-slices // ranks)
    room = share * ranks
    halves = [share // 2, share - share // 2]
    filler = ((0, 0), (0, room - slices), (0, 0))
    core_two, sketch_core = jnp.pad(core_two, filler), jnp.pad(sketch_core, filler)
    flat_one = core_one.reshape(local_rows * slices, width)
    flat_two = core_two.reshape(local_rows * room, width)

    sketched, part = sketch(core_two, right_sketch, sketch_core)

    def part_for(offset, source):
        return lax.dynamic_slice_in_dim(source, (rank ^ offset) * share, share, 0)

    cut_bits = [1 << bit for bit in range((cuts - 1).bit_length())]
    bits = [1 << bit for bit in range((ranks - 1).bit_length())]
    bridge_rows = jnp.sum(exchange(part.reshape(cuts, local_rows // cuts, columns), "cuts"), axis=0)
    flat_late, bridge_rows = after(flat_one, bridge_rows)
    sketched, bridge_rows = after(sketched, bridge_rows)
    moved = [swap(part_for(offset, sketched), "rank", offset) for offset in range(1, ranks)]
    bridge = gather_all(bridge_rows, ("rank", "cuts")).reshape(width, columns)
    square = square_of(flat_late)

    raw = product_of(square, bridge)
    sketched, raw = after(sketched, raw)
    own = part_for(0, sketched)
    raw = jnp.sum(exchange(raw.reshape(parts, -1, columns), both), axis=0)
    raw, moved = after(raw, moved)
    raw = gather_all(raw, both).reshape(width, columns)

    loose = loosen(rank_index, raw, [own] + moved, halves)
    loose, (bridge, raw) = after(loose, (bridge, raw))
    scale = math.sqrt(local_rows * ranks * slices * cuts)
    weight, solve = first_factor(rank_index, bridge, raw, scale, local_rows, band)
    everyone = []
    for half, order in enumerate((bits, bits[::-1])):
        found = {0: loose[half]}
        for bit in order:
            moved = {bit: swap(found[0], "rank", bit)}
            if len(found) > 1:
                late, weight = after({offset: found[offset] for offset in found if offset}, weight)
                moved.update({offset ^ bit: swap(held, "rank", bit) for offset, held in late.items()})
            found.update(moved)
        everyone += [found[offset] for offset in range(ranks)]

    left_core = apply_to(flat_one, solve).reshape(local_rows, slices, columns)
    weight, left_core = after(weight, left_core)
    raw, gram, middle = carry_rows(rank_index, weight, flat_two, everyone, halves, share, band)
    raw = jnp.sum(exchange(raw.reshape(parts, -1, columns), both), axis=0)
    for axis, pair in [("cuts", [1])] + pairs_of("rank", bits) + pairs_of("cuts", cut_bits[1:]):
        other = gram + swap(gram, axis, pair[0])
        if len(pair) > 1:
            other = other + (swap(gram, axis, pair[1]) + swap(gram, axis, pair[0] ^ pair[1]))
        gram = other
    raw, gram = after(raw, gram)
    raw = gather_all(raw, both).reshape(width, columns)
    scale = math.sqrt(columns * slices * cuts)
    inverse, middle = last_factor(gram, middle, scale)
    carry = exact(inverse, raw, NT)
    middle_core = middle.reshape(band, room, columns)[:, :slices]
    return (left_core, middle_core, carry)


def solution(mesh):
    placed = (P("rank", "cuts", None), P("rank", "cuts", None), P(), P(None, "cuts", None))
    return jax.shard_map(
        on_device,
        mesh=mesh,
        in_specs=placed,
        out_specs=(P("rank", "cuts", None), P("rank", "cuts", None), P()),
        check_vma=False,
    )
```

```python
import functools
import math

import jax
import jax.numpy as jnp
from jax import lax
from jax.experimental import pallas as pl
from jax.experimental.pallas import tpu as pltpu
from jax.sharding import PartitionSpec as P

NT = (((1,), (1,)), ((), ()))
NN = (((1,), (0,)), ((), ()))
TN = (((0,), (0,)), ((), ()))
VMEM_LIMIT = 56 * 1024 * 1024
BLOCK = 8


PARTS = 4


def tiles(block, width):
    size = block // PARTS
    return [pl.BlockSpec((size, width), lambda i, q=q: (i * PARTS + q, 0)) for q in range(PARTS)]


def joined_rows(refs):
    return jnp.concatenate([ref[...] for ref in refs], axis=0)


def call(kernel, flops, size, **more):
    return pl.pallas_call(
        kernel,
        compiler_params=pltpu.CompilerParams(vmem_limit_bytes=VMEM_LIMIT),
        cost_estimate=pl.CostEstimate(flops=flops, bytes_accessed=size, transcendentals=0),
        **more,
    )


def shape(*extent):
    return jax.ShapeDtypeStruct(extent, jnp.float32)


def split(value):
    high = value.astype(jnp.bfloat16)
    return high, (value - high.astype(jnp.float32)).astype(jnp.bfloat16)


def mxu(a, b, form):
    return lax.dot_general(a, b, form, preferred_element_type=jnp.float32)


def exact(a, b, form):
    return lax.dot_general(a, b, form, precision=lax.Precision.HIGHEST, preferred_element_type=jnp.float32)


def both_parts(value, axis):
    return jnp.concatenate(split(value), axis=axis)


def twice(value, axis):
    return jnp.concatenate([value, value], axis=axis)


def fold(value, axis):
    half = value.shape[axis] // 2
    return lax.slice_in_dim(value, 0, half, axis=axis) + lax.slice_in_dim(value, half, 2 * half, axis=axis)


def rows_of(ref):
    return ref.reshape(ref.shape[0] * ref.shape[1], ref.shape[2])


def sketch_kernel(*refs):
    core_refs, (right_ref, left_ref, sketched_ref, part_ref, rows_ref) = refs[:PARTS], refs[PARTS:]
    block = left_ref.shape[1]
    local_rows = rows_ref.shape[0] // block
    columns = right_ref.shape[1]
    right = both_parts(right_ref[...], 1)
    core = jnp.concatenate([rows_of(ref)[...] for ref in core_refs], axis=0)
    rows_ref[...] = fold(fold(mxu(both_parts(core, 0), right, NN), 0), 1)
    left_rows = rows_of(left_ref)

    @pl.when(pl.program_id(0) == 0)
    def _():
        part_ref[...] = jnp.zeros_like(part_ref)

    sides, lefts = [], []
    for n in range(block):
        rows = rows_ref[pl.ds(n, local_rows, stride=block), :]
        sketched_ref[n] = rows
        sides.append(rows)
        lefts.append(left_rows[pl.ds(n, columns, stride=block), :])
    side = both_parts(jnp.concatenate(sides, axis=1), 0)
    left = both_parts(jnp.concatenate(lefts, axis=1), 0)
    part = fold(fold(mxu(side, left, NT), 0), 1)
    part_ref[...] += part


def sketch(core_two, right_sketch, sketch_core):
    local_rows, slices, width = core_two.shape
    columns = right_sketch.shape[1]
    return call(
        sketch_kernel,
        2 * core_two.size * columns * 4,
        4 * (core_two.size + 2 * sketch_core.size),
        grid=(slices // BLOCK,),
        in_specs=[
            *[pl.BlockSpec((local_rows // PARTS, BLOCK, width), lambda i, q=q: (q, i, 0)) for q in range(PARTS)],
            pl.BlockSpec((width, columns), lambda i: (0, 0)),
            pl.BlockSpec((columns, BLOCK, columns), lambda i: (0, i, 0)),
        ],
        out_specs=[
            pl.BlockSpec((BLOCK, local_rows, columns), lambda i: (i, 0, 0)),
            pl.BlockSpec((local_rows, columns), lambda i: (0, 0)),
        ],
        out_shape=[shape(slices, local_rows, columns), shape(local_rows, columns)],
        scratch_shapes=[pltpu.VMEM((local_rows * BLOCK, columns), jnp.float32)],
    )(*[core_two] * PARTS, right_sketch, sketch_core)


def block_of(rows):
    block = 1024
    while rows % block:
        block //= 2
    return block


def square_kernel(last, core_ref, *refs):
    step = pl.program_id(0)
    before_refs, out_ref, sum_ref = refs[:-2], refs[-2], refs[-1]
    width = core_ref.shape[1]
    high, low = split(core_ref[...])

    @pl.when(step == 0)
    def _():
        sum_ref[...] = before_refs[0][...] if before_refs else jnp.zeros_like(sum_ref)

    sum_ref[...] += mxu(high, jnp.concatenate([high, low], axis=1), TN)

    @pl.when(step == pl.num_programs(0) - 1)
    def _():
        if last:
            cross = sum_ref[:, width:]
            out_ref[...] = both_parts(sum_ref[:, :width] + cross + cross.T, 1)
        else:
            out_ref[...] = sum_ref[...]


def square_of(flat_one, first, count, before, last):
    rows, width = flat_one.shape
    block = block_of(rows)
    whole = pl.BlockSpec((width, 2 * width), lambda i: (0, 0))
    return call(
        functools.partial(square_kernel, last),
        4 * count * block * width * width,
        4 * count * block * width,
        grid=(count,),
        in_specs=[pl.BlockSpec((block, width), lambda i: (i + first, 0))] + [whole] * len(before),
        out_specs=whole,
        out_shape=jax.ShapeDtypeStruct((width, 2 * width), jnp.bfloat16 if last else jnp.float32),
        scratch_shapes=[pltpu.VMEM((width, 2 * width), jnp.float32)],
    )(flat_one, *before)


def product_kernel(square_ref, bridge_ref, out_ref):
    bridge = twice(both_parts(bridge_ref[...], 1), 0)
    out_ref[...] = fold(mxu(square_ref[...], bridge, NN), 1)


def product_of(square, bridge):
    return call(
        product_kernel,
        4 * square.size * bridge.shape[1],
        2 * square.size + 8 * bridge.size,
        out_shape=shape(*bridge.shape),
    )(square, bridge)


def loose_kernel(plan, rank_ref, raw_ref, *refs):
    piece_refs, out_refs = refs[:-2], refs[-2:]
    ranks = len(plan[0])
    local_rows, columns = piece_refs[0].shape[1:]
    rows = []
    for offset in range(ranks):
        start = pl.multiple_of((rank_ref[0] ^ offset) * local_rows, local_rows)
        rows.append(raw_ref[pl.ds(start, local_rows), :])
    raw = twice(both_parts(jnp.concatenate(rows, axis=0), 1).T, 1)
    for places, out_ref in zip(plan, out_refs):
        count = out_ref.shape[0]
        value = [jnp.concatenate([piece_refs[ref][first + n] for n in range(count)], axis=1) for ref, first in places]
        product = fold(mxu(raw, both_parts(jnp.concatenate(value, axis=0), 0), NN), 0)
        for n in range(count):
            out_ref[n] = product[:, n * columns:(n + 1) * columns]


def loosen(rank_index, raw, pieces, plan, halves):
    columns = raw.shape[1]
    size = sum(piece.size for piece in pieces)
    whole = pl.BlockSpec(memory_space=pltpu.VMEM)
    return call(
        functools.partial(loose_kernel, plan),
        8 * size * columns,
        4 * raw.size + 4 * size,
        in_specs=[pl.BlockSpec(memory_space=pltpu.SMEM)] + [whole] * (len(pieces) + 1),
        out_specs=[whole] * 2,
        out_shape=[shape(count, columns, columns) for count in halves],
    )(rank_index, raw, *pieces)


def carry_kernel(halves, share, rank_ref, weight_ref, *refs):
    core_refs, piece_refs = refs[:PARTS], refs[PARTS:-5]
    raw_ref, gram_ref, middle_ref, rows_ref, sum_ref = refs[-5:]
    step = pl.program_id(0)
    block, width = core_refs[0].shape[0] * PARTS, core_refs[0].shape[1]
    columns = weight_ref.shape[1]
    ranks = len(piece_refs) // len(halves)
    room = share * ranks
    local_rows = rows_ref.shape[0] // room
    band = middle_ref.shape[0] // room

    @pl.when(step == 0)
    def _():
        sum_ref[...] = jnp.zeros_like(sum_ref)
        weight = twice(both_parts(weight_ref[...], 0), 1)
        for half, count in enumerate(halves):
            for offset in range(ranks):
                ref = piece_refs[half * ranks + offset]
                first = (rank_ref[0] ^ offset) * share + sum(halves[:half])
                value = both_parts(jnp.concatenate([ref[n] for n in range(count)], axis=1), 0)
                spread = fold(mxu(weight, value, NN), 0)
                for n in range(count):
                    piece = lax.slice_in_dim(spread, n * columns, (n + 1) * columns, axis=1)
                    rows_ref[pl.ds(first + n, local_rows, stride=room), :] = piece[:local_rows]
                    middle_ref[pl.ds(first + n, band, stride=room), :] = piece[local_rows:]

    rows = both_parts(rows_ref[pl.ds(pl.multiple_of(step * block, block), block), :], 1).T
    product = fold(mxu(twice(rows, 1), both_parts(joined_rows(core_refs), 0), NN), 0)
    sum_ref[...] += product

    @pl.when(step == pl.num_programs(0) - 1)
    def _():
        raw_ref[...] = sum_ref[...].T
        middle = both_parts(middle_ref[...], 1)
        gram_ref[...] = fold(fold(mxu(middle, middle, TN), 0), 1)


def carry_rows(rank_index, weight, flat_two, pieces, halves, share, band):
    rows, width = flat_two.shape
    columns = weight.shape[1]
    block = block_of(rows)
    ranks = len(pieces) // len(halves)
    whole = pl.BlockSpec(memory_space=pltpu.VMEM)
    return call(
        functools.partial(carry_kernel, halves, share),
        8 * flat_two.size * columns,
        4 * flat_two.size + 4 * sum(piece.size for piece in pieces),
        grid=(rows // block,),
        in_specs=[
            pl.BlockSpec(memory_space=pltpu.SMEM),
            pl.BlockSpec((weight.shape[0], columns), lambda i: (0, 0)),
            *tiles(block, width),
        ]
        + [pl.BlockSpec(piece.shape, lambda i: (0, 0, 0)) for piece in pieces],
        out_specs=[
            pl.BlockSpec((width, columns), lambda i: (0, 0)),
            pl.BlockSpec((columns, columns), lambda i: (0, 0)),
            pl.BlockSpec((band * share * ranks, columns), lambda i: (0, 0)),
        ],
        out_shape=[shape(width, columns), shape(columns, columns), shape(band * share * ranks, columns)],
        scratch_shapes=[pltpu.VMEM((rows, columns), jnp.float32), pltpu.VMEM((columns, width), jnp.float32)],
    )(rank_index, weight, *[flat_two] * PARTS, *pieces)


def apply_kernel(rows_ref, weight_ref, out_ref):
    weight = twice(both_parts(weight_ref[...], 1), 0)
    out_ref[...] = fold(mxu(both_parts(rows_ref[...], 1), weight, NN), 1)


def apply_to(rows, weight):
    count, width = rows.shape
    columns = weight.shape[1]
    block = block_of(count)
    return call(
        apply_kernel,
        8 * rows.size * columns,
        4 * (rows.size + count * columns),
        grid=(count // block,),
        in_specs=[
            pl.BlockSpec((block, width), lambda i: (i, 0)),
            pl.BlockSpec((width, columns), lambda i: (0, 0)),
        ],
        out_specs=pl.BlockSpec((block, columns), lambda i: (i, 0)),
        out_shape=shape(count, columns),
    )(rows, weight)


def small_inverse(entry):
    size = len(entry)
    entry = [list(row) for row in entry]
    inverse = [[None] * size for _ in range(size)]
    for k in range(size):
        pivot = entry[k][k]
        root = lax.rsqrt(pivot)
        inverse[k][k] = root
        for i in range(k + 1, size):
            entry[i][k] = entry[i][k] * root
        for i in range(k + 1, size):
            for m in range(k + 1, i + 1):
                entry[i][m] = entry[i][m] - entry[i][k] * entry[m][k]
    for k in range(size):
        for i in range(k + 1, size):
            total = entry[i][k] * inverse[k][k]
            for m in range(k + 1, i):
                total = total + entry[i][m] * inverse[m][k]
            inverse[i][k] = -total * inverse[i][i]
    return inverse


def factor(gram, inverse_ref):
    size, tile = gram.shape[0], BLOCK
    count = size // tile
    left = [gram[i * tile:(i + 1) * tile, :] for i in range(count)]
    lane = lax.broadcasted_iota(jnp.int32, (tile, size), 1)
    sublane = lax.broadcasted_iota(jnp.int32, (tile, size), 0)
    right = [jnp.where(lane == sublane + i * tile, 1.0, 0.0) for i in range(count)]

    def spread(value, row, column):
        return jnp.broadcast_to(value[row:row + 1, column:column + 1], (tile, size))

    for j in range(count):
        corner = [[spread(left[j], i, j * tile + k) for k in range(i + 1)] for i in range(tile)]
        small = small_inverse(corner)
        columns = []
        for k in range(tile):
            column = jnp.where(sublane == k, small[k][k], 0.0)
            for i in range(k + 1, tile):
                column = jnp.where(sublane == i, small[i][k], column)
            columns.append(column)
        done_left = sum(columns[k] * left[j][k:k + 1, :] for k in range(tile))
        done_right = sum(columns[k] * right[j][k:k + 1, :] for k in range(tile))
        inverse_ref[pl.ds(j * tile, tile), :] = done_right
        if j + 1 < count:
            turned = done_left.T
            for i in range(j + 1, count):
                for k in range(tile):
                    factor = jnp.broadcast_to(turned[i * tile:(i + 1) * tile, k:k + 1], (tile, size))
                    left[i] = left[i] - factor * done_left[k:k + 1, :]
                    right[i] = right[i] - factor * done_right[k:k + 1, :]


def first_kernel(scale, band, rank_ref, bridge_ref, raw_ref, weight_ref, solve_ref, inverse_ref):
    local_rows = weight_ref.shape[0] - band
    factor(exact(bridge_ref[...], raw_ref[...], TN), inverse_ref)
    inverse = inverse_ref[...]
    start = pl.multiple_of(rank_ref[0] * local_rows, local_rows)
    own = exact(raw_ref[pl.ds(start, local_rows), :], inverse, NT)
    weight_ref[:local_rows, :] = exact(own, inverse, NN)
    weight_ref[local_rows:, :] = inverse_ref[pl.ds(pl.multiple_of(rank_ref[0] * band, band), band), :]
    solve_ref[...] = scale * exact(bridge_ref[...], inverse, NT)


def first_factor(rank_index, bridge, raw, scale, local_rows, band):
    columns = raw.shape[1]
    whole = pl.BlockSpec(memory_space=pltpu.VMEM)
    return call(
        functools.partial(first_kernel, scale, band),
        8 * raw.size * columns,
        16 * raw.size,
        in_specs=[pl.BlockSpec(memory_space=pltpu.SMEM), whole, whole],
        out_specs=[whole, whole],
        out_shape=[shape(local_rows + band, columns), shape(*raw.shape)],
        scratch_shapes=[pltpu.VMEM((columns, columns), jnp.float32)],
    )(rank_index, bridge, raw)


def last_kernel(scale, gram_ref, middle_ref, inverse_ref, out_ref):
    factor(gram_ref[...], inverse_ref)
    out_ref[...] = exact(middle_ref[...], scale * inverse_ref[...], NT)


def last_factor(gram, middle, scale):
    columns = gram.shape[0]
    whole = pl.BlockSpec(memory_space=pltpu.VMEM)
    return call(
        functools.partial(last_kernel, scale),
        8 * middle.size * columns,
        8 * middle.size,
        in_specs=[whole, whole],
        out_specs=[whole, whole],
        out_shape=[shape(columns, columns), shape(*middle.shape)],
    )(gram, middle)


def swap(value, axis, offset):
    return lax.ppermute(value, axis, [(i, i ^ offset) for i in range(lax.axis_size(axis))])


def exchange(value, axes):
    return lax.all_to_all(value, axes, 0, 0, tiled=True)


def gather_all(value, axes):
    parts = lax.axis_size(axes)
    return exchange(jnp.broadcast_to(value[None], (parts,) + value.shape), axes)


def pairs_of(axis, bits):
    return [(axis, bits[start:start + 2]) for start in range(0, len(bits), 2)]


def after(value, others):
    return lax.optimization_barrier((value, others))


def on_device(core_one, core_two, right_sketch, sketch_core):
    local_rows, slices, width = core_one.shape
    columns = right_sketch.shape[1]
    ranks, cuts = lax.axis_size("rank"), lax.axis_size("cuts")
    rank = lax.axis_index("rank")
    rank_index = rank.astype(jnp.int32).reshape(1)
    both = ("cuts", "rank")
    parts = ranks * cuts
    band = columns // ranks
    share = -(-slices // ranks)
    room = share * ranks
    halves = [share // 2, share - share // 2]
    filler = ((0, 0), (0, room - slices), (0, 0))
    core_two, sketch_core = jnp.pad(core_two, filler), jnp.pad(sketch_core, filler)
    flat_one = core_one.reshape(local_rows * slices, width)
    flat_two = core_two.reshape(local_rows * room, width)

    sketched, part = sketch(core_two, right_sketch, sketch_core)

    def part_for(offset, source, half=None):
        start = (rank ^ offset) * share + (halves[0] if half else 0)
        return lax.dynamic_slice_in_dim(source, start, share if half is None else halves[half], 0)

    cut_bits = [1 << bit for bit in range((cuts - 1).bit_length())]
    bits = [1 << bit for bit in range((ranks - 1).bit_length())]
    far = ranks - 1
    blocks = flat_one.shape[0] // block_of(flat_one.shape[0])
    early = 2 * blocks // 5
    bridge_rows = jnp.sum(exchange(part.reshape(cuts, local_rows // cuts, columns), "cuts"), axis=0)
    flat_late, part = after(flat_one, part)
    square = [square_of(flat_late, 0, early, [], False)] if early else []
    flat_late, (bridge_rows, square) = after(flat_one, (bridge_rows, square))
    sketched, bridge_rows = after(sketched, bridge_rows)
    moved = [swap(part_for(offset, sketched), "rank", offset) for offset in range(1, far)]
    moved.append(swap(part_for(far, sketched, 0), "rank", far))
    bridge = gather_all(bridge_rows, ("rank", "cuts")).reshape(width, columns)
    square = square_of(flat_late, early, blocks - early, square, True)

    raw = product_of(square, bridge)
    sketched, raw = after(sketched, raw)
    own = part_for(0, sketched)
    raw = jnp.sum(exchange(raw.reshape(parts, -1, columns), both), axis=0)
    raw, moved = after(raw, moved)
    sketched, raw = after(sketched, raw)
    pieces = [own] + moved + [swap(part_for(far, sketched, 1), "rank", far)]
    raw = gather_all(raw, both).reshape(width, columns)

    near = list(range(far))
    plan = [[(ref, 0) for ref in near + [far]], [(ref, halves[0]) for ref in near] + [(ranks, 0)]]
    loose = loosen(rank_index, raw, pieces, plan, halves)
    loose, (bridge, raw) = after(loose, (bridge, raw))
    scale = math.sqrt(local_rows * ranks * slices * cuts)
    weight, solve = first_factor(rank_index, bridge, raw, scale, local_rows, band)
    everyone = []
    for half, order in enumerate((bits, bits[::-1])):
        found = {0: loose[half]}
        for bit in order:
            moved = {bit: swap(found[0], "rank", bit)}
            if len(found) > 1:
                late, weight = after({offset: found[offset] for offset in found if offset}, weight)
                moved.update({offset ^ bit: swap(held, "rank", bit) for offset, held in late.items()})
            found.update(moved)
        everyone += [found[offset] for offset in range(ranks)]

    raw, gram, middle = carry_rows(rank_index, weight, flat_two, everyone, halves, share, band)
    flat_late, raw = after(flat_one, raw)
    left_core = apply_to(flat_late, solve)
    raw = jnp.sum(exchange(raw.reshape(parts, -1, columns), both), axis=0)
    for axis, pair in [("cuts", [1])] + pairs_of("rank", bits) + pairs_of("cuts", cut_bits[1:]):
        other = gram + swap(gram, axis, pair[0])
        if len(pair) > 1:
            other = other + (swap(gram, axis, pair[1]) + swap(gram, axis, pair[0] ^ pair[1]))
        gram = other
    raw, (gram, left_core) = after(raw, (gram, left_core))
    left_core = left_core.reshape(local_rows, slices, columns)
    raw = gather_all(raw, both).reshape(width, columns)
    scale = math.sqrt(columns * slices * cuts)
    inverse, middle = last_factor(gram, middle, scale)
    carry = exact(inverse, raw, NT)
    middle_core = middle.reshape(band, room, columns)[:, :slices]
    return (left_core, middle_core, carry)


def solution(mesh):
    placed = (P("rank", "cuts", None), P("rank", "cuts", None), P(), P(None, "cuts", None))
    return jax.shard_map(
        on_device,
        mesh=mesh,
        in_specs=placed,
        out_specs=(P("rank", "cuts", None), P("rank", "cuts", None), P()),
        check_vma=False,
    )
```

```python
import functools
import math

import jax
import jax.numpy as jnp
from jax import lax
from jax.experimental import pallas as pl
from jax.experimental.pallas import tpu as pltpu
from jax.sharding import PartitionSpec as P

NT = (((1,), (1,)), ((), ()))
NN = (((1,), (0,)), ((), ()))
TN = (((0,), (0,)), ((), ()))
VMEM_LIMIT = 56 * 1024 * 1024
BLOCK = 8


PARTS = 4


def tiles(block, width):
    size = block // PARTS
    return [pl.BlockSpec((size, width), lambda i, q=q: (i * PARTS + q, 0)) for q in range(PARTS)]


def joined_rows(refs):
    return jnp.concatenate([ref[...] for ref in refs], axis=0)


def call(kernel, flops, size, **more):
    return pl.pallas_call(
        kernel,
        compiler_params=pltpu.CompilerParams(vmem_limit_bytes=VMEM_LIMIT),
        cost_estimate=pl.CostEstimate(flops=flops, bytes_accessed=size, transcendentals=0),
        **more,
    )


def shape(*extent):
    return jax.ShapeDtypeStruct(extent, jnp.float32)


def split(value):
    high = value.astype(jnp.bfloat16)
    return high, (value - high.astype(jnp.float32)).astype(jnp.bfloat16)


def mxu(a, b, form):
    return lax.dot_general(a, b, form, preferred_element_type=jnp.float32)


def exact(a, b, form):
    return lax.dot_general(a, b, form, precision=lax.Precision.HIGHEST, preferred_element_type=jnp.float32)


def both_parts(value, axis):
    return jnp.concatenate(split(value), axis=axis)


def twice(value, axis):
    return jnp.concatenate([value, value], axis=axis)


def fold(value, axis):
    half = value.shape[axis] // 2
    return lax.slice_in_dim(value, 0, half, axis=axis) + lax.slice_in_dim(value, half, 2 * half, axis=axis)


def rows_of(ref):
    return ref.reshape(ref.shape[0] * ref.shape[1], ref.shape[2])


def sketch_kernel(*refs):
    core_refs, (right_ref, left_ref, sketched_ref, part_ref, rows_ref) = refs[:PARTS], refs[PARTS:]
    block = left_ref.shape[1]
    local_rows = rows_ref.shape[0] // block
    columns = right_ref.shape[1]
    right = both_parts(right_ref[...], 1)
    core = jnp.concatenate([rows_of(ref)[...] for ref in core_refs], axis=0)
    rows_ref[...] = fold(fold(mxu(both_parts(core, 0), right, NN), 0), 1)
    left_rows = rows_of(left_ref)

    @pl.when(pl.program_id(0) == 0)
    def _():
        part_ref[...] = jnp.zeros_like(part_ref)

    sides, lefts = [], []
    for n in range(block):
        rows = rows_ref[pl.ds(n, local_rows, stride=block), :]
        sketched_ref[n] = rows
        sides.append(rows)
        lefts.append(left_rows[pl.ds(n, columns, stride=block), :])
    side = both_parts(jnp.concatenate(sides, axis=1), 0)
    left = both_parts(jnp.concatenate(lefts, axis=1), 0)
    part = fold(fold(mxu(side, left, NT), 0), 1)
    part_ref[...] += part


def sketch(core_two, right_sketch, sketch_core):
    local_rows, slices, width = core_two.shape
    columns = right_sketch.shape[1]
    return call(
        sketch_kernel,
        2 * core_two.size * columns * 4,
        4 * (core_two.size + 2 * sketch_core.size),
        grid=(slices // BLOCK,),
        in_specs=[
            *[pl.BlockSpec((local_rows // PARTS, BLOCK, width), lambda i, q=q: (q, i, 0)) for q in range(PARTS)],
            pl.BlockSpec((width, columns), lambda i: (0, 0)),
            pl.BlockSpec((columns, BLOCK, columns), lambda i: (0, i, 0)),
        ],
        out_specs=[
            pl.BlockSpec((BLOCK, local_rows, columns), lambda i: (i, 0, 0)),
            pl.BlockSpec((local_rows, columns), lambda i: (0, 0)),
        ],
        out_shape=[shape(slices, local_rows, columns), shape(local_rows, columns)],
        scratch_shapes=[pltpu.VMEM((local_rows * BLOCK, columns), jnp.float32)],
    )(*[core_two] * PARTS, right_sketch, sketch_core)


def block_of(rows):
    block = 1024
    while rows % block:
        block //= 2
    return block


def square_kernel(last, core_ref, *refs):
    step = pl.program_id(0)
    before_refs, out_ref, sum_ref = refs[:-2], refs[-2], refs[-1]
    width = core_ref.shape[1]
    high, low = split(core_ref[...])

    @pl.when(step == 0)
    def _():
        sum_ref[...] = before_refs[0][...] if before_refs else jnp.zeros_like(sum_ref)

    sum_ref[...] += mxu(high, jnp.concatenate([high, low], axis=1), TN)

    @pl.when(step == pl.num_programs(0) - 1)
    def _():
        if last:
            cross = sum_ref[:, width:]
            out_ref[...] = both_parts(sum_ref[:, :width] + cross + cross.T, 1)
        else:
            out_ref[...] = sum_ref[...]


def square_of(flat_one, first, count, before, last):
    rows, width = flat_one.shape
    block = block_of(rows)
    whole = pl.BlockSpec((width, 2 * width), lambda i: (0, 0))
    return call(
        functools.partial(square_kernel, last),
        4 * count * block * width * width,
        4 * count * block * width,
        grid=(count,),
        in_specs=[pl.BlockSpec((block, width), lambda i: (i + first, 0))] + [whole] * len(before),
        out_specs=whole,
        out_shape=jax.ShapeDtypeStruct((width, 2 * width), jnp.bfloat16 if last else jnp.float32),
        scratch_shapes=[pltpu.VMEM((width, 2 * width), jnp.float32)],
    )(flat_one, *before)


def product_kernel(square_ref, bridge_ref, out_ref):
    bridge = twice(both_parts(bridge_ref[...], 1), 0)
    out_ref[...] = fold(mxu(square_ref[...], bridge, NN), 1)


def product_of(square, bridge):
    return call(
        product_kernel,
        4 * square.size * bridge.shape[1],
        2 * square.size + 8 * bridge.size,
        out_shape=shape(*bridge.shape),
    )(square, bridge)


def loose_kernel(rank_ref, raw_ref, *refs):
    piece_refs, out_refs = refs[:-2], refs[-2:]
    local_rows, columns = piece_refs[0].shape[1:]
    rows = []
    for offset in range(len(piece_refs)):
        start = pl.multiple_of((rank_ref[0] ^ offset) * local_rows, local_rows)
        rows.append(raw_ref[pl.ds(start, local_rows), :])
    raw = twice(both_parts(jnp.concatenate(rows, axis=0), 1).T, 1)
    first = 0
    for out_ref in out_refs:
        count = out_ref.shape[0]
        value = [jnp.concatenate([ref[first + n] for n in range(count)], axis=1) for ref in piece_refs]
        product = fold(mxu(raw, both_parts(jnp.concatenate(value, axis=0), 0), NN), 0)
        for n in range(count):
            out_ref[n] = product[:, n * columns:(n + 1) * columns]
        first += count


def loosen(rank_index, raw, pieces, halves):
    columns = raw.shape[1]
    size = sum(piece.size for piece in pieces)
    whole = pl.BlockSpec(memory_space=pltpu.VMEM)
    return call(
        loose_kernel,
        8 * size * columns,
        4 * raw.size + 4 * size,
        in_specs=[pl.BlockSpec(memory_space=pltpu.SMEM)] + [whole] * (len(pieces) + 1),
        out_specs=[whole] * 2,
        out_shape=[shape(count, columns, columns) for count in halves],
    )(rank_index, raw, *pieces)


def gram_kernel(inverse_ref, *refs):
    loose_refs, gram_ref = refs[:-1], refs[-1]
    columns = inverse_ref.shape[0]
    inverse = twice(both_parts(inverse_ref[...], 0), 1)
    value = jnp.concatenate([ref[n] for ref in loose_refs for n in range(ref.shape[0])], axis=1)
    rows = fold(mxu(inverse, both_parts(value, 0), NN), 0)
    count = rows.shape[1] // columns
    rows = jnp.concatenate([rows[:, n * columns:(n + 1) * columns] for n in range(count)], axis=0)
    rows = both_parts(rows, 1)
    gram_ref[...] = fold(fold(mxu(rows, rows, TN), 0), 1)


def gram_of(inverse, loose):
    size = sum(value.size for value in loose)
    return call(
        gram_kernel,
        16 * size * inverse.shape[0],
        4 * size,
        out_shape=shape(*inverse.shape),
    )(inverse, *loose)


def carry_kernel(halves, share, rank_ref, weight_ref, *refs):
    core_refs, piece_refs = refs[:PARTS], refs[PARTS:-4]
    raw_ref, middle_ref, rows_ref, sum_ref = refs[-4:]
    step = pl.program_id(0)
    block, width = core_refs[0].shape[0] * PARTS, core_refs[0].shape[1]
    columns = weight_ref.shape[1]
    ranks = len(piece_refs) // len(halves)
    room = share * ranks
    local_rows = rows_ref.shape[0] // room
    band = middle_ref.shape[0] // room

    @pl.when(step == 0)
    def _():
        sum_ref[...] = jnp.zeros_like(sum_ref)
        weight = twice(both_parts(weight_ref[...], 0), 1)
        for half, count in enumerate(halves):
            for offset in range(ranks):
                ref = piece_refs[half * ranks + offset]
                first = (rank_ref[0] ^ offset) * share + sum(halves[:half])
                value = both_parts(jnp.concatenate([ref[n] for n in range(count)], axis=1), 0)
                spread = fold(mxu(weight, value, NN), 0)
                for n in range(count):
                    piece = lax.slice_in_dim(spread, n * columns, (n + 1) * columns, axis=1)
                    rows_ref[pl.ds(first + n, local_rows, stride=room), :] = piece[:local_rows]
                    middle_ref[pl.ds(first + n, band, stride=room), :] = piece[local_rows:]

    rows = both_parts(rows_ref[pl.ds(pl.multiple_of(step * block, block), block), :], 1).T
    product = fold(mxu(twice(rows, 1), both_parts(joined_rows(core_refs), 0), NN), 0)
    sum_ref[...] += product

    @pl.when(step == pl.num_programs(0) - 1)
    def _():
        raw_ref[...] = sum_ref[...].T


def carry_rows(rank_index, weight, flat_two, pieces, halves, share, band):
    rows, width = flat_two.shape
    columns = weight.shape[1]
    block = block_of(rows)
    ranks = len(pieces) // len(halves)
    whole = pl.BlockSpec(memory_space=pltpu.VMEM)
    return call(
        functools.partial(carry_kernel, halves, share),
        8 * flat_two.size * columns,
        4 * flat_two.size + 4 * sum(piece.size for piece in pieces),
        grid=(rows // block,),
        in_specs=[
            pl.BlockSpec(memory_space=pltpu.SMEM),
            pl.BlockSpec((weight.shape[0], columns), lambda i: (0, 0)),
            *tiles(block, width),
        ]
        + [pl.BlockSpec(piece.shape, lambda i: (0, 0, 0)) for piece in pieces],
        out_specs=[
            pl.BlockSpec((width, columns), lambda i: (0, 0)),
            pl.BlockSpec((band * share * ranks, columns), lambda i: (0, 0)),
        ],
        out_shape=[shape(width, columns), shape(band * share * ranks, columns)],
        scratch_shapes=[pltpu.VMEM((rows, columns), jnp.float32), pltpu.VMEM((columns, width), jnp.float32)],
    )(rank_index, weight, *[flat_two] * PARTS, *pieces)


def apply_kernel(rows_ref, weight_ref, out_ref):
    weight = twice(both_parts(weight_ref[...], 1), 0)
    out_ref[...] = fold(mxu(both_parts(rows_ref[...], 1), weight, NN), 1)


def apply_to(rows, weight):
    count, width = rows.shape
    columns = weight.shape[1]
    block = block_of(count)
    return call(
        apply_kernel,
        8 * rows.size * columns,
        4 * (rows.size + count * columns),
        grid=(count // block,),
        in_specs=[
            pl.BlockSpec((block, width), lambda i: (i, 0)),
            pl.BlockSpec((width, columns), lambda i: (0, 0)),
        ],
        out_specs=pl.BlockSpec((block, columns), lambda i: (i, 0)),
        out_shape=shape(count, columns),
    )(rows, weight)


def small_inverse(entry):
    size = len(entry)
    entry = [list(row) for row in entry]
    inverse = [[None] * size for _ in range(size)]
    for k in range(size):
        pivot = entry[k][k]
        root = lax.rsqrt(pivot)
        inverse[k][k] = root
        for i in range(k + 1, size):
            entry[i][k] = entry[i][k] * root
        for i in range(k + 1, size):
            for m in range(k + 1, i + 1):
                entry[i][m] = entry[i][m] - entry[i][k] * entry[m][k]
    for k in range(size):
        for i in range(k + 1, size):
            total = entry[i][k] * inverse[k][k]
            for m in range(k + 1, i):
                total = total + entry[i][m] * inverse[m][k]
            inverse[i][k] = -total * inverse[i][i]
    return inverse


def factor(gram, inverse_ref):
    size, tile = gram.shape[0], BLOCK
    count = size // tile
    left = [gram[i * tile:(i + 1) * tile, :] for i in range(count)]
    lane = lax.broadcasted_iota(jnp.int32, (tile, size), 1)
    sublane = lax.broadcasted_iota(jnp.int32, (tile, size), 0)
    right = [jnp.where(lane == sublane + i * tile, 1.0, 0.0) for i in range(count)]

    def spread(value, row, column):
        return jnp.broadcast_to(value[row:row + 1, column:column + 1], (tile, size))

    for j in range(count):
        corner = [[spread(left[j], i, j * tile + k) for k in range(i + 1)] for i in range(tile)]
        small = small_inverse(corner)
        columns = []
        for k in range(tile):
            column = jnp.where(sublane == k, small[k][k], 0.0)
            for i in range(k + 1, tile):
                column = jnp.where(sublane == i, small[i][k], column)
            columns.append(column)
        done_left = sum(columns[k] * left[j][k:k + 1, :] for k in range(tile))
        done_right = sum(columns[k] * right[j][k:k + 1, :] for k in range(tile))
        inverse_ref[pl.ds(j * tile, tile), :] = done_right
        if j + 1 < count:
            turned = done_left.T
            for i in range(j + 1, count):
                for k in range(tile):
                    factor = jnp.broadcast_to(turned[i * tile:(i + 1) * tile, k:k + 1], (tile, size))
                    left[i] = left[i] - factor * done_left[k:k + 1, :]
                    right[i] = right[i] - factor * done_right[k:k + 1, :]


def first_kernel(scale, band, rank_ref, bridge_ref, raw_ref, weight_ref, solve_ref, inverse_ref):
    local_rows = weight_ref.shape[0] - band
    factor(exact(bridge_ref[...], raw_ref[...], TN), inverse_ref)
    inverse = inverse_ref[...]
    start = pl.multiple_of(rank_ref[0] * local_rows, local_rows)
    own = exact(raw_ref[pl.ds(start, local_rows), :], inverse, NT)
    weight_ref[:local_rows, :] = exact(own, inverse, NN)
    weight_ref[local_rows:, :] = inverse_ref[pl.ds(pl.multiple_of(rank_ref[0] * band, band), band), :]
    solve_ref[...] = scale * exact(bridge_ref[...], inverse, NT)


def first_factor(rank_index, bridge, raw, scale, local_rows, band):
    columns = raw.shape[1]
    whole = pl.BlockSpec(memory_space=pltpu.VMEM)
    return call(
        functools.partial(first_kernel, scale, band),
        8 * raw.size * columns,
        16 * raw.size,
        in_specs=[pl.BlockSpec(memory_space=pltpu.SMEM), whole, whole],
        out_specs=[whole] * 3,
        out_shape=[shape(local_rows + band, columns), shape(*raw.shape), shape(columns, columns)],
    )(rank_index, bridge, raw)


def last_kernel(scale, gram_ref, middle_ref, inverse_ref, out_ref):
    factor(gram_ref[...], inverse_ref)
    out_ref[...] = exact(middle_ref[...], scale * inverse_ref[...], NT)


def last_factor(gram, middle, scale):
    columns = gram.shape[0]
    whole = pl.BlockSpec(memory_space=pltpu.VMEM)
    return call(
        functools.partial(last_kernel, scale),
        8 * middle.size * columns,
        8 * middle.size,
        in_specs=[whole, whole],
        out_specs=[whole, whole],
        out_shape=[shape(columns, columns), shape(*middle.shape)],
    )(gram, middle)


def swap(value, axis, offset):
    return lax.ppermute(value, axis, [(i, i ^ offset) for i in range(lax.axis_size(axis))])


def exchange(value, axes):
    return lax.all_to_all(value, axes, 0, 0, tiled=True)


def gather_all(value, axes):
    parts = lax.axis_size(axes)
    return exchange(jnp.broadcast_to(value[None], (parts,) + value.shape), axes)


def pairs_of(axis, bits):
    return [(axis, bits[start:start + 2]) for start in range(0, len(bits), 2)]


def total_over(value, steps):
    for axis, pair in steps:
        other = value + swap(value, axis, pair[0])
        if len(pair) > 1:
            other = other + (swap(value, axis, pair[1]) + swap(value, axis, pair[0] ^ pair[1]))
        value = other
    return value


def after(value, others):
    return lax.optimization_barrier((value, others))


def on_device(core_one, core_two, right_sketch, sketch_core):
    local_rows, slices, width = core_one.shape
    columns = right_sketch.shape[1]
    ranks, cuts = lax.axis_size("rank"), lax.axis_size("cuts")
    rank = lax.axis_index("rank")
    rank_index = rank.astype(jnp.int32).reshape(1)
    both = ("cuts", "rank")
    parts = ranks * cuts
    band = columns // ranks
    share = -(-slices // ranks)
    room = share * ranks
    halves = [share // 2, share - share // 2]
    filler = ((0, 0), (0, room - slices), (0, 0))
    core_two, sketch_core = jnp.pad(core_two, filler), jnp.pad(sketch_core, filler)
    flat_one = core_one.reshape(local_rows * slices, width)
    flat_two = core_two.reshape(local_rows * room, width)

    sketched, part = sketch(core_two, right_sketch, sketch_core)

    def part_for(offset, source):
        return lax.dynamic_slice_in_dim(source, (rank ^ offset) * share, share, 0)

    cut_bits = [1 << bit for bit in range((cuts - 1).bit_length())]
    bits = [1 << bit for bit in range((ranks - 1).bit_length())]
    far = ranks - 1
    blocks = flat_one.shape[0] // block_of(flat_one.shape[0])
    early = 2 * blocks // 5
    bridge_rows = jnp.sum(exchange(part.reshape(cuts, local_rows // cuts, columns), "cuts"), axis=0)
    flat_late, part = after(flat_one, part)
    square = [square_of(flat_late, 0, early, [], False)] if early else []
    moved = [swap(part_for(offset, sketched), "rank", offset) for offset in range(1, far)]
    flat_late, (bridge_rows, square, moved) = after(flat_one, (bridge_rows, square, moved))
    sketched, bridge_rows = after(sketched, bridge_rows)
    moved.append(swap(part_for(far, sketched), "rank", far))
    bridge = gather_all(bridge_rows, ("rank", "cuts")).reshape(width, columns)
    square = square_of(flat_late, early, blocks - early, square, True)

    raw = product_of(square, bridge)
    sketched, raw = after(sketched, raw)
    own = part_for(0, sketched)
    raw = jnp.sum(exchange(raw.reshape(parts, -1, columns), both), axis=0)
    raw, moved = after(raw, moved)
    raw = gather_all(raw, both).reshape(width, columns)

    loose = loosen(rank_index, raw, [own] + moved, halves)
    loose, (bridge, raw) = after(loose, (bridge, raw))
    scale = math.sqrt(local_rows * ranks * slices * cuts)
    weight, solve, inverse = first_factor(rank_index, bridge, raw, scale, local_rows, band)
    everyone, sent = [], []
    for half, order in enumerate((bits, bits[::-1])):
        found = {0: loose[half]}
        for bit in order:
            moved = {bit: swap(found[0], "rank", bit)}
            sent.append(moved[bit])
            if len(found) > 1:
                late, weight = after({offset: found[offset] for offset in found if offset}, weight)
                moved.update({offset ^ bit: swap(held, "rank", bit) for offset, held in late.items()})
            found.update(moved)
        everyone += [found[offset] for offset in range(ranks)]

    inverse, sent = after(inverse, sent)
    gram = total_over(gram_of(inverse, loose), [("cuts", [1])])
    weight, gram = after(weight, gram)
    raw, middle = carry_rows(rank_index, weight, flat_two, everyone, halves, share, band)
    (flat_late, gram), raw = after((flat_one, gram), raw)
    left_core = apply_to(flat_late, solve)
    raw = jnp.sum(exchange(raw.reshape(parts, -1, columns), both), axis=0)
    gram = total_over(gram, pairs_of("rank", bits) + pairs_of("cuts", cut_bits[1:]))
    raw, (gram, left_core) = after(raw, (gram, left_core))
    left_core = left_core.reshape(local_rows, slices, columns)
    raw = gather_all(raw, both).reshape(width, columns)
    scale = math.sqrt(columns * slices * cuts)
    inverse, middle = last_factor(gram, middle, scale)
    carry = exact(inverse, raw, NT)
    middle_core = middle.reshape(band, room, columns)[:, :slices]
    return (left_core, middle_core, carry)


def solution(mesh):
    placed = (P("rank", "cuts", None), P("rank", "cuts", None), P(), P(None, "cuts", None))
    return jax.shard_map(
        on_device,
        mesh=mesh,
        in_specs=placed,
        out_specs=(P("rank", "cuts", None), P("rank", "cuts", None), P()),
        check_vma=False,
    )
```

```python
import functools
import math

import jax
import jax.numpy as jnp
from jax import lax
from jax.experimental import pallas as pl
from jax.experimental.pallas import tpu as pltpu
from jax.sharding import PartitionSpec as P

NT = (((1,), (1,)), ((), ()))
NN = (((1,), (0,)), ((), ()))
TN = (((0,), (0,)), ((), ()))
VMEM_LIMIT = 56 * 1024 * 1024
BLOCK = 8


PARTS = 1


def tiles(block, width):
    size = block // PARTS
    return [pl.BlockSpec((size, width), lambda i, q=q: (i * PARTS + q, 0)) for q in range(PARTS)]


def joined_rows(refs):
    return jnp.concatenate([ref[...] for ref in refs], axis=0)


def call(kernel, flops, size, **more):
    return pl.pallas_call(
        kernel,
        compiler_params=pltpu.CompilerParams(vmem_limit_bytes=VMEM_LIMIT),
        cost_estimate=pl.CostEstimate(flops=flops, bytes_accessed=size, transcendentals=0),
        **more,
    )


def shape(*extent):
    return jax.ShapeDtypeStruct(extent, jnp.float32)


def split(value):
    high = value.astype(jnp.bfloat16)
    return high, (value - high.astype(jnp.float32)).astype(jnp.bfloat16)


def mxu(a, b, form):
    return lax.dot_general(a, b, form, preferred_element_type=jnp.float32)


def exact(a, b, form):
    return lax.dot_general(a, b, form, precision=lax.Precision.HIGHEST, preferred_element_type=jnp.float32)


def both_parts(value, axis):
    return jnp.concatenate(split(value), axis=axis)


def twice(value, axis):
    return jnp.concatenate([value, value], axis=axis)


def fold(value, axis):
    half = value.shape[axis] // 2
    return lax.slice_in_dim(value, 0, half, axis=axis) + lax.slice_in_dim(value, half, 2 * half, axis=axis)


def rows_of(ref):
    return ref.reshape(ref.shape[0] * ref.shape[1], ref.shape[2])


def sketch_kernel(*refs):
    core_refs, (right_ref, left_ref, sketched_ref, part_ref, rows_ref) = refs[:PARTS], refs[PARTS:]
    block = left_ref.shape[1]
    local_rows = rows_ref.shape[0] // block
    columns = right_ref.shape[1]
    right = both_parts(right_ref[...], 1)
    core = jnp.concatenate([rows_of(ref)[...] for ref in core_refs], axis=0)
    rows_ref[...] = fold(fold(mxu(both_parts(core, 0), right, NN), 0), 1)
    left_rows = rows_of(left_ref)

    @pl.when(pl.program_id(0) == 0)
    def _():
        part_ref[...] = jnp.zeros_like(part_ref)

    sides, lefts = [], []
    for n in range(block):
        rows = rows_ref[pl.ds(n, local_rows, stride=block), :]
        sketched_ref[n] = rows
        sides.append(rows)
        lefts.append(left_rows[pl.ds(n, columns, stride=block), :])
    side = both_parts(jnp.concatenate(sides, axis=1), 0)
    left = both_parts(jnp.concatenate(lefts, axis=1), 0)
    part = fold(fold(mxu(side, left, NT), 0), 1)
    part_ref[...] += part


def sketch(core_two, right_sketch, sketch_core):
    local_rows, slices, width = core_two.shape
    columns = right_sketch.shape[1]
    return call(
        sketch_kernel,
        2 * core_two.size * columns * 4,
        4 * (core_two.size + 2 * sketch_core.size),
        grid=(slices // BLOCK,),
        in_specs=[
            *[pl.BlockSpec((local_rows // PARTS, BLOCK, width), lambda i, q=q: (q, i, 0)) for q in range(PARTS)],
            pl.BlockSpec((width, columns), lambda i: (0, 0)),
            pl.BlockSpec((columns, BLOCK, columns), lambda i: (0, i, 0)),
        ],
        out_specs=[
            pl.BlockSpec((BLOCK, local_rows, columns), lambda i: (i, 0, 0)),
            pl.BlockSpec((local_rows, columns), lambda i: (0, 0)),
        ],
        out_shape=[shape(slices, local_rows, columns), shape(local_rows, columns)],
        scratch_shapes=[pltpu.VMEM((local_rows * BLOCK, columns), jnp.float32)],
    )(*[core_two] * PARTS, right_sketch, sketch_core)


def block_of(rows, block=1024):
    while rows % block:
        block //= 2
    return block


def square_kernel(last, core_ref, *refs):
    step = pl.program_id(0)
    before_refs, out_ref, sum_ref = refs[:-2], refs[-2], refs[-1]
    width = core_ref.shape[1]
    high, low = split(core_ref[...])

    @pl.when(step == 0)
    def _():
        sum_ref[...] = before_refs[0][...] if before_refs else jnp.zeros_like(sum_ref)

    sum_ref[...] += mxu(high, jnp.concatenate([high, low], axis=1), TN)

    @pl.when(step == pl.num_programs(0) - 1)
    def _():
        if last:
            cross = sum_ref[:, width:]
            out_ref[...] = both_parts(sum_ref[:, :width] + cross + cross.T, 1)
        else:
            out_ref[...] = sum_ref[...]


def square_of(flat_one, first, count, before, last):
    rows, width = flat_one.shape
    block = block_of(rows)
    whole = pl.BlockSpec((width, 2 * width), lambda i: (0, 0))
    return call(
        functools.partial(square_kernel, last),
        4 * count * block * width * width,
        4 * count * block * width,
        grid=(count,),
        in_specs=[pl.BlockSpec((block, width), lambda i: (i + first, 0))] + [whole] * len(before),
        out_specs=whole,
        out_shape=jax.ShapeDtypeStruct((width, 2 * width), jnp.bfloat16 if last else jnp.float32),
        scratch_shapes=[pltpu.VMEM((width, 2 * width), jnp.float32)],
    )(flat_one, *before)


def product_kernel(square_ref, bridge_ref, out_ref):
    bridge = twice(both_parts(bridge_ref[...], 1), 0)
    out_ref[...] = fold(mxu(square_ref[...], bridge, NN), 1)


def product_of(square, bridge):
    return call(
        product_kernel,
        4 * square.size * bridge.shape[1],
        2 * square.size + 8 * bridge.size,
        out_shape=shape(*bridge.shape),
    )(square, bridge)


def loose_kernel(rank_ref, raw_ref, *refs):
    piece_refs, out_refs = refs[:-2], refs[-2:]
    local_rows, columns = piece_refs[0].shape[1:]
    rows = []
    for offset in range(len(piece_refs)):
        start = pl.multiple_of((rank_ref[0] ^ offset) * local_rows, local_rows)
        rows.append(raw_ref[pl.ds(start, local_rows), :])
    raw = twice(both_parts(jnp.concatenate(rows, axis=0), 1).T, 1)
    first = 0
    for out_ref in out_refs:
        count = out_ref.shape[0]
        value = [jnp.concatenate([ref[first + n] for n in range(count)], axis=1) for ref in piece_refs]
        product = fold(mxu(raw, both_parts(jnp.concatenate(value, axis=0), 0), NN), 0)
        for n in range(count):
            out_ref[n] = product[:, n * columns:(n + 1) * columns]
        first += count


def loosen(rank_index, raw, pieces, halves):
    columns = raw.shape[1]
    size = sum(piece.size for piece in pieces)
    whole = pl.BlockSpec(memory_space=pltpu.VMEM)
    return call(
        loose_kernel,
        8 * size * columns,
        4 * raw.size + 4 * size,
        in_specs=[pl.BlockSpec(memory_space=pltpu.SMEM)] + [whole] * (len(pieces) + 1),
        out_specs=[whole] * 2,
        out_shape=[shape(count, columns, columns) for count in halves],
    )(rank_index, raw, *pieces)


def gram_kernel(inverse_ref, *refs):
    loose_refs, gram_ref = refs[:-1], refs[-1]
    columns = inverse_ref.shape[0]
    inverse = twice(both_parts(inverse_ref[...], 0), 1)
    value = jnp.concatenate([ref[n] for ref in loose_refs for n in range(ref.shape[0])], axis=1)
    rows = fold(mxu(inverse, both_parts(value, 0), NN), 0)
    count = rows.shape[1] // columns
    rows = jnp.concatenate([rows[:, n * columns:(n + 1) * columns] for n in range(count)], axis=0)
    rows = both_parts(rows, 1)
    gram_ref[...] = fold(fold(mxu(rows, rows, TN), 0), 1)


def gram_of(inverse, loose):
    size = sum(value.size for value in loose)
    return call(
        gram_kernel,
        16 * size * inverse.shape[0],
        4 * size,
        out_shape=shape(*inverse.shape),
    )(inverse, *loose)


def carry_kernel(halves, share, rank_ref, weight_ref, *refs):
    core_refs, piece_refs = refs[:PARTS], refs[PARTS:-4]
    raw_ref, middle_ref, rows_ref, sum_ref = refs[-4:]
    step = pl.program_id(0)
    block, width = core_refs[0].shape[0] * PARTS, core_refs[0].shape[1]
    columns = weight_ref.shape[1]
    ranks = len(piece_refs) // len(halves)
    room = share * ranks
    local_rows = rows_ref.shape[0] // room
    band = middle_ref.shape[0] // room

    @pl.when(step == 0)
    def _():
        sum_ref[...] = jnp.zeros_like(sum_ref)
        weight = twice(both_parts(weight_ref[...], 0), 1)
        for half, count in enumerate(halves):
            for offset in range(ranks):
                ref = piece_refs[half * ranks + offset]
                first = (rank_ref[0] ^ offset) * share + sum(halves[:half])
                value = both_parts(jnp.concatenate([ref[n] for n in range(count)], axis=1), 0)
                spread = fold(mxu(weight, value, NN), 0)
                for n in range(count):
                    piece = lax.slice_in_dim(spread, n * columns, (n + 1) * columns, axis=1)
                    rows_ref[pl.ds(first + n, local_rows, stride=room), :] = piece[:local_rows]
                    middle_ref[pl.ds(first + n, band, stride=room), :] = piece[local_rows:]

    rows = both_parts(rows_ref[pl.ds(pl.multiple_of(step * block, block), block), :], 1).T
    product = fold(mxu(twice(rows, 1), both_parts(joined_rows(core_refs), 0), NN), 0)
    sum_ref[...] += product

    @pl.when(step == pl.num_programs(0) - 1)
    def _():
        raw_ref[...] = sum_ref[...].T


def carry_rows(rank_index, weight, flat_two, pieces, halves, share, band):
    rows, width = flat_two.shape
    columns = weight.shape[1]
    block = block_of(rows, 512)
    ranks = len(pieces) // len(halves)
    whole = pl.BlockSpec(memory_space=pltpu.VMEM)
    return call(
        functools.partial(carry_kernel, halves, share),
        8 * flat_two.size * columns,
        4 * flat_two.size + 4 * sum(piece.size for piece in pieces),
        grid=(rows // block,),
        in_specs=[
            pl.BlockSpec(memory_space=pltpu.SMEM),
            pl.BlockSpec((weight.shape[0], columns), lambda i: (0, 0)),
            *tiles(block, width),
        ]
        + [pl.BlockSpec(piece.shape, lambda i: (0, 0, 0)) for piece in pieces],
        out_specs=[
            pl.BlockSpec((width, columns), lambda i: (0, 0)),
            pl.BlockSpec((band * share * ranks, columns), lambda i: (0, 0)),
        ],
        out_shape=[shape(width, columns), shape(band * share * ranks, columns)],
        scratch_shapes=[pltpu.VMEM((rows, columns), jnp.float32), pltpu.VMEM((columns, width), jnp.float32)],
    )(rank_index, weight, *[flat_two] * PARTS, *pieces)


def apply_kernel(rows_ref, weight_ref, out_ref):
    weight = twice(both_parts(weight_ref[...], 1), 0)
    out_ref[...] = fold(mxu(both_parts(rows_ref[...], 1), weight, NN), 1)


def apply_to(rows, weight):
    count, width = rows.shape
    columns = weight.shape[1]
    block = block_of(count, 512)
    return call(
        apply_kernel,
        8 * rows.size * columns,
        4 * (rows.size + count * columns),
        grid=(count // block,),
        in_specs=[
            pl.BlockSpec((block, width), lambda i: (i, 0)),
            pl.BlockSpec((width, columns), lambda i: (0, 0)),
        ],
        out_specs=pl.BlockSpec((block, columns), lambda i: (i, 0)),
        out_shape=shape(count, columns),
    )(rows, weight)


def small_inverse(entry):
    size = len(entry)
    entry = [list(row) for row in entry]
    inverse = [[None] * size for _ in range(size)]
    for k in range(size):
        pivot = entry[k][k]
        root = lax.rsqrt(pivot)
        inverse[k][k] = root
        for i in range(k + 1, size):
            entry[i][k] = entry[i][k] * root
        for i in range(k + 1, size):
            for m in range(k + 1, i + 1):
                entry[i][m] = entry[i][m] - entry[i][k] * entry[m][k]
    for k in range(size):
        for i in range(k + 1, size):
            total = entry[i][k] * inverse[k][k]
            for m in range(k + 1, i):
                total = total + entry[i][m] * inverse[m][k]
            inverse[i][k] = -total * inverse[i][i]
    return inverse


def factor(gram, inverse_ref):
    size, tile = gram.shape[0], BLOCK
    count = size // tile
    left = [gram[i * tile:(i + 1) * tile, :] for i in range(count)]
    lane = lax.broadcasted_iota(jnp.int32, (tile, size), 1)
    sublane = lax.broadcasted_iota(jnp.int32, (tile, size), 0)
    right = [jnp.where(lane == sublane + i * tile, 1.0, 0.0) for i in range(count)]

    def spread(value, row, column):
        return jnp.broadcast_to(value[row:row + 1, column:column + 1], (tile, size))

    for j in range(count):
        corner = [[spread(left[j], i, j * tile + k) for k in range(i + 1)] for i in range(tile)]
        small = small_inverse(corner)
        columns = []
        for k in range(tile):
            column = jnp.where(sublane == k, small[k][k], 0.0)
            for i in range(k + 1, tile):
                column = jnp.where(sublane == i, small[i][k], column)
            columns.append(column)
        done_left = sum(columns[k] * left[j][k:k + 1, :] for k in range(tile))
        done_right = sum(columns[k] * right[j][k:k + 1, :] for k in range(tile))
        inverse_ref[pl.ds(j * tile, tile), :] = done_right
        if j + 1 < count:
            turned = done_left.T
            for i in range(j + 1, count):
                for k in range(tile):
                    factor = jnp.broadcast_to(turned[i * tile:(i + 1) * tile, k:k + 1], (tile, size))
                    left[i] = left[i] - factor * done_left[k:k + 1, :]
                    right[i] = right[i] - factor * done_right[k:k + 1, :]


def first_kernel(scale, band, rank_ref, bridge_ref, raw_ref, weight_ref, solve_ref, inverse_ref):
    local_rows = weight_ref.shape[0] - band
    factor(exact(bridge_ref[...], raw_ref[...], TN), inverse_ref)
    inverse = inverse_ref[...]
    start = pl.multiple_of(rank_ref[0] * local_rows, local_rows)
    own = exact(raw_ref[pl.ds(start, local_rows), :], inverse, NT)
    weight_ref[:local_rows, :] = exact(own, inverse, NN)
    weight_ref[local_rows:, :] = inverse_ref[pl.ds(pl.multiple_of(rank_ref[0] * band, band), band), :]
    solve_ref[...] = scale * exact(bridge_ref[...], inverse, NT)


def first_factor(rank_index, bridge, raw, scale, local_rows, band):
    columns = raw.shape[1]
    whole = pl.BlockSpec(memory_space=pltpu.VMEM)
    return call(
        functools.partial(first_kernel, scale, band),
        8 * raw.size * columns,
        16 * raw.size,
        in_specs=[pl.BlockSpec(memory_space=pltpu.SMEM), whole, whole],
        out_specs=[whole] * 3,
        out_shape=[shape(local_rows + band, columns), shape(*raw.shape), shape(columns, columns)],
    )(rank_index, bridge, raw)


def last_kernel(scale, gram_ref, middle_ref, inverse_ref, out_ref):
    factor(gram_ref[...], inverse_ref)
    out_ref[...] = exact(middle_ref[...], scale * inverse_ref[...], NT)


def last_factor(gram, middle, scale):
    columns = gram.shape[0]
    whole = pl.BlockSpec(memory_space=pltpu.VMEM)
    return call(
        functools.partial(last_kernel, scale),
        8 * middle.size * columns,
        8 * middle.size,
        in_specs=[whole, whole],
        out_specs=[whole, whole],
        out_shape=[shape(columns, columns), shape(*middle.shape)],
    )(gram, middle)


def swap(value, axis, offset):
    return lax.ppermute(value, axis, [(i, i ^ offset) for i in range(lax.axis_size(axis))])


def exchange(value, axes):
    return lax.all_to_all(value, axes, 0, 0, tiled=True)


def gather_all(value, axes):
    parts = lax.axis_size(axes)
    return exchange(jnp.broadcast_to(value[None], (parts,) + value.shape), axes)


def pairs_of(axis, bits):
    return [(axis, bits[start:start + 2]) for start in range(0, len(bits), 2)]


def total_over(value, steps):
    for axis, pair in steps:
        other = value + swap(value, axis, pair[0])
        if len(pair) > 1:
            other = other + (swap(value, axis, pair[1]) + swap(value, axis, pair[0] ^ pair[1]))
        value = other
    return value


def after(value, others):
    return lax.optimization_barrier((value, others))


def on_device(core_one, core_two, right_sketch, sketch_core):
    local_rows, slices, width = core_one.shape
    columns = right_sketch.shape[1]
    ranks, cuts = lax.axis_size("rank"), lax.axis_size("cuts")
    rank = lax.axis_index("rank")
    rank_index = rank.astype(jnp.int32).reshape(1)
    both = ("cuts", "rank")
    parts = ranks * cuts
    band = columns // ranks
    share = -(-slices // ranks)
    room = share * ranks
    halves = [share // 2, share - share // 2]
    filler = ((0, 0), (0, room - slices), (0, 0))
    core_two, sketch_core = jnp.pad(core_two, filler), jnp.pad(sketch_core, filler)
    flat_one = core_one.reshape(local_rows * slices, width)
    flat_two = core_two.reshape(local_rows * room, width)

    sketched, part = sketch(core_two, right_sketch, sketch_core)

    def part_for(offset, source):
        return lax.dynamic_slice_in_dim(source, (rank ^ offset) * share, share, 0)

    cut_bits = [1 << bit for bit in range((cuts - 1).bit_length())]
    bits = [1 << bit for bit in range((ranks - 1).bit_length())]
    far = ranks - 1
    blocks = flat_one.shape[0] // block_of(flat_one.shape[0])
    early = 3 * blocks // 5
    bridge_rows = jnp.sum(exchange(part.reshape(cuts, local_rows // cuts, columns), "cuts"), axis=0)
    flat_late, part = after(flat_one, part)
    square = [square_of(flat_late, 0, early, [], False)] if early else []
    moved = [swap(part_for(offset, sketched), "rank", offset) for offset in range(1, far)]
    flat_late, (bridge_rows, square, moved) = after(flat_one, (bridge_rows, square, moved))
    sketched, bridge_rows = after(sketched, bridge_rows)
    moved.append(swap(part_for(far, sketched), "rank", far))
    bridge = gather_all(bridge_rows, ("rank", "cuts")).reshape(width, columns)
    square = square_of(flat_late, early, blocks - early, square, True)

    raw = product_of(square, bridge)
    sketched, raw = after(sketched, raw)
    own = part_for(0, sketched)
    raw = jnp.sum(exchange(raw.reshape(parts, -1, columns), both), axis=0)
    raw, moved = after(raw, moved)
    raw = gather_all(raw, both).reshape(width, columns)

    loose = loosen(rank_index, raw, [own] + moved, halves)
    loose, (bridge, raw) = after(loose, (bridge, raw))
    scale = math.sqrt(local_rows * ranks * slices * cuts)
    weight, solve, inverse = first_factor(rank_index, bridge, raw, scale, local_rows, band)
    everyone, sent = [], []
    for half, order in enumerate((bits, bits[::-1])):
        found = {0: loose[half]}
        for bit in order:
            moved = {bit: swap(found[0], "rank", bit)}
            sent.append(moved[bit])
            if len(found) > 1:
                late, weight = after({offset: found[offset] for offset in found if offset}, weight)
                moved.update({offset ^ bit: swap(held, "rank", bit) for offset, held in late.items()})
            found.update(moved)
        everyone += [found[offset] for offset in range(ranks)]

    inverse, sent = after(inverse, sent)
    gram = total_over(gram_of(inverse, loose), [("cuts", [1])])
    weight, gram = after(weight, gram)
    raw, middle = carry_rows(rank_index, weight, flat_two, everyone, halves, share, band)
    (flat_late, gram), raw = after((flat_one, gram), raw)
    left_core = apply_to(flat_late, solve)
    raw = jnp.sum(exchange(raw.reshape(parts, -1, columns), both), axis=0)
    gram = total_over(gram, pairs_of("rank", bits) + pairs_of("cuts", cut_bits[1:]))
    raw, (gram, left_core) = after(raw, (gram, left_core))
    left_core = left_core.reshape(local_rows, slices, columns)
    raw = gather_all(raw, both).reshape(width, columns)
    scale = math.sqrt(columns * slices * cuts)
    inverse, middle = last_factor(gram, middle, scale)
    carry = exact(inverse, raw, NT)
    middle_core = middle.reshape(band, room, columns)[:, :slices]
    return (left_core, middle_core, carry)


def solution(mesh):
    placed = (P("rank", "cuts", None), P("rank", "cuts", None), P(), P(None, "cuts", None))
    return jax.shard_map(
        on_device,
        mesh=mesh,
        in_specs=placed,
        out_specs=(P("rank", "cuts", None), P("rank", "cuts", None), P()),
        check_vma=False,
    )
```

```python
import functools
import math

import jax
import jax.numpy as jnp
from jax import lax
from jax.experimental import pallas as pl
from jax.experimental.pallas import tpu as pltpu
from jax.sharding import PartitionSpec as P

NT = (((1,), (1,)), ((), ()))
NN = (((1,), (0,)), ((), ()))
TN = (((0,), (0,)), ((), ()))
VMEM_LIMIT = 56 * 1024 * 1024
BLOCK = 8


PARTS = 1


def tiles(block, width):
    size = block // PARTS
    return [pl.BlockSpec((size, width), lambda i, q=q: (i * PARTS + q, 0)) for q in range(PARTS)]


def joined_rows(refs):
    return jnp.concatenate([ref[...] for ref in refs], axis=0)


def call(kernel, flops, size, **more):
    return pl.pallas_call(
        kernel,
        compiler_params=pltpu.CompilerParams(vmem_limit_bytes=VMEM_LIMIT),
        cost_estimate=pl.CostEstimate(flops=flops, bytes_accessed=size, transcendentals=0),
        **more,
    )


def shape(*extent):
    return jax.ShapeDtypeStruct(extent, jnp.float32)


def split(value):
    high = value.astype(jnp.bfloat16)
    return high, (value - high.astype(jnp.float32)).astype(jnp.bfloat16)


def mxu(a, b, form):
    return lax.dot_general(a, b, form, preferred_element_type=jnp.float32)


def exact(a, b, form):
    return lax.dot_general(a, b, form, precision=lax.Precision.HIGHEST, preferred_element_type=jnp.float32)


def both_parts(value, axis):
    return jnp.concatenate(split(value), axis=axis)


def twice(value, axis):
    return jnp.concatenate([value, value], axis=axis)


def fold(value, axis):
    half = value.shape[axis] // 2
    return lax.slice_in_dim(value, 0, half, axis=axis) + lax.slice_in_dim(value, half, 2 * half, axis=axis)


def rows_of(ref):
    return ref.reshape(ref.shape[0] * ref.shape[1], ref.shape[2])


def sketch_kernel(*refs):
    core_refs, (right_ref, left_ref, sketched_ref, part_ref, rows_ref) = refs[:PARTS], refs[PARTS:]
    block = left_ref.shape[1]
    local_rows = rows_ref.shape[0] // block
    columns = right_ref.shape[1]
    right = both_parts(right_ref[...], 1)
    core = jnp.concatenate([rows_of(ref)[...] for ref in core_refs], axis=0)
    rows_ref[...] = fold(fold(mxu(both_parts(core, 0), right, NN), 0), 1)
    left_rows = rows_of(left_ref)

    @pl.when(pl.program_id(0) == 0)
    def _():
        part_ref[...] = jnp.zeros_like(part_ref)

    sides, lefts = [], []
    for n in range(block):
        rows = rows_ref[pl.ds(n, local_rows, stride=block), :]
        sketched_ref[n] = rows
        sides.append(rows)
        lefts.append(left_rows[pl.ds(n, columns, stride=block), :])
    side = both_parts(jnp.concatenate(sides, axis=1), 0)
    left = both_parts(jnp.concatenate(lefts, axis=1), 0)
    part = fold(fold(mxu(side, left, NT), 0), 1)
    part_ref[...] += part


def sketch(core_two, right_sketch, sketch_core):
    local_rows, slices, width = core_two.shape
    columns = right_sketch.shape[1]
    return call(
        sketch_kernel,
        2 * core_two.size * columns * 4,
        4 * (core_two.size + 2 * sketch_core.size),
        grid=(slices // BLOCK,),
        in_specs=[
            *[pl.BlockSpec((local_rows // PARTS, BLOCK, width), lambda i, q=q: (q, i, 0)) for q in range(PARTS)],
            pl.BlockSpec((width, columns), lambda i: (0, 0)),
            pl.BlockSpec((columns, BLOCK, columns), lambda i: (0, i, 0)),
        ],
        out_specs=[
            pl.BlockSpec((BLOCK, local_rows, columns), lambda i: (i, 0, 0)),
            pl.BlockSpec((local_rows, columns), lambda i: (0, 0)),
        ],
        out_shape=[shape(slices, local_rows, columns), shape(local_rows, columns)],
        scratch_shapes=[pltpu.VMEM((local_rows * BLOCK, columns), jnp.float32)],
    )(*[core_two] * PARTS, right_sketch, sketch_core)


def block_of(rows):
    block = 1024
    while rows % block:
        block //= 2
    return block


def square_kernel(last, core_ref, *refs):
    step = pl.program_id(0)
    before_refs, out_ref, sum_ref = refs[:-2], refs[-2], refs[-1]
    width = core_ref.shape[1]
    high, low = split(core_ref[...])

    @pl.when(step == 0)
    def _():
        sum_ref[...] = before_refs[0][...] if before_refs else jnp.zeros_like(sum_ref)

    sum_ref[...] += mxu(high, jnp.concatenate([high, low], axis=1), TN)

    @pl.when(step == pl.num_programs(0) - 1)
    def _():
        if last:
            cross = sum_ref[:, width:]
            out_ref[...] = both_parts(sum_ref[:, :width] + cross + cross.T, 1)
        else:
            out_ref[...] = sum_ref[...]


def square_of(flat_one, first, count, before, last):
    rows, width = flat_one.shape
    block = block_of(rows)
    whole = pl.BlockSpec((width, 2 * width), lambda i: (0, 0))
    return call(
        functools.partial(square_kernel, last),
        4 * count * block * width * width,
        4 * count * block * width,
        grid=(count,),
        in_specs=[pl.BlockSpec((block, width), lambda i: (i + first, 0))] + [whole] * len(before),
        out_specs=whole,
        out_shape=jax.ShapeDtypeStruct((width, 2 * width), jnp.bfloat16 if last else jnp.float32),
        scratch_shapes=[pltpu.VMEM((width, 2 * width), jnp.float32)],
    )(flat_one, *before)


def product_kernel(square_ref, bridge_ref, out_ref):
    bridge = twice(both_parts(bridge_ref[...], 1), 0)
    out_ref[...] = fold(mxu(square_ref[...], bridge, NN), 1)


def product_of(square, bridge):
    return call(
        product_kernel,
        4 * square.size * bridge.shape[1],
        2 * square.size + 8 * bridge.size,
        out_shape=shape(*bridge.shape),
    )(square, bridge)


def loose_kernel(rank_ref, raw_ref, *refs):
    piece_refs, out_refs = refs[:-2], refs[-2:]
    local_rows, columns = piece_refs[0].shape[1:]
    rows = []
    for offset in range(len(piece_refs)):
        start = pl.multiple_of((rank_ref[0] ^ offset) * local_rows, local_rows)
        rows.append(raw_ref[pl.ds(start, local_rows), :])
    raw = twice(both_parts(jnp.concatenate(rows, axis=0), 1).T, 1)
    first = 0
    for out_ref in out_refs:
        count = out_ref.shape[0]
        value = [jnp.concatenate([ref[first + n] for n in range(count)], axis=1) for ref in piece_refs]
        product = fold(mxu(raw, both_parts(jnp.concatenate(value, axis=0), 0), NN), 0)
        for n in range(count):
            out_ref[n] = product[:, n * columns:(n + 1) * columns]
        first += count


def loosen(rank_index, raw, pieces, halves):
    columns = raw.shape[1]
    size = sum(piece.size for piece in pieces)
    whole = pl.BlockSpec(memory_space=pltpu.VMEM)
    return call(
        loose_kernel,
        8 * size * columns,
        4 * raw.size + 4 * size,
        in_specs=[pl.BlockSpec(memory_space=pltpu.SMEM)] + [whole] * (len(pieces) + 1),
        out_specs=[whole] * 2,
        out_shape=[shape(count, columns, columns) for count in halves],
    )(rank_index, raw, *pieces)


def gram_kernel(inverse_ref, *refs):
    loose_refs, gram_ref = refs[:-1], refs[-1]
    columns = inverse_ref.shape[0]
    inverse = twice(both_parts(inverse_ref[...], 0), 1)
    value = jnp.concatenate([ref[n] for ref in loose_refs for n in range(ref.shape[0])], axis=1)
    rows = fold(mxu(inverse, both_parts(value, 0), NN), 0)
    count = rows.shape[1] // columns
    rows = jnp.concatenate([rows[:, n * columns:(n + 1) * columns] for n in range(count)], axis=0)
    rows = both_parts(rows, 1)
    gram_ref[...] = fold(fold(mxu(rows, rows, TN), 0), 1)


def gram_of(inverse, loose):
    size = sum(value.size for value in loose)
    return call(
        gram_kernel,
        16 * size * inverse.shape[0],
        4 * size,
        out_shape=shape(*inverse.shape),
    )(inverse, *loose)


def carry_kernel(halves, share, rank_ref, weight_ref, *refs):
    core_refs, piece_refs = refs[:PARTS], refs[PARTS:-4]
    raw_ref, middle_ref, rows_ref, sum_ref = refs[-4:]
    step = pl.program_id(0)
    block, width = core_refs[0].shape[0] * PARTS, core_refs[0].shape[1]
    columns = weight_ref.shape[1]
    ranks = len(piece_refs) // len(halves)
    room = share * ranks
    local_rows = rows_ref.shape[0] // room
    band = middle_ref.shape[0] // room

    @pl.when(step == 0)
    def _():
        sum_ref[...] = jnp.zeros_like(sum_ref)
        weight = twice(both_parts(weight_ref[...], 0), 1)
        for half, count in enumerate(halves):
            for offset in range(ranks):
                ref = piece_refs[half * ranks + offset]
                first = (rank_ref[0] ^ offset) * share + sum(halves[:half])
                value = both_parts(jnp.concatenate([ref[n] for n in range(count)], axis=1), 0)
                spread = fold(mxu(weight, value, NN), 0)
                for n in range(count):
                    piece = lax.slice_in_dim(spread, n * columns, (n + 1) * columns, axis=1)
                    rows_ref[pl.ds(first + n, local_rows, stride=room), :] = piece[:local_rows]
                    middle_ref[pl.ds(first + n, band, stride=room), :] = piece[local_rows:]

    rows = both_parts(rows_ref[pl.ds(pl.multiple_of(step * block, block), block), :], 1).T
    product = fold(mxu(twice(rows, 1), both_parts(joined_rows(core_refs), 0), NN), 0)
    sum_ref[...] += product

    @pl.when(step == pl.num_programs(0) - 1)
    def _():
        raw_ref[...] = sum_ref[...].T


def carry_rows(rank_index, weight, flat_two, pieces, halves, share, band):
    rows, width = flat_two.shape
    columns = weight.shape[1]
    block = block_of(rows)
    ranks = len(pieces) // len(halves)
    whole = pl.BlockSpec(memory_space=pltpu.VMEM)
    return call(
        functools.partial(carry_kernel, halves, share),
        8 * flat_two.size * columns,
        4 * flat_two.size + 4 * sum(piece.size for piece in pieces),
        grid=(rows // block,),
        in_specs=[
            pl.BlockSpec(memory_space=pltpu.SMEM),
            pl.BlockSpec((weight.shape[0], columns), lambda i: (0, 0)),
            *tiles(block, width),
        ]
        + [pl.BlockSpec(piece.shape, lambda i: (0, 0, 0)) for piece in pieces],
        out_specs=[
            pl.BlockSpec((width, columns), lambda i: (0, 0)),
            pl.BlockSpec((band * share * ranks, columns), lambda i: (0, 0)),
        ],
        out_shape=[shape(width, columns), shape(band * share * ranks, columns)],
        scratch_shapes=[pltpu.VMEM((rows, columns), jnp.float32), pltpu.VMEM((columns, width), jnp.float32)],
    )(rank_index, weight, *[flat_two] * PARTS, *pieces)


def apply_kernel(rows_ref, weight_ref, out_ref):
    weight = twice(both_parts(weight_ref[...], 1), 0)
    out_ref[...] = fold(mxu(both_parts(rows_ref[...], 1), weight, NN), 1)


def apply_to(rows, weight):
    count, width = rows.shape
    columns = weight.shape[1]
    block = block_of(count)
    return call(
        apply_kernel,
        8 * rows.size * columns,
        4 * (rows.size + count * columns),
        grid=(count // block,),
        in_specs=[
            pl.BlockSpec((block, width), lambda i: (i, 0)),
            pl.BlockSpec((width, columns), lambda i: (0, 0)),
        ],
        out_specs=pl.BlockSpec((block, columns), lambda i: (i, 0)),
        out_shape=shape(count, columns),
    )(rows, weight)


def small_inverse(entry):
    size = len(entry)
    entry = [list(row) for row in entry]
    inverse = [[None] * size for _ in range(size)]
    for k in range(size):
        pivot = entry[k][k]
        root = lax.rsqrt(pivot)
        inverse[k][k] = root
        for i in range(k + 1, size):
            entry[i][k] = entry[i][k] * root
        for i in range(k + 1, size):
            for m in range(k + 1, i + 1):
                entry[i][m] = entry[i][m] - entry[i][k] * entry[m][k]
    for k in range(size):
        for i in range(k + 1, size):
            total = entry[i][k] * inverse[k][k]
            for m in range(k + 1, i):
                total = total + entry[i][m] * inverse[m][k]
            inverse[i][k] = -total * inverse[i][i]
    return inverse


def factor(gram, inverse_ref):
    size, tile = gram.shape[0], BLOCK
    count = size // tile
    left = [gram[i * tile:(i + 1) * tile, :] for i in range(count)]
    lane = lax.broadcasted_iota(jnp.int32, (tile, size), 1)
    sublane = lax.broadcasted_iota(jnp.int32, (tile, size), 0)
    right = [jnp.where(lane == sublane + i * tile, 1.0, 0.0) for i in range(count)]

    def spread(value, row, column):
        return jnp.broadcast_to(value[row:row + 1, column:column + 1], (tile, size))

    for j in range(count):
        corner = [[spread(left[j], i, j * tile + k) for k in range(i + 1)] for i in range(tile)]
        small = small_inverse(corner)
        columns = []
        for k in range(tile):
            column = jnp.where(sublane == k, small[k][k], 0.0)
            for i in range(k + 1, tile):
                column = jnp.where(sublane == i, small[i][k], column)
            columns.append(column)
        done_left = sum(columns[k] * left[j][k:k + 1, :] for k in range(tile))
        done_right = sum(columns[k] * right[j][k:k + 1, :] for k in range(tile))
        inverse_ref[pl.ds(j * tile, tile), :] = done_right
        if j + 1 < count:
            turned = done_left.T
            for i in range(j + 1, count):
                for k in range(tile):
                    factor = jnp.broadcast_to(turned[i * tile:(i + 1) * tile, k:k + 1], (tile, size))
                    left[i] = left[i] - factor * done_left[k:k + 1, :]
                    right[i] = right[i] - factor * done_right[k:k + 1, :]


def first_kernel(scale, band, rank_ref, bridge_ref, raw_ref, weight_ref, solve_ref, inverse_ref):
    local_rows = weight_ref.shape[0] - band
    factor(exact(bridge_ref[...], raw_ref[...], TN), inverse_ref)
    inverse = inverse_ref[...]
    start = pl.multiple_of(rank_ref[0] * local_rows, local_rows)
    own = exact(raw_ref[pl.ds(start, local_rows), :], inverse, NT)
    weight_ref[:local_rows, :] = exact(own, inverse, NN)
    weight_ref[local_rows:, :] = inverse_ref[pl.ds(pl.multiple_of(rank_ref[0] * band, band), band), :]
    solve_ref[...] = scale * exact(bridge_ref[...], inverse, NT)


def first_factor(rank_index, bridge, raw, scale, local_rows, band):
    columns = raw.shape[1]
    whole = pl.BlockSpec(memory_space=pltpu.VMEM)
    return call(
        functools.partial(first_kernel, scale, band),
        8 * raw.size * columns,
        16 * raw.size,
        in_specs=[pl.BlockSpec(memory_space=pltpu.SMEM), whole, whole],
        out_specs=[whole] * 3,
        out_shape=[shape(local_rows + band, columns), shape(*raw.shape), shape(columns, columns)],
    )(rank_index, bridge, raw)


def last_kernel(scale, gram_ref, middle_ref, inverse_ref, out_ref):
    factor(gram_ref[...], inverse_ref)
    out_ref[...] = exact(middle_ref[...], scale * inverse_ref[...], NT)


def last_factor(gram, middle, scale):
    columns = gram.shape[0]
    whole = pl.BlockSpec(memory_space=pltpu.VMEM)
    return call(
        functools.partial(last_kernel, scale),
        8 * middle.size * columns,
        8 * middle.size,
        in_specs=[whole, whole],
        out_specs=[whole, whole],
        out_shape=[shape(columns, columns), shape(*middle.shape)],
    )(gram, middle)


def swap(value, axis, offset):
    return lax.ppermute(value, axis, [(i, i ^ offset) for i in range(lax.axis_size(axis))])


def exchange(value, axes):
    return lax.all_to_all(value, axes, 0, 0, tiled=True)


def gather_all(value, axes):
    parts = lax.axis_size(axes)
    return exchange(jnp.broadcast_to(value[None], (parts,) + value.shape), axes)


def pairs_of(axis, bits):
    return [(axis, bits[start:start + 2]) for start in range(0, len(bits), 2)]


def total_over(value, steps):
    for axis, pair in steps:
        other = value + swap(value, axis, pair[0])
        if len(pair) > 1:
            other = other + (swap(value, axis, pair[1]) + swap(value, axis, pair[0] ^ pair[1]))
        value = other
    return value


def after(value, others):
    return lax.optimization_barrier((value, others))


def on_device(core_one, core_two, right_sketch, sketch_core):
    local_rows, slices, width = core_one.shape
    columns = right_sketch.shape[1]
    ranks, cuts = lax.axis_size("rank"), lax.axis_size("cuts")
    rank = lax.axis_index("rank")
    rank_index = rank.astype(jnp.int32).reshape(1)
    both = ("cuts", "rank")
    parts = ranks * cuts
    band = columns // ranks
    share = -(-slices // ranks)
    room = share * ranks
    halves = [share // 2, share - share // 2]
    filler = ((0, 0), (0, room - slices), (0, 0))
    core_two, sketch_core = jnp.pad(core_two, filler), jnp.pad(sketch_core, filler)
    flat_one = core_one.reshape(local_rows * slices, width)
    flat_two = core_two.reshape(local_rows * room, width)

    sketched, part = sketch(core_two, right_sketch, sketch_core)

    def part_for(offset, source):
        return lax.dynamic_slice_in_dim(source, (rank ^ offset) * share, share, 0)

    cut_bits = [1 << bit for bit in range((cuts - 1).bit_length())]
    bits = [1 << bit for bit in range((ranks - 1).bit_length())]
    far = ranks - 1
    blocks = flat_one.shape[0] // block_of(flat_one.shape[0])
    early = 4 * blocks // 5
    bridge_rows = jnp.sum(exchange(part.reshape(cuts, local_rows // cuts, columns), "cuts"), axis=0)
    flat_late, part = after(flat_one, part)
    square = [square_of(flat_late, 0, early, [], False)] if early else []
    moved = [swap(part_for(offset, sketched), "rank", offset) for offset in range(1, far)]
    flat_late, (bridge_rows, square, moved) = after(flat_one, (bridge_rows, square, moved))
    sketched, bridge_rows = after(sketched, bridge_rows)
    moved.append(swap(part_for(far, sketched), "rank", far))
    bridge = gather_all(bridge_rows, ("rank", "cuts")).reshape(width, columns)
    square = square_of(flat_late, early, blocks - early, square, True)

    raw = product_of(square, bridge)
    sketched, raw = after(sketched, raw)
    own = part_for(0, sketched)
    raw = jnp.sum(exchange(raw.reshape(parts, -1, columns), both), axis=0)
    raw, moved = after(raw, moved)
    raw = gather_all(raw, both).reshape(width, columns)

    loose = loosen(rank_index, raw, [own] + moved, halves)
    loose, (bridge, raw) = after(loose, (bridge, raw))
    scale = math.sqrt(local_rows * ranks * slices * cuts)
    weight, solve, inverse = first_factor(rank_index, bridge, raw, scale, local_rows, band)
    everyone, sent = [], []
    for half, order in enumerate((bits, bits[::-1])):
        found = {0: loose[half]}
        for bit in order:
            moved = {bit: swap(found[0], "rank", bit)}
            sent.append(moved[bit])
            if len(found) > 1:
                late, weight = after({offset: found[offset] for offset in found if offset}, weight)
                moved.update({offset ^ bit: swap(held, "rank", bit) for offset, held in late.items()})
            found.update(moved)
        everyone += [found[offset] for offset in range(ranks)]

    inverse, sent = after(inverse, sent)
    gram = total_over(gram_of(inverse, loose), [("cuts", [1])])
    weight, gram = after(weight, gram)
    raw, middle = carry_rows(rank_index, weight, flat_two, everyone, halves, share, band)
    (flat_late, gram), raw = after((flat_one, gram), raw)
    left_core = apply_to(flat_late, solve)
    raw = jnp.sum(exchange(raw.reshape(parts, -1, columns), both), axis=0)
    gram = total_over(gram, pairs_of("rank", bits) + pairs_of("cuts", cut_bits[1:]))
    raw, (gram, left_core) = after(raw, (gram, left_core))
    left_core = left_core.reshape(local_rows, slices, columns)
    raw = gather_all(raw, both).reshape(width, columns)
    scale = math.sqrt(columns * slices * cuts)
    inverse, middle = last_factor(gram, middle, scale)
    carry = exact(inverse, raw, NT)
    middle_core = middle.reshape(band, room, columns)[:, :slices]
    return (left_core, middle_core, carry)


def solution(mesh):
    placed = (P("rank", "cuts", None), P("rank", "cuts", None), P(), P(None, "cuts", None))
    return jax.shard_map(
        on_device,
        mesh=mesh,
        in_specs=placed,
        out_specs=(P("rank", "cuts", None), P("rank", "cuts", None), P()),
        check_vma=False,
    )
```

```python
import functools
import math

import jax
import jax.numpy as jnp
from jax import lax
from jax.experimental import pallas as pl
from jax.experimental.pallas import tpu as pltpu
from jax.sharding import PartitionSpec as P

NT = (((1,), (1,)), ((), ()))
NN = (((1,), (0,)), ((), ()))
TN = (((0,), (0,)), ((), ()))
VMEM_LIMIT = 56 * 1024 * 1024
BLOCK = 8


PARTS = 1


def tiles(block, width):
    size = block // PARTS
    return [pl.BlockSpec((size, width), lambda i, q=q: (i * PARTS + q, 0)) for q in range(PARTS)]


def joined_rows(refs):
    return jnp.concatenate([ref[...] for ref in refs], axis=0)


def call(kernel, flops, size, **more):
    return pl.pallas_call(
        kernel,
        compiler_params=pltpu.CompilerParams(vmem_limit_bytes=VMEM_LIMIT),
        cost_estimate=pl.CostEstimate(flops=flops, bytes_accessed=size, transcendentals=0),
        **more,
    )


def shape(*extent):
    return jax.ShapeDtypeStruct(extent, jnp.float32)


def split(value):
    high = value.astype(jnp.bfloat16)
    return high, (value - high.astype(jnp.float32)).astype(jnp.bfloat16)


def mxu(a, b, form):
    return lax.dot_general(a, b, form, preferred_element_type=jnp.float32)


def exact(a, b, form):
    return lax.dot_general(a, b, form, precision=lax.Precision.HIGHEST, preferred_element_type=jnp.float32)


def both_parts(value, axis):
    return jnp.concatenate(split(value), axis=axis)


def twice(value, axis):
    return jnp.concatenate([value, value], axis=axis)


def fold(value, axis):
    half = value.shape[axis] // 2
    return lax.slice_in_dim(value, 0, half, axis=axis) + lax.slice_in_dim(value, half, 2 * half, axis=axis)


def rows_of(ref):
    return ref.reshape(ref.shape[0] * ref.shape[1], ref.shape[2])


def sketch_kernel(*refs):
    core_refs, (right_ref, left_ref, sketched_ref, part_ref, rows_ref) = refs[:PARTS], refs[PARTS:]
    block = left_ref.shape[1]
    local_rows = rows_ref.shape[0] // block
    columns = right_ref.shape[1]
    right = both_parts(right_ref[...], 1)
    core = jnp.concatenate([rows_of(ref)[...] for ref in core_refs], axis=0)
    rows_ref[...] = fold(fold(mxu(both_parts(core, 0), right, NN), 0), 1)
    left_rows = rows_of(left_ref)

    @pl.when(pl.program_id(0) == 0)
    def _():
        part_ref[...] = jnp.zeros_like(part_ref)

    sides, lefts = [], []
    for n in range(block):
        rows = rows_ref[pl.ds(n, local_rows, stride=block), :]
        sketched_ref[n] = rows
        sides.append(rows)
        lefts.append(left_rows[pl.ds(n, columns, stride=block), :])
    side = both_parts(jnp.concatenate(sides, axis=1), 0)
    left = both_parts(jnp.concatenate(lefts, axis=1), 0)
    part = fold(fold(mxu(side, left, NT), 0), 1)
    part_ref[...] += part


def sketch(core_two, right_sketch, sketch_core):
    local_rows, slices, width = core_two.shape
    columns = right_sketch.shape[1]
    return call(
        sketch_kernel,
        2 * core_two.size * columns * 4,
        4 * (core_two.size + 2 * sketch_core.size),
        grid=(slices // BLOCK,),
        in_specs=[
            *[pl.BlockSpec((local_rows // PARTS, BLOCK, width), lambda i, q=q: (q, i, 0)) for q in range(PARTS)],
            pl.BlockSpec((width, columns), lambda i: (0, 0)),
            pl.BlockSpec((columns, BLOCK, columns), lambda i: (0, i, 0)),
        ],
        out_specs=[
            pl.BlockSpec((BLOCK, local_rows, columns), lambda i: (i, 0, 0)),
            pl.BlockSpec((local_rows, columns), lambda i: (0, 0)),
        ],
        out_shape=[shape(slices, local_rows, columns), shape(local_rows, columns)],
        scratch_shapes=[pltpu.VMEM((local_rows * BLOCK, columns), jnp.float32)],
    )(*[core_two] * PARTS, right_sketch, sketch_core)


def block_of(rows):
    block = 1024
    while rows % block:
        block //= 2
    return block


def square_kernel(last, core_ref, *refs):
    step = pl.program_id(0)
    before_refs, out_ref, sum_ref = refs[:-2], refs[-2], refs[-1]
    width = core_ref.shape[1]
    high, low = split(core_ref[...])

    @pl.when(step == 0)
    def _():
        sum_ref[...] = before_refs[0][...] if before_refs else jnp.zeros_like(sum_ref)

    sum_ref[...] += mxu(high, jnp.concatenate([high, low], axis=1), TN)

    @pl.when(step == pl.num_programs(0) - 1)
    def _():
        if last:
            cross = sum_ref[:, width:]
            out_ref[...] = both_parts(sum_ref[:, :width] + cross + cross.T, 1)
        else:
            out_ref[...] = sum_ref[...]


def square_of(flat_one, first, count, before, last):
    rows, width = flat_one.shape
    block = block_of(rows)
    whole = pl.BlockSpec((width, 2 * width), lambda i: (0, 0))
    return call(
        functools.partial(square_kernel, last),
        4 * count * block * width * width,
        4 * count * block * width,
        grid=(count,),
        in_specs=[pl.BlockSpec((block, width), lambda i: (i + first, 0))] + [whole] * len(before),
        out_specs=whole,
        out_shape=jax.ShapeDtypeStruct((width, 2 * width), jnp.bfloat16 if last else jnp.float32),
        scratch_shapes=[pltpu.VMEM((width, 2 * width), jnp.float32)],
    )(flat_one, *before)


def product_kernel(square_ref, bridge_ref, out_ref):
    bridge = twice(both_parts(bridge_ref[...], 1), 0)
    out_ref[...] = fold(mxu(square_ref[...], bridge, NN), 1)


def product_of(square, bridge):
    return call(
        product_kernel,
        4 * square.size * bridge.shape[1],
        2 * square.size + 8 * bridge.size,
        out_shape=shape(*bridge.shape),
    )(square, bridge)


def loose_kernel(rank_ref, raw_ref, *refs):
    piece_refs, out_refs = refs[:-2], refs[-2:]
    local_rows, columns = piece_refs[0].shape[1:]
    rows = []
    for offset in range(len(piece_refs)):
        start = pl.multiple_of((rank_ref[0] ^ offset) * local_rows, local_rows)
        rows.append(raw_ref[pl.ds(start, local_rows), :])
    raw = twice(both_parts(jnp.concatenate(rows, axis=0), 1).T, 1)
    first = 0
    for out_ref in out_refs:
        count = out_ref.shape[0]
        value = [jnp.concatenate([ref[first + n] for n in range(count)], axis=1) for ref in piece_refs]
        product = fold(mxu(raw, both_parts(jnp.concatenate(value, axis=0), 0), NN), 0)
        for n in range(count):
            out_ref[n] = product[:, n * columns:(n + 1) * columns]
        first += count


def loosen(rank_index, raw, pieces, halves):
    columns = raw.shape[1]
    size = sum(piece.size for piece in pieces)
    whole = pl.BlockSpec(memory_space=pltpu.VMEM)
    return call(
        loose_kernel,
        8 * size * columns,
        4 * raw.size + 4 * size,
        in_specs=[pl.BlockSpec(memory_space=pltpu.SMEM)] + [whole] * (len(pieces) + 1),
        out_specs=[whole] * 2,
        out_shape=[shape(count, columns, columns) for count in halves],
    )(rank_index, raw, *pieces)


def gram_kernel(inverse_ref, *refs):
    loose_refs, gram_ref = refs[:-1], refs[-1]
    columns = inverse_ref.shape[0]
    inverse = twice(both_parts(inverse_ref[...], 0), 1)
    value = jnp.concatenate([ref[n] for ref in loose_refs for n in range(ref.shape[0])], axis=1)
    rows = fold(mxu(inverse, both_parts(value, 0), NN), 0)
    count = rows.shape[1] // columns
    rows = jnp.concatenate([rows[:, n * columns:(n + 1) * columns] for n in range(count)], axis=0)
    rows = both_parts(rows, 1)
    gram_ref[...] = fold(fold(mxu(rows, rows, TN), 0), 1)


def gram_of(inverse, loose):
    size = sum(value.size for value in loose)
    return call(
        gram_kernel,
        16 * size * inverse.shape[0],
        4 * size,
        out_shape=shape(*inverse.shape),
    )(inverse, *loose)


def carry_kernel(halves, share, rank_ref, weight_ref, *refs):
    core_refs, piece_refs = refs[:PARTS], refs[PARTS:-4]
    raw_ref, middle_ref, rows_ref, sum_ref = refs[-4:]
    step = pl.program_id(0)
    block, width = core_refs[0].shape[0] * PARTS, core_refs[0].shape[1]
    columns = weight_ref.shape[1]
    ranks = len(piece_refs) // len(halves)
    room = share * ranks
    local_rows = rows_ref.shape[0] // room
    band = middle_ref.shape[0] // room

    @pl.when(step == 0)
    def _():
        sum_ref[...] = jnp.zeros_like(sum_ref)
        weight = twice(both_parts(weight_ref[...], 0), 1)
        for half, count in enumerate(halves):
            for offset in range(ranks):
                ref = piece_refs[half * ranks + offset]
                first = (rank_ref[0] ^ offset) * share + sum(halves[:half])
                value = both_parts(jnp.concatenate([ref[n] for n in range(count)], axis=1), 0)
                spread = fold(mxu(weight, value, NN), 0)
                for n in range(count):
                    piece = lax.slice_in_dim(spread, n * columns, (n + 1) * columns, axis=1)
                    rows_ref[pl.ds(first + n, local_rows, stride=room), :] = piece[:local_rows]
                    middle_ref[pl.ds(first + n, band, stride=room), :] = piece[local_rows:]

    rows = both_parts(rows_ref[pl.ds(pl.multiple_of(step * block, block), block), :], 1).T
    product = fold(mxu(twice(rows, 1), both_parts(joined_rows(core_refs), 0), NN), 0)
    sum_ref[...] += product

    @pl.when(step == pl.num_programs(0) - 1)
    def _():
        raw_ref[...] = sum_ref[...].T


def carry_rows(rank_index, weight, flat_two, pieces, halves, share, band):
    rows, width = flat_two.shape
    columns = weight.shape[1]
    block = block_of(rows)
    ranks = len(pieces) // len(halves)
    whole = pl.BlockSpec(memory_space=pltpu.VMEM)
    return call(
        functools.partial(carry_kernel, halves, share),
        8 * flat_two.size * columns,
        4 * flat_two.size + 4 * sum(piece.size for piece in pieces),
        grid=(rows // block,),
        in_specs=[
            pl.BlockSpec(memory_space=pltpu.SMEM),
            pl.BlockSpec((weight.shape[0], columns), lambda i: (0, 0)),
            *tiles(block, width),
        ]
        + [pl.BlockSpec(piece.shape, lambda i: (0, 0, 0)) for piece in pieces],
        out_specs=[
            pl.BlockSpec((width, columns), lambda i: (0, 0)),
            pl.BlockSpec((band * share * ranks, columns), lambda i: (0, 0)),
        ],
        out_shape=[shape(width, columns), shape(band * share * ranks, columns)],
        scratch_shapes=[pltpu.VMEM((rows, columns), jnp.float32), pltpu.VMEM((columns, width), jnp.float32)],
    )(rank_index, weight, *[flat_two] * PARTS, *pieces)


def apply_kernel(rows_ref, weight_ref, out_ref):
    weight = twice(both_parts(weight_ref[...], 1), 0)
    out_ref[...] = fold(mxu(both_parts(rows_ref[...], 1), weight, NN), 1)


def apply_to(rows, weight):
    count, width = rows.shape
    columns = weight.shape[1]
    block = block_of(count)
    return call(
        apply_kernel,
        8 * rows.size * columns,
        4 * (rows.size + count * columns),
        grid=(count // block,),
        in_specs=[
            pl.BlockSpec((block, width), lambda i: (i, 0)),
            pl.BlockSpec((width, columns), lambda i: (0, 0)),
        ],
        out_specs=pl.BlockSpec((block, columns), lambda i: (i, 0)),
        out_shape=shape(count, columns),
    )(rows, weight)


def small_inverse(entry):
    size = len(entry)
    entry = [list(row) for row in entry]
    inverse = [[None] * size for _ in range(size)]
    for k in range(size):
        pivot = entry[k][k]
        root = lax.rsqrt(pivot)
        inverse[k][k] = root
        for i in range(k + 1, size):
            entry[i][k] = entry[i][k] * root
        for i in range(k + 1, size):
            for m in range(k + 1, i + 1):
                entry[i][m] = entry[i][m] - entry[i][k] * entry[m][k]
    for k in range(size):
        for i in range(k + 1, size):
            total = entry[i][k] * inverse[k][k]
            for m in range(k + 1, i):
                total = total + entry[i][m] * inverse[m][k]
            inverse[i][k] = -total * inverse[i][i]
    return inverse


def factor(gram, inverse_ref):
    size, tile = gram.shape[0], BLOCK
    count = size // tile
    left = [gram[i * tile:(i + 1) * tile, :] for i in range(count)]
    lane = lax.broadcasted_iota(jnp.int32, (tile, size), 1)
    sublane = lax.broadcasted_iota(jnp.int32, (tile, size), 0)
    right = [jnp.where(lane == sublane + i * tile, 1.0, 0.0) for i in range(count)]

    def spread(value, row, column):
        return jnp.broadcast_to(value[row:row + 1, column:column + 1], (tile, size))

    for j in range(count):
        corner = [[spread(left[j], i, j * tile + k) for k in range(i + 1)] for i in range(tile)]
        small = small_inverse(corner)
        columns = []
        for k in range(tile):
            column = jnp.where(sublane == k, small[k][k], 0.0)
            for i in range(k + 1, tile):
                column = jnp.where(sublane == i, small[i][k], column)
            columns.append(column)
        done_left = sum(columns[k] * left[j][k:k + 1, :] for k in range(tile))
        done_right = sum(columns[k] * right[j][k:k + 1, :] for k in range(tile))
        inverse_ref[pl.ds(j * tile, tile), :] = done_right
        if j + 1 < count:
            turned = done_left.T
            for i in range(j + 1, count):
                for k in range(tile):
                    factor = jnp.broadcast_to(turned[i * tile:(i + 1) * tile, k:k + 1], (tile, size))
                    left[i] = left[i] - factor * done_left[k:k + 1, :]
                    right[i] = right[i] - factor * done_right[k:k + 1, :]


def first_kernel(scale, band, rank_ref, bridge_ref, raw_ref, weight_ref, solve_ref, inverse_ref):
    local_rows = weight_ref.shape[0] - band
    factor(exact(bridge_ref[...], raw_ref[...], TN), inverse_ref)
    inverse = inverse_ref[...]
    start = pl.multiple_of(rank_ref[0] * local_rows, local_rows)
    own = exact(raw_ref[pl.ds(start, local_rows), :], inverse, NT)
    weight_ref[:local_rows, :] = exact(own, inverse, NN)
    weight_ref[local_rows:, :] = inverse_ref[pl.ds(pl.multiple_of(rank_ref[0] * band, band), band), :]
    solve_ref[...] = scale * exact(bridge_ref[...], inverse, NT)


def first_factor(rank_index, bridge, raw, scale, local_rows, band):
    columns = raw.shape[1]
    whole = pl.BlockSpec(memory_space=pltpu.VMEM)
    return call(
        functools.partial(first_kernel, scale, band),
        8 * raw.size * columns,
        16 * raw.size,
        in_specs=[pl.BlockSpec(memory_space=pltpu.SMEM), whole, whole],
        out_specs=[whole] * 3,
        out_shape=[shape(local_rows + band, columns), shape(*raw.shape), shape(columns, columns)],
    )(rank_index, bridge, raw)


def last_kernel(scale, gram_ref, middle_ref, inverse_ref, out_ref):
    factor(gram_ref[...], inverse_ref)
    out_ref[...] = exact(middle_ref[...], scale * inverse_ref[...], NT)


def last_factor(gram, middle, scale):
    columns = gram.shape[0]
    whole = pl.BlockSpec(memory_space=pltpu.VMEM)
    return call(
        functools.partial(last_kernel, scale),
        8 * middle.size * columns,
        8 * middle.size,
        in_specs=[whole, whole],
        out_specs=[whole, whole],
        out_shape=[shape(columns, columns), shape(*middle.shape)],
    )(gram, middle)


def swap(value, axis, offset):
    return lax.ppermute(value, axis, [(i, i ^ offset) for i in range(lax.axis_size(axis))])


def exchange(value, axes):
    return lax.all_to_all(value, axes, 0, 0, tiled=True)


def gather_all(value, axes):
    parts = lax.axis_size(axes)
    return exchange(jnp.broadcast_to(value[None], (parts,) + value.shape), axes)


def pairs_of(axis, bits):
    return [(axis, bits[start:start + 2]) for start in range(0, len(bits), 2)]


def total_over(value, steps):
    for axis, pair in steps:
        other = value + swap(value, axis, pair[0])
        if len(pair) > 1:
            other = other + (swap(value, axis, pair[1]) + swap(value, axis, pair[0] ^ pair[1]))
        value = other
    return value


def after(value, others):
    return lax.optimization_barrier((value, others))


def on_device(core_one, core_two, right_sketch, sketch_core):
    local_rows, slices, width = core_one.shape
    columns = right_sketch.shape[1]
    ranks, cuts = lax.axis_size("rank"), lax.axis_size("cuts")
    rank = lax.axis_index("rank")
    rank_index = rank.astype(jnp.int32).reshape(1)
    both = ("cuts", "rank")
    parts = ranks * cuts
    band = columns // ranks
    share = -(-slices // ranks)
    room = share * ranks
    halves = [share // 2, share - share // 2]
    filler = ((0, 0), (0, room - slices), (0, 0))
    core_two, sketch_core = jnp.pad(core_two, filler), jnp.pad(sketch_core, filler)
    flat_one = core_one.reshape(local_rows * slices, width)
    flat_two = core_two.reshape(local_rows * room, width)

    sketched, part = sketch(core_two, right_sketch, sketch_core)

    def part_for(offset, source):
        return lax.dynamic_slice_in_dim(source, (rank ^ offset) * share, share, 0)

    cut_bits = [1 << bit for bit in range((cuts - 1).bit_length())]
    bits = [1 << bit for bit in range((ranks - 1).bit_length())]
    far = ranks - 1
    blocks = flat_one.shape[0] // block_of(flat_one.shape[0])
    early = 2 * blocks // 5
    bridge_rows = jnp.sum(exchange(part.reshape(cuts, local_rows // cuts, columns), "cuts"), axis=0)
    flat_late, part = after(flat_one, part)
    square = [square_of(flat_late, 0, early, [], False)] if early else []
    moved = [swap(part_for(offset, sketched), "rank", offset) for offset in range(1, far)]
    flat_late, (bridge_rows, square) = after(flat_one, (bridge_rows, square))
    sketched, (_, moved) = after(sketched, (bridge_rows, moved))
    moved.append(swap(part_for(far, sketched), "rank", far))
    bridge = gather_all(bridge_rows, ("rank", "cuts")).reshape(width, columns)
    square = square_of(flat_late, early, blocks - early, square, True)

    raw = product_of(square, bridge)
    sketched, raw = after(sketched, raw)
    own = part_for(0, sketched)
    raw = jnp.sum(exchange(raw.reshape(parts, -1, columns), both), axis=0)
    raw, moved = after(raw, moved)
    raw = gather_all(raw, both).reshape(width, columns)

    loose = loosen(rank_index, raw, [own] + moved, halves)
    loose, (bridge, raw) = after(loose, (bridge, raw))
    scale = math.sqrt(local_rows * ranks * slices * cuts)
    weight, solve, inverse = first_factor(rank_index, bridge, raw, scale, local_rows, band)
    everyone, sent = [], []
    for half, order in enumerate((bits, bits[::-1])):
        found = {0: loose[half]}
        for bit in order:
            moved = {bit: swap(found[0], "rank", bit)}
            sent.append(moved[bit])
            if len(found) > 1:
                late, weight = after({offset: found[offset] for offset in found if offset}, weight)
                moved.update({offset ^ bit: swap(held, "rank", bit) for offset, held in late.items()})
            found.update(moved)
        everyone += [found[offset] for offset in range(ranks)]

    inverse, sent = after(inverse, sent)
    gram = total_over(gram_of(inverse, loose), [("cuts", [1])])
    weight, gram = after(weight, gram)
    raw, middle = carry_rows(rank_index, weight, flat_two, everyone, halves, share, band)
    (flat_late, gram), raw = after((flat_one, gram), raw)
    left_core = apply_to(flat_late, solve)
    raw = jnp.sum(exchange(raw.reshape(parts, -1, columns), both), axis=0)
    gram = total_over(gram, pairs_of("rank", bits) + pairs_of("cuts", cut_bits[1:]))
    raw, (gram, left_core) = after(raw, (gram, left_core))
    left_core = left_core.reshape(local_rows, slices, columns)
    raw = gather_all(raw, both).reshape(width, columns)
    scale = math.sqrt(columns * slices * cuts)
    inverse, middle = last_factor(gram, middle, scale)
    carry = exact(inverse, raw, NT)
    middle_core = middle.reshape(band, room, columns)[:, :slices]
    return (left_core, middle_core, carry)


def solution(mesh):
    placed = (P("rank", "cuts", None), P("rank", "cuts", None), P(), P(None, "cuts", None))
    return jax.shard_map(
        on_device,
        mesh=mesh,
        in_specs=placed,
        out_specs=(P("rank", "cuts", None), P("rank", "cuts", None), P()),
        check_vma=False,
    )
```

```python
import functools
import math

import jax
import jax.numpy as jnp
from jax import lax
from jax.experimental import pallas as pl
from jax.experimental.pallas import tpu as pltpu
from jax.sharding import PartitionSpec as P

NT = (((1,), (1,)), ((), ()))
NN = (((1,), (0,)), ((), ()))
TN = (((0,), (0,)), ((), ()))
VMEM_LIMIT = 56 * 1024 * 1024
BLOCK = 8


PARTS = 1


def tiles(block, width):
    size = block // PARTS
    return [pl.BlockSpec((size, width), lambda i, q=q: (i * PARTS + q, 0)) for q in range(PARTS)]


def joined_rows(refs):
    return jnp.concatenate([ref[...] for ref in refs], axis=0)


def call(kernel, flops, size, **more):
    return pl.pallas_call(
        kernel,
        compiler_params=pltpu.CompilerParams(vmem_limit_bytes=VMEM_LIMIT),
        cost_estimate=pl.CostEstimate(flops=flops, bytes_accessed=size, transcendentals=0),
        **more,
    )


def shape(*extent):
    return jax.ShapeDtypeStruct(extent, jnp.float32)


def split(value):
    high = value.astype(jnp.bfloat16)
    return high, (value - high.astype(jnp.float32)).astype(jnp.bfloat16)


def mxu(a, b, form):
    return lax.dot_general(a, b, form, preferred_element_type=jnp.float32)


def exact(a, b, form):
    return lax.dot_general(a, b, form, precision=lax.Precision.HIGHEST, preferred_element_type=jnp.float32)


def both_parts(value, axis):
    return jnp.concatenate(split(value), axis=axis)


def twice(value, axis):
    return jnp.concatenate([value, value], axis=axis)


def fold(value, axis):
    half = value.shape[axis] // 2
    return lax.slice_in_dim(value, 0, half, axis=axis) + lax.slice_in_dim(value, half, 2 * half, axis=axis)


def rows_of(ref):
    return ref.reshape(ref.shape[0] * ref.shape[1], ref.shape[2])


def sketch_kernel(*refs):
    core_refs, (right_ref, left_ref, sketched_ref, part_ref, rows_ref) = refs[:PARTS], refs[PARTS:]
    block = left_ref.shape[1]
    local_rows = rows_ref.shape[0] // block
    columns = right_ref.shape[1]
    right = both_parts(right_ref[...], 1)
    core = jnp.concatenate([rows_of(ref)[...] for ref in core_refs], axis=0)
    rows_ref[...] = fold(fold(mxu(both_parts(core, 0), right, NN), 0), 1)
    left_rows = rows_of(left_ref)

    @pl.when(pl.program_id(0) == 0)
    def _():
        part_ref[...] = jnp.zeros_like(part_ref)

    sides, lefts = [], []
    for n in range(block):
        rows = rows_ref[pl.ds(n, local_rows, stride=block), :]
        sketched_ref[n] = rows
        sides.append(rows)
        lefts.append(left_rows[pl.ds(n, columns, stride=block), :])
    side = both_parts(jnp.concatenate(sides, axis=1), 0)
    left = both_parts(jnp.concatenate(lefts, axis=1), 0)
    part = fold(fold(mxu(side, left, NT), 0), 1)
    part_ref[...] += part


def sketch(core_two, right_sketch, sketch_core):
    local_rows, slices, width = core_two.shape
    columns = right_sketch.shape[1]
    return call(
        sketch_kernel,
        2 * core_two.size * columns * 4,
        4 * (core_two.size + 2 * sketch_core.size),
        grid=(slices // BLOCK,),
        in_specs=[
            *[pl.BlockSpec((local_rows // PARTS, BLOCK, width), lambda i, q=q: (q, i, 0)) for q in range(PARTS)],
            pl.BlockSpec((width, columns), lambda i: (0, 0)),
            pl.BlockSpec((columns, BLOCK, columns), lambda i: (0, i, 0)),
        ],
        out_specs=[
            pl.BlockSpec((BLOCK, local_rows, columns), lambda i: (i, 0, 0)),
            pl.BlockSpec((local_rows, columns), lambda i: (0, 0)),
        ],
        out_shape=[shape(slices, local_rows, columns), shape(local_rows, columns)],
        scratch_shapes=[pltpu.VMEM((local_rows * BLOCK, columns), jnp.float32)],
    )(*[core_two] * PARTS, right_sketch, sketch_core)


def block_of(rows):
    block = 1024
    while rows % block:
        block //= 2
    return block


def square_kernel(last, core_ref, *refs):
    step = pl.program_id(0)
    before_refs, out_ref, sum_ref = refs[:-2], refs[-2], refs[-1]
    width = core_ref.shape[1]
    high, low = split(core_ref[...])

    @pl.when(step == 0)
    def _():
        sum_ref[...] = before_refs[0][...] if before_refs else jnp.zeros_like(sum_ref)

    half = width // 2
    pair = jnp.concatenate([high, low], axis=1)
    upper = mxu(high[:, :half], pair, TN)
    lower = mxu(high[:, half:], pair[:, half:], TN)
    sum_ref[:half, :] += upper
    sum_ref[half:, half:] += lower

    @pl.when(step == pl.num_programs(0) - 1)
    def _():
        if last:
            cross = sum_ref[:, width:]
            left = jnp.concatenate([sum_ref[:half, :half], sum_ref[:half, half:width].T], axis=0)
            same = jnp.concatenate([left, sum_ref[:, half:width]], axis=1)
            out_ref[...] = both_parts(same + cross + cross.T, 1)
        else:
            out_ref[...] = sum_ref[...]


def square_of(flat_one, first, count, before, last):
    rows, width = flat_one.shape
    block = block_of(rows)
    whole = pl.BlockSpec((width, 2 * width), lambda i: (0, 0))
    return call(
        functools.partial(square_kernel, last),
        4 * count * block * width * width,
        4 * count * block * width,
        grid=(count,),
        in_specs=[pl.BlockSpec((block, width), lambda i: (i + first, 0))] + [whole] * len(before),
        out_specs=whole,
        out_shape=jax.ShapeDtypeStruct((width, 2 * width), jnp.bfloat16 if last else jnp.float32),
        scratch_shapes=[pltpu.VMEM((width, 2 * width), jnp.float32)],
    )(flat_one, *before)


def product_kernel(square_ref, bridge_ref, out_ref):
    bridge = twice(both_parts(bridge_ref[...], 1), 0)
    out_ref[...] = fold(mxu(square_ref[...], bridge, NN), 1)


def product_of(square, bridge):
    return call(
        product_kernel,
        4 * square.size * bridge.shape[1],
        2 * square.size + 8 * bridge.size,
        out_shape=shape(*bridge.shape),
    )(square, bridge)


def loose_kernel(rank_ref, raw_ref, *refs):
    piece_refs, out_refs = refs[:-2], refs[-2:]
    local_rows, columns = piece_refs[0].shape[1:]
    rows = []
    for offset in range(len(piece_refs)):
        start = pl.multiple_of((rank_ref[0] ^ offset) * local_rows, local_rows)
        rows.append(raw_ref[pl.ds(start, local_rows), :])
    raw = twice(both_parts(jnp.concatenate(rows, axis=0), 1).T, 1)
    first = 0
    for out_ref in out_refs:
        count = out_ref.shape[0]
        value = [jnp.concatenate([ref[first + n] for n in range(count)], axis=1) for ref in piece_refs]
        product = fold(mxu(raw, both_parts(jnp.concatenate(value, axis=0), 0), NN), 0)
        for n in range(count):
            out_ref[n] = product[:, n * columns:(n + 1) * columns]
        first += count


def loosen(rank_index, raw, pieces, halves):
    columns = raw.shape[1]
    size = sum(piece.size for piece in pieces)
    whole = pl.BlockSpec(memory_space=pltpu.VMEM)
    return call(
        loose_kernel,
        8 * size * columns,
        4 * raw.size + 4 * size,
        in_specs=[pl.BlockSpec(memory_space=pltpu.SMEM)] + [whole] * (len(pieces) + 1),
        out_specs=[whole] * 2,
        out_shape=[shape(count, columns, columns) for count in halves],
    )(rank_index, raw, *pieces)


def gram_kernel(inverse_ref, *refs):
    loose_refs, gram_ref = refs[:-1], refs[-1]
    columns = inverse_ref.shape[0]
    inverse = twice(both_parts(inverse_ref[...], 0), 1)
    value = jnp.concatenate([ref[n] for ref in loose_refs for n in range(ref.shape[0])], axis=1)
    rows = fold(mxu(inverse, both_parts(value, 0), NN), 0)
    count = rows.shape[1] // columns
    rows = jnp.concatenate([rows[:, n * columns:(n + 1) * columns] for n in range(count)], axis=0)
    rows = both_parts(rows, 1)
    gram_ref[...] = fold(fold(mxu(rows, rows, TN), 0), 1)


def gram_of(inverse, loose):
    size = sum(value.size for value in loose)
    return call(
        gram_kernel,
        16 * size * inverse.shape[0],
        4 * size,
        out_shape=shape(*inverse.shape),
    )(inverse, *loose)


def carry_kernel(halves, share, rank_ref, weight_ref, *refs):
    core_refs, piece_refs = refs[:PARTS], refs[PARTS:-4]
    raw_ref, middle_ref, rows_ref, sum_ref = refs[-4:]
    step = pl.program_id(0)
    block, width = core_refs[0].shape[0] * PARTS, core_refs[0].shape[1]
    columns = weight_ref.shape[1]
    ranks = len(piece_refs) // len(halves)
    room = share * ranks
    local_rows = rows_ref.shape[0] // room
    band = middle_ref.shape[0] // room

    @pl.when(step == 0)
    def _():
        sum_ref[...] = jnp.zeros_like(sum_ref)
        weight = twice(both_parts(weight_ref[...], 0), 1)
        for half, count in enumerate(halves):
            for offset in range(ranks):
                ref = piece_refs[half * ranks + offset]
                first = (rank_ref[0] ^ offset) * share + sum(halves[:half])
                value = both_parts(jnp.concatenate([ref[n] for n in range(count)], axis=1), 0)
                spread = fold(mxu(weight, value, NN), 0)
                for n in range(count):
                    piece = lax.slice_in_dim(spread, n * columns, (n + 1) * columns, axis=1)
                    rows_ref[pl.ds(first + n, local_rows, stride=room), :] = piece[:local_rows]
                    middle_ref[pl.ds(first + n, band, stride=room), :] = piece[local_rows:]

    rows = both_parts(rows_ref[pl.ds(pl.multiple_of(step * block, block), block), :], 1).T
    product = fold(mxu(twice(rows, 1), both_parts(joined_rows(core_refs), 0), NN), 0)
    sum_ref[...] += product

    @pl.when(step == pl.num_programs(0) - 1)
    def _():
        raw_ref[...] = sum_ref[...].T


def carry_rows(rank_index, weight, flat_two, pieces, halves, share, band):
    rows, width = flat_two.shape
    columns = weight.shape[1]
    block = block_of(rows)
    ranks = len(pieces) // len(halves)
    whole = pl.BlockSpec(memory_space=pltpu.VMEM)
    return call(
        functools.partial(carry_kernel, halves, share),
        8 * flat_two.size * columns,
        4 * flat_two.size + 4 * sum(piece.size for piece in pieces),
        grid=(rows // block,),
        in_specs=[
            pl.BlockSpec(memory_space=pltpu.SMEM),
            pl.BlockSpec((weight.shape[0], columns), lambda i: (0, 0)),
            *tiles(block, width),
        ]
        + [pl.BlockSpec(piece.shape, lambda i: (0, 0, 0)) for piece in pieces],
        out_specs=[
            pl.BlockSpec((width, columns), lambda i: (0, 0)),
            pl.BlockSpec((band * share * ranks, columns), lambda i: (0, 0)),
        ],
        out_shape=[shape(width, columns), shape(band * share * ranks, columns)],
        scratch_shapes=[pltpu.VMEM((rows, columns), jnp.float32), pltpu.VMEM((columns, width), jnp.float32)],
    )(rank_index, weight, *[flat_two] * PARTS, *pieces)


def apply_kernel(rows_ref, weight_ref, out_ref):
    weight = twice(both_parts(weight_ref[...], 1), 0)
    out_ref[...] = fold(mxu(both_parts(rows_ref[...], 1), weight, NN), 1)


def apply_to(rows, weight):
    count, width = rows.shape
    columns = weight.shape[1]
    block = block_of(count)
    return call(
        apply_kernel,
        8 * rows.size * columns,
        4 * (rows.size + count * columns),
        grid=(count // block,),
        in_specs=[
            pl.BlockSpec((block, width), lambda i: (i, 0)),
            pl.BlockSpec((width, columns), lambda i: (0, 0)),
        ],
        out_specs=pl.BlockSpec((block, columns), lambda i: (i, 0)),
        out_shape=shape(count, columns),
    )(rows, weight)


def small_inverse(entry):
    size = len(entry)
    entry = [list(row) for row in entry]
    inverse = [[None] * size for _ in range(size)]
    for k in range(size):
        pivot = entry[k][k]
        root = lax.rsqrt(pivot)
        inverse[k][k] = root
        for i in range(k + 1, size):
            entry[i][k] = entry[i][k] * root
        for i in range(k + 1, size):
            for m in range(k + 1, i + 1):
                entry[i][m] = entry[i][m] - entry[i][k] * entry[m][k]
    for k in range(size):
        for i in range(k + 1, size):
            total = entry[i][k] * inverse[k][k]
            for m in range(k + 1, i):
                total = total + entry[i][m] * inverse[m][k]
            inverse[i][k] = -total * inverse[i][i]
    return inverse


def factor(gram, inverse_ref):
    size, tile = gram.shape[0], BLOCK
    count = size // tile
    left = [gram[i * tile:(i + 1) * tile, :] for i in range(count)]
    lane = lax.broadcasted_iota(jnp.int32, (tile, size), 1)
    sublane = lax.broadcasted_iota(jnp.int32, (tile, size), 0)
    right = [jnp.where(lane == sublane + i * tile, 1.0, 0.0) for i in range(count)]

    def spread(value, row, column):
        return jnp.broadcast_to(value[row:row + 1, column:column + 1], (tile, size))

    for j in range(count):
        corner = [[spread(left[j], i, j * tile + k) for k in range(i + 1)] for i in range(tile)]
        small = small_inverse(corner)
        columns = []
        for k in range(tile):
            column = jnp.where(sublane == k, small[k][k], 0.0)
            for i in range(k + 1, tile):
                column = jnp.where(sublane == i, small[i][k], column)
            columns.append(column)
        done_left = sum(columns[k] * left[j][k:k + 1, :] for k in range(tile))
        done_right = sum(columns[k] * right[j][k:k + 1, :] for k in range(tile))
        inverse_ref[pl.ds(j * tile, tile), :] = done_right
        if j + 1 < count:
            turned = done_left.T
            for i in range(j + 1, count):
                for k in range(tile):
                    factor = jnp.broadcast_to(turned[i * tile:(i + 1) * tile, k:k + 1], (tile, size))
                    left[i] = left[i] - factor * done_left[k:k + 1, :]
                    right[i] = right[i] - factor * done_right[k:k + 1, :]


def first_kernel(scale, band, rank_ref, bridge_ref, raw_ref, weight_ref, solve_ref, inverse_ref):
    local_rows = weight_ref.shape[0] - band
    factor(exact(bridge_ref[...], raw_ref[...], TN), inverse_ref)
    inverse = inverse_ref[...]
    start = pl.multiple_of(rank_ref[0] * local_rows, local_rows)
    own = exact(raw_ref[pl.ds(start, local_rows), :], inverse, NT)
    weight_ref[:local_rows, :] = exact(own, inverse, NN)
    weight_ref[local_rows:, :] = inverse_ref[pl.ds(pl.multiple_of(rank_ref[0] * band, band), band), :]
    solve_ref[...] = scale * exact(bridge_ref[...], inverse, NT)


def first_factor(rank_index, bridge, raw, scale, local_rows, band):
    columns = raw.shape[1]
    whole = pl.BlockSpec(memory_space=pltpu.VMEM)
    return call(
        functools.partial(first_kernel, scale, band),
        8 * raw.size * columns,
        16 * raw.size,
        in_specs=[pl.BlockSpec(memory_space=pltpu.SMEM), whole, whole],
        out_specs=[whole] * 3,
        out_shape=[shape(local_rows + band, columns), shape(*raw.shape), shape(columns, columns)],
    )(rank_index, bridge, raw)


def last_kernel(scale, gram_ref, middle_ref, inverse_ref, out_ref):
    factor(gram_ref[...], inverse_ref)
    out_ref[...] = exact(middle_ref[...], scale * inverse_ref[...], NT)


def last_factor(gram, middle, scale):
    columns = gram.shape[0]
    whole = pl.BlockSpec(memory_space=pltpu.VMEM)
    return call(
        functools.partial(last_kernel, scale),
        8 * middle.size * columns,
        8 * middle.size,
        in_specs=[whole, whole],
        out_specs=[whole, whole],
        out_shape=[shape(columns, columns), shape(*middle.shape)],
    )(gram, middle)


def swap(value, axis, offset):
    return lax.ppermute(value, axis, [(i, i ^ offset) for i in range(lax.axis_size(axis))])


def exchange(value, axes):
    return lax.all_to_all(value, axes, 0, 0, tiled=True)


def gather_all(value, axes):
    parts = lax.axis_size(axes)
    return exchange(jnp.broadcast_to(value[None], (parts,) + value.shape), axes)


def pairs_of(axis, bits):
    return [(axis, bits[start:start + 2]) for start in range(0, len(bits), 2)]


def total_over(value, steps):
    for axis, pair in steps:
        other = value + swap(value, axis, pair[0])
        if len(pair) > 1:
            other = other + (swap(value, axis, pair[1]) + swap(value, axis, pair[0] ^ pair[1]))
        value = other
    return value


def after(value, others):
    return lax.optimization_barrier((value, others))


def on_device(core_one, core_two, right_sketch, sketch_core):
    local_rows, slices, width = core_one.shape
    columns = right_sketch.shape[1]
    ranks, cuts = lax.axis_size("rank"), lax.axis_size("cuts")
    rank = lax.axis_index("rank")
    rank_index = rank.astype(jnp.int32).reshape(1)
    both = ("cuts", "rank")
    parts = ranks * cuts
    band = columns // ranks
    share = -(-slices // ranks)
    room = share * ranks
    halves = [share // 2, share - share // 2]
    filler = ((0, 0), (0, room - slices), (0, 0))
    core_two, sketch_core = jnp.pad(core_two, filler), jnp.pad(sketch_core, filler)
    flat_one = core_one.reshape(local_rows * slices, width)
    flat_two = core_two.reshape(local_rows * room, width)

    sketched, part = sketch(core_two, right_sketch, sketch_core)

    def part_for(offset, source):
        return lax.dynamic_slice_in_dim(source, (rank ^ offset) * share, share, 0)

    cut_bits = [1 << bit for bit in range((cuts - 1).bit_length())]
    bits = [1 << bit for bit in range((ranks - 1).bit_length())]
    far = ranks - 1
    blocks = flat_one.shape[0] // block_of(flat_one.shape[0])
    early = 2 * blocks // 5
    bridge_rows = jnp.sum(exchange(part.reshape(cuts, local_rows // cuts, columns), "cuts"), axis=0)
    flat_late, part = after(flat_one, part)
    square = [square_of(flat_late, 0, early, [], False)] if early else []
    moved = [swap(part_for(offset, sketched), "rank", offset) for offset in range(1, far)]
    flat_late, (bridge_rows, square) = after(flat_one, (bridge_rows, square))
    sketched, (_, moved) = after(sketched, (bridge_rows, moved))
    moved.append(swap(part_for(far, sketched), "rank", far))
    bridge = gather_all(bridge_rows, ("rank", "cuts")).reshape(width, columns)
    square = square_of(flat_late, early, blocks - early, square, True)

    raw = product_of(square, bridge)
    sketched, raw = after(sketched, raw)
    own = part_for(0, sketched)
    raw = jnp.sum(exchange(raw.reshape(parts, -1, columns), both), axis=0)
    raw, moved = after(raw, moved)
    raw = gather_all(raw, both).reshape(width, columns)

    loose = loosen(rank_index, raw, [own] + moved, halves)
    loose, (bridge, raw) = after(loose, (bridge, raw))
    scale = math.sqrt(local_rows * ranks * slices * cuts)
    weight, solve, inverse = first_factor(rank_index, bridge, raw, scale, local_rows, band)
    everyone, sent = [], []
    for half, order in enumerate((bits, bits[::-1])):
        found = {0: loose[half]}
        for bit in order:
            moved = {bit: swap(found[0], "rank", bit)}
            sent.append(moved[bit])
            if len(found) > 1:
                late, weight = after({offset: found[offset] for offset in found if offset}, weight)
                moved.update({offset ^ bit: swap(held, "rank", bit) for offset, held in late.items()})
            found.update(moved)
        everyone += [found[offset] for offset in range(ranks)]

    inverse, sent = after(inverse, sent)
    gram = total_over(gram_of(inverse, loose), [("cuts", [1])])
    weight, gram = after(weight, gram)
    raw, middle = carry_rows(rank_index, weight, flat_two, everyone, halves, share, band)
    (flat_late, gram), raw = after((flat_one, gram), raw)
    left_core = apply_to(flat_late, solve)
    raw = jnp.sum(exchange(raw.reshape(parts, -1, columns), both), axis=0)
    gram = total_over(gram, pairs_of("rank", bits) + pairs_of("cuts", cut_bits[1:]))
    raw, (gram, left_core) = after(raw, (gram, left_core))
    left_core = left_core.reshape(local_rows, slices, columns)
    raw = gather_all(raw, both).reshape(width, columns)
    scale = math.sqrt(columns * slices * cuts)
    inverse, middle = last_factor(gram, middle, scale)
    carry = exact(inverse, raw, NT)
    middle_core = middle.reshape(band, room, columns)[:, :slices]
    return (left_core, middle_core, carry)


def solution(mesh):
    placed = (P("rank", "cuts", None), P("rank", "cuts", None), P(), P(None, "cuts", None))
    return jax.shard_map(
        on_device,
        mesh=mesh,
        in_specs=placed,
        out_specs=(P("rank", "cuts", None), P("rank", "cuts", None), P()),
        check_vma=False,
    )
```
